32 devices in a mesh: dp: 2 (over x), ctx: 8 (over z, core), tensor: 2 (over y).
Axes of the slice: x: 2, y: 2, z: 4, core: 2. Of those that a mesh axis runs over, the one named last changes fastest.
Arguments:
- inputs: bfloat16 [16, 2, 8, 64, 512], P('dp', None, 'ctx'), may hold values from -6 to 6
- cotangent: bfloat16 [16, 2, 8, 64, 512], P('dp', None, 'ctx'), may hold values from -6 to 6
- live_frames: int32 [16], P('dp'), may hold values from 1 to 16, as said below
- gain_attn: float32 [512], replicated, may hold values from 0.5 to 1.5
- shift_attn: float32 [512], replicated, may hold values from -3 to 3
- w_qkv: bfloat16 [512, 8, 192], P(None, 'tensor'), may hold values from -0.25 to 0.25
- w_out: bfloat16 [512, 512], P('tensor'), may hold values from -4 to 4
- gain_mlp: float32 [512], replicated, may hold values from 0.5 to 1.5
- shift_mlp: float32 [512], replicated, may hold values from -3 to 3
- w_up: bfloat16 [512, 2048], P(None, 'tensor'), may hold values from -0.25 to 0.25
- up_bias: float32 [2048], P('tensor'), may hold values from -3 to 3
- w_down: bfloat16 [2048, 512], P('tensor'), may hold values from -0.125 to 0.125
Outputs:
- output: bfloat16 [16, 2, 8, 64, 512], P('dp', None, 'ctx')
- input_grad: bfloat16 [16, 2, 8, 64, 512], P('dp', None, 'ctx')
- grad_gain_attn: float32 [512], P('tensor')
- grad_shift_attn: float32 [512], P('tensor')
- grad_qkv: float32 [512, 8, 192], P(None, 'tensor')
- grad_out: float32 [512, 512], P('tensor')
- grad_gain_mlp: float32 [512], P('tensor')
- grad_shift_mlp: float32 [512], P('tensor')
- grad_up: float32 [512, 2048], P(None, 'tensor')
- grad_up_bias: float32 [2048], P('tensor')
- grad_down: float32 [2048, 512], P('tensor')
The draws below stay inside these ranges and needn't reach their ends.
Inputs may be any that keep to these rules, and one draw needn't show every extreme that they name: `live_frames`: in the 8 clips of one index of dp, one clip, drawn from the seed, has all 16 frames live.
All inputs are finite; a program needn't handle non-finite values.
Results may differ from the reference program's by a relative error of at most 0.022.
Values may be sent and summed in bfloat16 or wider, within the bound.
A program may use at most 128 MiB of HBM per device.

```python
import jax
import jax.numpy as jnp
from jax import lax

D = 512
HEADS = 8
HEAD_DIM = 64
FF = 2048
FRAMES = 16
PATCH = 64
CLIPS_DP = 8
CLIPS = 16
BLOCK = 64
N_CTX = 8


def draw_live_frames(key, part):
    key = jax.random.fold_in(key, 7)
    base_key, pick_key = jax.random.split(key)
    counts = jax.random.randint(base_key, (CLIPS,), 1, FRAMES + 1)
    chosen = jax.random.randint(pick_key, (CLIPS // CLIPS_DP,), 0, CLIPS_DP)
    position = jnp.arange(CLIPS) % CLIPS_DP
    whole_clip = position == jnp.repeat(chosen, CLIPS_DP)
    return jnp.where(whole_clip, FRAMES, counts).astype(jnp.int32)


def block_scale(stream_key, extent, pieces, least, largest):
    gain = 1.0
    for dim, parts in pieces:
        steps = jax.random.uniform(jax.random.fold_in(jax.random.fold_in(stream_key, 6), dim), (parts,), jnp.float32, least / len(pieces), largest / len(pieces))
        gain = gain * jnp.repeat(jnp.exp(steps), extent[dim] // parts).reshape((-1,) + (1,) * (len(extent) - 1 - dim))
    return gain


def bell_draw(own_key, shape, spread, limit, pieces=(), kind=jnp.bfloat16):
    entries = jax.random.normal(own_key, shape, jnp.float32) * spread
    if len(pieces) > 0:
        entries = block_scale(own_key, shape, pieces, -0.22, 0.18) * entries
    return jnp.clip(entries, min=-limit, max=limit).astype(kind)


def setup_inputs(seed: int = 0) -> dict:
    splits = jax.random.split(jax.random.key(seed), 13)
    inputs = bell_draw(splits[0], (CLIPS, 2, N_CTX, BLOCK, D), 1.0, 6.0, ((0, 2), (2, 8)))
    cotangent = bell_draw(splits[1], (CLIPS, 2, N_CTX, BLOCK, D), 1.0, 6.0, ((0, 2), (2, 8)))
    live_frames = draw_live_frames(jax.random.fold_in(splits[12], 71), 0)
    gain_attn = jnp.clip(1.0 + 0.1 * jax.random.normal(splits[3], (D,), jnp.float32), 0.5, 1.5)
    shift_attn = bell_draw(splits[4], (D,), 0.5, 3.0, (), jnp.float32)
    w_qkv = bell_draw(splits[5], (D, HEADS, 3 * HEAD_DIM), D ** -0.5, 0.25, ((1, 2),))
    w_out = bell_draw(splits[6], (D, D), (max(D // 256, 1)) ** -0.5, 4.0, ((0, 2),))
    gain_mlp = jnp.clip(1.0 + 0.1 * jax.random.normal(splits[7], (D,), jnp.float32), 0.5, 1.5)
    shift_mlp = bell_draw(splits[8], (D,), 0.5, 3.0, (), jnp.float32)
    w_up = bell_draw(splits[9], (D, FF), D ** -0.5, 0.25, ((1, 2),))
    up_bias = bell_draw(splits[10], (FF,), 0.5, 3.0, ((0, 2),), jnp.float32)
    w_down = bell_draw(splits[11], (FF, D), FF ** -0.5, 0.125, ((0, 2),))
    return dict(inputs=inputs, cotangent=cotangent, live_frames=live_frames, gain_attn=gain_attn, shift_attn=shift_attn, w_qkv=w_qkv, w_out=w_out, gain_mlp=gain_mlp, shift_mlp=shift_mlp, w_up=w_up, up_bias=up_bias, w_down=w_down)


EPSILON = 1e-05
EXACT = lax.Precision.HIGHEST

@jax.custom_vjp
def low(v):
    return lax.optimization_barrier(v.astype(jnp.bfloat16)).astype(jnp.float32)

@jax.custom_vjp
def low_back(v):
    return v

def low_keep(v):
    return (low(v), None)

def low_pass(kept, grad):
    return (grad,)

def back_keep(v):
    return (v, None)

def back_low(kept, grad):
    return (low(grad),)
low.defvjp(low_keep, low_pass)
low_back.defvjp(back_keep, back_low)

def layer_norm(values, norm_gain, norm_shift):
    row_mean = lax.optimization_barrier(jnp.mean(values, axis=-1, keepdims=True))
    centered = values - row_mean
    variance = lax.optimization_barrier(jnp.mean(centered * centered, axis=-1, keepdims=True))
    return centered * lax.rsqrt(variance + EPSILON) * norm_gain + norm_shift

def to_natural(blocked):
    joined = jnp.concatenate([blocked[:, 0], jnp.flip(blocked[:, 1], axis=1)], axis=1)
    return joined.reshape(CLIPS, FRAMES * PATCH, blocked.shape[-1])

def to_blocks(merged):
    shaped = merged.reshape(CLIPS, 2 * N_CTX, BLOCK, merged.shape[-1])
    return jnp.stack([shaped[:, :N_CTX], jnp.flip(shaped[:, N_CTX:], axis=1)], axis=1)

def attend_clip(operands):
    query, key_part, value_part, live_count = operands
    token_frame = jnp.arange(FRAMES * PATCH) // PATCH
    allowed = (token_frame[None, :] <= token_frame[:, None]) & (token_frame[None, :] < live_count)
    scores = jnp.einsum('qhd,khd->hqk', query, key_part, precision=EXACT) * HEAD_DIM ** (-0.5)
    scores = low_back(jnp.where(allowed[None], scores, -1e+30))
    row_top = lax.optimization_barrier(jnp.max(scores, axis=-1, keepdims=True))
    weights = jnp.exp(scores - row_top)
    attn_probs = weights / lax.optimization_barrier(jnp.sum(weights, axis=-1, keepdims=True))
    mixed = jnp.einsum('hqk,khd->qhd', low(attn_probs), value_part, precision=EXACT)
    return low(low_back(mixed))

def forward(inputs, gain_attn, shift_attn, w_qkv, w_out, gain_mlp, shift_mlp, w_up, up_bias, w_down, live_frames):
    flat_rows = to_natural(inputs).reshape(-1, D)
    normed = low(layer_norm(flat_rows, gain_attn, shift_attn))
    packed = jnp.dot(normed, w_qkv.reshape(D, -1), precision=EXACT)
    packed = low(low_back(packed)).reshape(CLIPS, FRAMES * PATCH, HEADS, 3 * HEAD_DIM)
    query = packed[..., :HEAD_DIM]
    key_part = packed[..., HEAD_DIM:2 * HEAD_DIM]
    value_part = packed[..., 2 * HEAD_DIM:]
    mixed = lax.map(jax.checkpoint(attend_clip), (query, key_part, value_part, live_frames))
    attn_out = low_back(jnp.dot(mixed.reshape(-1, D), w_out, precision=EXACT))
    middle = flat_rows + attn_out
    second = low(layer_norm(middle, gain_mlp, shift_mlp))
    pre_act = low_back(jnp.dot(second, w_up, precision=EXACT) + up_bias)
    activated = low(jax.nn.gelu(pre_act, approximate=True))
    result = middle + jnp.dot(activated, w_down, precision=EXACT)
    return to_blocks(result.reshape(CLIPS, FRAMES * PATCH, D))

def reference(inputs, cotangent, live_frames, gain_attn, shift_attn, w_qkv, w_out, gain_mlp, shift_mlp, w_up, up_bias, w_down):
    floats = [element.astype(jnp.float32) for element in (inputs, gain_attn, shift_attn, w_qkv, w_out, gain_mlp, shift_mlp, w_up, up_bias, w_down)]

    def wrapped(*params):
        return forward(*params, live_frames)
    result, pullback = jax.vjp(wrapped, *floats)
    gradients = pullback(cotangent.astype(jnp.float32))
    return (result.astype(jnp.bfloat16), gradients[0].astype(jnp.bfloat16), gradients[1], gradients[2], gradients[3], gradients[4], gradients[5], gradients[6], gradients[7], gradients[8], gradients[9])
```

```python
import functools

import jax
import jax.numpy as jnp
from jax import lax
from jax.experimental import pallas as pl
from jax.experimental.pallas import tpu as pltpu
from jax.sharding import PartitionSpec as P

PATCH = 64
EPSILON = 1e-05
MESH = pl.DeviceIdType.MESH
BF = jnp.bfloat16
F32 = jnp.float32

NN = (((1,), (0,)), ((), ()))
NT = (((1,), (1,)), ((), ()))
TN = (((0,), (0,)), ((), ()))


def dot(a, b, dims=NN):
    return lax.dot_general(a, b, dims, preferred_element_type=F32)


def bits_of(size):
    found, bit = [], 1
    while bit < size:
        found.append(bit)
        bit *= 2
    return found


def flip(index, bit):
    return index + bit - 2 * bit * ((index // bit) % 2)


def bit_of(index, bit):
    return (index // bit) % 2


def row_ds(start, size, unit=16):
    return pl.ds(pl.multiple_of(start, unit), size)


def remote(src, dst, send_sem, recv_sem, where):
    return pltpu.make_async_remote_copy(
        src_ref=src,
        dst_ref=dst,
        send_sem=send_sem,
        recv_sem=recv_sem,
        device_id=where,
        device_id_type=MESH,
    )


def arrived(dst, sem):
    pltpu.make_async_copy(dst, dst, sem).wait()


def norm_parts(values):
    mean = jnp.mean(values, axis=-1, keepdims=True)
    centered = values - mean
    var = jnp.mean(centered * centered, axis=-1, keepdims=True)
    rstd = lax.rsqrt(var + EPSILON)
    return centered * rstd, rstd


def norm_back(grad, gain, xhat, rstd):
    scaled = grad * gain
    first = jnp.mean(scaled, axis=-1, keepdims=True)
    second = jnp.mean(scaled * xhat, axis=-1, keepdims=True)
    return rstd * (scaled - first - xhat * second)


def plan_levels(lead, rows, order):
    levels = []
    for axis, bit in order:
        if axis == "tensor":
            lead //= 2
            kind = "t"
        elif rows % 32 == 0:
            rows //= 2
            kind = "r"
        else:
            kind = "f"
        levels.append((axis, bit, kind, lead, rows))
    return levels


class Reduce:
    def __init__(self, levels, acc, fin, bufs, ss, rs, place):
        self.levels, self.acc, self.fin = levels, acc, fin
        self.bufs, self.ss, self.rs, self.place = bufs, ss, rs, place
        self.lead, self.rows = acc.shape[0], acc.shape[1]
        self.toff, self.roff = 0, 0
        self.marks = []
        self.copy = None
        self.steps = []
        count = len(levels)
        for n in range(count):
            self.steps.append(functools.partial(self.step, n))
        self.steps.append(self.turn)

    def send(self, n):
        axis, bit, kind, lead, rows = self.levels[n]
        mine = bit_of(self.place[axis], bit)
        self.marks.append((self.toff, self.roff, self.lead, self.rows))
        toff, roff = self.toff, self.roff
        if kind == "t":
            toff = self.toff + (1 - mine) * lead
            self.toff = self.toff + mine * lead
        elif kind == "r":
            roff = self.roff + (1 - mine) * rows
            self.roff = self.roff + mine * rows
        self.lead, self.rows = lead, rows
        self.copy = remote(
            self.acc.at[pl.ds(toff, lead), row_ds(roff, rows)],
            self.bufs[n],
            self.ss.at[n],
            self.rs.at[n],
            {axis: flip(self.place[axis], bit)},
        )
        self.copy.start()

    def absorb(self, n):
        self.copy.wait()
        buf = self.bufs[n]
        part = 32 if self.rows % 32 == 0 else 16
        for a in range(self.lead):

            def add(b, _):
                off = pl.multiple_of(b * part, 16)
                at = row_ds(self.roff + off, part)
                old = self.acc[self.toff + a, at, :].astype(F32)
                new = buf[a, pl.ds(off, part), :].astype(F32)
                self.acc[self.toff + a, at, :] = (old + new).astype(BF)
                return 0

            lax.fori_loop(0, self.rows // part, add, 0)

    def step(self, n):
        if n > 0:
            self.absorb(n - 1)
        self.send(n)

    def turn(self):
        count = len(self.levels)
        self.absorb(count - 1)
        at = row_ds(self.roff, self.rows)
        self.fin[at, :] = self.acc[self.toff, at, :]
        back = [n for n in reversed(range(count)) if self.levels[n][2] == "r"]
        for k, n in enumerate(back):
            self.steps.append(functools.partial(self.gather, n, k == 0))
        self.steps.append(self.close)

    def gather(self, n, first):
        if not first:
            self.copy.wait()
        axis, bit, kind, lead, rows = self.levels[n]
        part = self.fin.at[row_ds(self.roff, rows)]
        count = len(self.levels)
        self.copy = remote(
            part,
            part,
            self.ss.at[count + n],
            self.rs.at[count + n],
            {axis: flip(self.place[axis], bit)},
        )
        self.copy.start()
        self.roff = self.marks[n][1]

    def close(self):
        self.copy.wait()

    def tick(self):
        if self.steps:
            self.steps.pop(0)()
            return True
        return False

    def drain(self):
        while self.tick():
            pass


def kernel(cfg, names, *refs):
    ref = dict(zip(names, refs))
    N, T, DP = cfg["N"], cfg["T"], cfg["DP"]
    L, R, FO, tok = cfg["L"], cfg["R"], cfg["FO"], cfg["tok"]
    D, HW, GW, G, FFh, QB = cfg["D"], cfg["HW"], cfg["GW"], cfg["G"], cfg["FFh"], cfg["QB"]
    head_dim = cfg["head_dim"]
    HG = GW // head_dim
    scale = head_dim ** (-0.5)
    d = lax.axis_index("dp")
    i = lax.axis_index("ctx")
    t = lax.axis_index("tensor")
    place = {"dp": d, "ctx": i, "tensor": t}
    x_in, cot_in = ref["x"], ref["cot"]
    sends = []

    bar = pltpu.get_barrier_semaphore()
    peers = [{"ctx": lax.rem(i + p, N)} for p in range(1, N)]
    peers += [{"tensor": lax.rem(t + p, T)} for p in range(1, T)]
    peers += [{"dp": flip(d, b)} for b in bits_of(DP)]
    for peer in peers:
        pl.semaphore_signal(bar, inc=1, device_id=peer, device_id_type=MESH)
    pl.semaphore_wait(bar, len(peers))

    frames = (i, 2 * N - 1 - i)

    def owns(h):
        return frames[h] // FO == t

    xb, rx, sx, fx = ref["xb"], ref["rx"], ref["sx"], ref["fx"]
    for p in range(N):
        c = lax.rem(i + p, N)
        for h in (0, 1):
            to = xb.at[row_ds(frames[h] * tok, tok)]

            @pl.when(owns(h))
            def _(p=p, c=c, h=h, to=to):
                if p == 0:
                    pltpu.make_async_copy(x_in.at[c, h], to, rx.at[frames[h]]).start()
                else:
                    remote(
                        x_in.at[c, h], to, sx.at[p, h], rx.at[frames[h]], {"ctx": c}
                    ).start()

            if p > 0:

                def done(p=p, c=c, h=h, to=to):
                    @pl.when(owns(h))
                    def _():
                        remote(
                            x_in.at[c, h], to, sx.at[p, h], rx.at[frames[h]], {"ctx": c}
                        ).wait_send()

                sends.append(done)

    def near(k):
        return t * FO + lax.rem(i + k, FO)

    for k in range(FO):
        f = near(k)
        part = xb.at[row_ds(f * tok, tok)]
        arrived(part, rx.at[f])
        for p in range(1, T):
            copy = remote(
                part, part, fx.at[p, k], rx.at[f], {"tensor": lax.rem(t + p, T)}
            )
            copy.start()
            sends.append(copy.wait_send)

    cb, rc, sc = ref["cb"], ref["rc"], ref["sc"]
    for p in range(N):
        c = lax.rem(i + p, N)
        for h in (0, 1):
            slot = lax.rem(frames[h], FO)
            to = cb.at[row_ds(slot * tok, tok)]

            @pl.when(owns(h))
            def _(p=p, c=c, h=h, to=to, slot=slot):
                if p == 0:
                    pltpu.make_async_copy(cot_in.at[c, h], to, rc.at[slot]).start()
                else:
                    remote(cot_in.at[c, h], to, sc.at[p, h], rc.at[slot], {"ctx": c}).start()

            if p > 0:

                def done(p=p, c=c, h=h, to=to, slot=slot):
                    @pl.when(owns(h))
                    def _():
                        remote(
                            cot_in.at[c, h], to, sc.at[p, h], rc.at[slot], {"ctx": c}
                        ).wait_send()

                sends.append(done)

    share = 2 * lax.rem(d, 2) + lax.rem(i, 2)
    wide = ("w_out", "w_up", "w_down")
    full = {n: ref[n + "_full"] for n in wide + ("bias",)}
    rw, sw, lw = ref["rw"], ref["sw"], ref["lw"]
    own_copies = []
    for n, name in enumerate(wide + ("bias",)):
        copy = pltpu.make_async_copy(ref[name], full[name].at[t], lw.at[n])
        copy.start()
        own_copies.append(copy)
    for p in range(1, T):
        to = {"tensor": lax.rem(t + p, T)}
        copy = remote(ref["bias"], full["bias"].at[t], sw.at[3, 0, p], rw.at[3, 0, t], to)
        copy.start()
        sends.append(copy.wait_send)
    for n, name in enumerate(wide):
        quarter = ref[name].shape[0] // 4
        at = row_ds(share * quarter, quarter)
        for p in range(1, T):
            to = {"tensor": lax.rem(t + p, T)}
            copy = remote(
                ref[name].at[at], full[name].at[t, at], sw.at[n, 0, p], rw.at[n, 0, t], to
            )
            copy.start()
            sends.append(copy.wait_send)

    other_dp = 2 * (1 - lax.rem(d, 2)) + lax.rem(i, 2)
    other_core = 2 * lax.rem(d, 2) + 1 - lax.rem(i, 2)
    other_both = 2 * (1 - lax.rem(d, 2)) + 1 - lax.rem(i, 2)

    def weight_part(name, s, which):
        quarter = ref[name].shape[0] // 4
        return full[name].at[s, row_ds(which * quarter, quarter)]

    def weights_second(n, name):
        for p in range(1, T):
            s = lax.rem(t + p, T)
            part = weight_part(name, s, share)
            arrived(part, rw.at[n, 0, s])
            for stage, to in ((1, {"dp": flip(d, 1)}), (2, {"ctx": flip(i, 1)})):
                copy = remote(part, part, sw.at[n, stage, p], rw.at[n, stage, s], to)
                copy.start()
                sends.append(copy.wait_send)

    def weights_third(n, name):
        for p in range(1, T):
            s = lax.rem(t + p, T)
            part = weight_part(name, s, other_dp)
            arrived(part, rw.at[n, 1, s])
            copy = remote(
                part, part, sw.at[n, 3, p], rw.at[n, 3, s], {"ctx": flip(i, 1)}
            )
            copy.start()
            sends.append(copy.wait_send)

    def weights_ready(n, name):
        own_copies[n].wait()
        for p in range(1, T):
            s = lax.rem(t + p, T)
            if name == "bias":
                arrived(full[name].at[s], rw.at[n, 0, s])
            else:
                arrived(weight_part(name, s, other_core), rw.at[n, 2, s])
                arrived(weight_part(name, s, other_both), rw.at[n, 3, s])

    RB = min(256, R)
    nb, qb_, kb_, vb_ = ref["nb"], ref["q"], ref["k"], ref["v"]
    vec = ref["vec"]
    wqkv = ref["w_qkv"]

    def project(start):
        rows = row_ds(start, RB, 64)
        xhat, _ = norm_parts(xb[rows, :].astype(F32))
        normed = (xhat * vec[0:1, :] + vec[1:2, :]).astype(BF)
        nb[rows, :] = normed
        packed = dot(normed, wqkv[...])
        for g in range(G):
            lo = g * GW
            qb_[g, rows, :] = (packed[:, lo : lo + GW].astype(BF).astype(F32) * scale).astype(BF)
            kb_[g, rows, :] = packed[:, HW + lo : HW + lo + GW].astype(BF)
            vb_[g, rows, :] = packed[:, 2 * HW + lo : 2 * HW + lo + GW].astype(BF)

    for k in range(R // RB):
        project(t * R + k * RB)
    for p in range(1, T):
        s = lax.rem(t + p, T)
        for k in range(FO):
            f = s * FO + k
            arrived(xb.at[row_ds(f * tok, tok)], rx.at[f])
        for k in range(R // RB):
            project(s * R + k * RB)

    for n, name in enumerate(wide):
        weights_second(n, name)

    live = ref["live"][i]
    probs, mo, mr = ref["probs"], ref["mo"], ref["mr"]
    rm, sm = ref["rm"], ref["sm"]
    piece = min(QB, R)
    NQ = L // QB
    lane = lax.broadcasted_iota(jnp.int32, (QB, GW), 1) // head_dim

    def pick(parts):
        out = parts[0]
        for a in range(1, HG):
            out = jnp.where(lane == a, parts[a], out)
        return out

    def only(values, a):
        if HG == 1:
            return values
        return jnp.where(lane == a, values, jnp.zeros_like(values))

    def hand_over(qb, g):
        for b in range(QB // piece):
            row = qb * QB + b * piece
            s = row // R
            slot = (row - s * R) // piece
            src = mo.at[pl.ds(row, piece), pl.ds(g * GW, GW)]
            dst = mr.at[t, pl.ds(row - s * R, piece), pl.ds(g * GW, GW)]
            index = row // piece

            @pl.when(s == t)
            def _():
                mr[t, pl.ds(row - s * R, piece), pl.ds(g * GW, GW)] = mo[
                    pl.ds(row, piece), pl.ds(g * GW, GW)
                ]

            @pl.when(s != t)
            def _():
                remote(src, dst, sm.at[index, g], rm.at[t, slot, g], {"tensor": s}).start()

            def done(s=s, src=src, dst=dst, index=index, slot=slot):
                @pl.when(s != t)
                def _():
                    remote(
                        src, dst, sm.at[index, g], rm.at[t, slot, g], {"tensor": s}
                    ).wait_send()

            sends.append(done)

    pumps = [functools.partial(weights_third, n, name) for n, name in enumerate(wide)]
    for qb in reversed(range(NQ)):
        K = (qb + 1) * QB
        rows = pl.ds(qb * QB, QB)
        row_frame = (qb * QB + lax.broadcasted_iota(jnp.int32, (QB, K), 0)) // PATCH
        col_frame = lax.broadcasted_iota(jnp.int32, (QB, K), 1) // PATCH
        allowed = (col_frame <= row_frame) & (col_frame < live)
        shift = jnp.where(allowed, 0.0, -1e30)
        for g in range(G):
            qv = qb_[g, rows, :]
            kv = kb_[g, pl.ds(0, K), :]
            vv = vb_[g, pl.ds(0, K), :]
            outs = []
            for a in range(HG):
                scores = dot(only(qv, a), kv, NT) + shift
                top = jnp.max(scores, axis=-1, keepdims=True)
                weights = jnp.exp(scores - top)
                total = jnp.sum(weights, axis=-1, keepdims=True)
                prob = (weights * (1.0 / total)).astype(BF)
                probs[g * HG + a, rows, pl.ds(0, K)] = prob
                outs.append(dot(prob, vv))
            mo[rows, pl.ds(g * GW, GW)] = pick(outs).astype(BF)
            hand_over(qb, g)
        if pumps:
            pumps.pop(0)()
    while pumps:
        pumps.pop(0)()

    for n, name in enumerate(wide + ("bias",)):
        weights_ready(n, name)
    for p in range(1, T):
        s = lax.rem(t + p, T)
        for slot in range(R // piece):
            for g in range(G):
                arrived(
                    mr.at[s, pl.ds(slot * piece, piece), pl.ds(g * GW, GW)], rm.at[s, slot, g]
                )
    for k in range(FO):
        arrived(cb.at[pl.ds(k * tok, tok)], rc.at[k])

    wof, wuf, wdf, bf_ = full["w_out"], full["w_up"], full["w_down"], full["bias"]
    second, act, gpre = ref["second"], ref["act"], ref["gpre"]
    mlow, gmid, gst, gx = ref["mlow"], ref["gmid"], ref["gst"], ref["gx"]
    ob, out_ref, ig_ref = ref["ob"], ref["out"], ref["ig"]
    sv = ref["sv"]
    mlp_sum, sec_sum = ref["mlp_sum"], ref["sec_sum"]
    RC = min(256, R)
    FT = min(512, FFh)
    c0 = 0.7978845608028654
    sv[0] = jnp.zeros_like(sv[0])

    def frame_home(k):
        f = t * FO + k
        high = f // N
        j = f * (1 - high) + (2 * N - 1 - f) * high
        return j, high

    def give_back(buf, dst_ref, ss, rs, k):
        j, h = frame_home(k)
        src = buf.at[pl.ds(k * tok, tok)]

        @pl.when(j == i)
        def _():
            pltpu.make_async_copy(src, dst_ref.at[i, h], rs.at[i, h]).start()

        @pl.when(j != i)
        def _():
            remote(src, dst_ref.at[i, h], ss.at[k], rs.at[i, h], {"ctx": j}).start()

        def done():
            @pl.when(j != i)
            def _():
                remote(src, dst_ref.at[i, h], ss.at[k], rs.at[i, h], {"ctx": j}).wait_send()

        sends.append(done)

    def pass_on(dst_ref, fs, rs):
        for p in range(N):
            c = lax.rem(i + p, N)
            for h in (0, 1):
                part = dst_ref.at[c, h]

                @pl.when(owns(h))
                def _(p=p, c=c, h=h, part=part):
                    arrived(part, rs.at[c, h])
                    for q in range(1, T):
                        remote(
                            part, part, fs.at[q, p, h], rs.at[c, h], {"tensor": lax.rem(t + q, T)}
                        ).start()

                def done(p=p, c=c, h=h, part=part):
                    @pl.when(owns(h))
                    def _():
                        for q in range(1, T):
                            remote(
                                part,
                                part,
                                fs.at[q, p, h],
                                rs.at[c, h],
                                {"tensor": lax.rem(t + q, T)},
                            ).wait_send()

                sends.append(done)

    def take_rest(dst_ref, rs):
        for c in range(N):
            for h in (0, 1):

                @pl.when(frames[h] // FO != t)
                def _(c=c, h=h):
                    arrived(dst_ref.at[c, h], rs.at[c, h])

    sg, rg = ref["sg"], ref["rg"]
    for rc_index in range(R // RC):
        rows = pl.ds(rc_index * RC, RC)
        attn = dot(mr[0, rows, :], wof[0])
        for s in range(1, T):
            attn = attn + dot(mr[s, rows, :], wof[s])
        middle = xb[row_ds(t * R + rc_index * RC, RC, 64), :].astype(F32) + attn
        xhat, rstd = norm_parts(middle)
        sec = (xhat * vec[2:3, :] + vec[3:4, :]).astype(BF)
        second[rows, :] = sec
        cot = cb[rows, :]
        for s in range(T):
            for j in range(FFh // FT):
                cols = pl.ds(j * FT, FT)
                pre = dot(sec, wuf[s, :, cols]) + bf_[s, 0:1, cols]
                gact = dot(cot, wdf[s, cols, :], NT)
                sq = pre * pre
                th = jnp.tanh(c0 * pre * (1.0 + 0.044715 * sq))
                half = 0.5 * (1.0 + th)
                a = (pre * half).astype(BF)
                slope = half + 0.5 * pre * (1.0 - th * th) * (c0 * (1.0 + 0.134145 * sq))
                gp = (gact * slope).astype(BF)
                act[s, rows, cols] = a
                gpre[s, rows, cols] = gp
                sv[0, 4 + s : 5 + s, cols] = sv[0, 4 + s : 5 + s, cols] + jnp.sum(
                    gp.astype(F32), axis=0, keepdims=True
                )
                up = dot(a, wdf[s, cols, :])
                back = dot(gp, wuf[s, :, cols], NT)
                if s == 0 and j == 0:
                    mlp_sum[...] = up
                    sec_sum[...] = back
                else:
                    mlp_sum[...] = mlp_sum[...] + up
                    sec_sum[...] = sec_sum[...] + back
        ob[rows, :] = (middle + mlp_sum[...]).astype(BF)
        gsec = sec_sum[...]
        sv[0, 2:3, 0:D] = sv[0, 2:3, 0:D] + jnp.sum(gsec * xhat, axis=0, keepdims=True)
        sv[0, 3:4, 0:D] = sv[0, 3:4, 0:D] + jnp.sum(gsec, axis=0, keepdims=True)
        gm = cot.astype(F32) + norm_back(gsec, vec[2:3, :], xhat, rstd)
        gmid[rows, :] = gm
        low = gm.astype(BF)
        mlow[rows, :] = low
        for s in range(T):
            gst[s, rows, :] = dot(low, wof[s], NT).astype(BF)
            src = gst.at[s, rows]
            dst = gx.at[row_ds(t * R + rc_index * RC, RC, 64)]

            @pl.when(s == t)
            def _():
                gx[row_ds(t * R + rc_index * RC, RC, 64), :] = gst[s, rows, :]

            @pl.when(s != t)
            def _():
                remote(
                    src, dst, sg.at[s, rc_index], rg.at[t, rc_index], {"tensor": s}
                ).start()

            def done(s=s, src=src, dst=dst, rc_index=rc_index):
                @pl.when(s != t)
                def _():
                    remote(
                        src, dst, sg.at[s, rc_index], rg.at[t, rc_index], {"tensor": s}
                    ).wait_send()

            sends.append(done)
        for k in range(rc_index * RC // tok, (rc_index + 1) * RC // tok):
            give_back(ob, out_ref, ref["so"], ref["ro"], k)

    reduces = {}
    for name in cfg["plans"]:
        levels = cfg["plans"][name]
        bufs = [ref[f"{name}_buf{n}"] for n in range(len(levels))]
        reduces[name] = Reduce(
            levels, ref[name + "_acc"], ref[name + "_fin"], bufs, ref[name + "_ss"],
            ref[name + "_rs"], place,
        )
    cot = cb[...]
    for s in range(T):
        ref["down_acc"][s] = dot(act[s], cot, TN).astype(BF)
    reduces["down"].tick()
    for s in range(T):
        ref["up_acc"][s] = dot(second[...], gpre[s], TN).astype(BF)
    reduces["up"].tick()
    for s in range(T):
        ref["out_acc"][s] = dot(mr[s], mlow[...], TN).astype(BF)
    reduces["out"].tick()

    for p in range(1, T):
        s = lax.rem(t + p, T)
        for n in range(R // RC):
            arrived(gx.at[row_ds(s * R + n * RC, RC, 64)], rg.at[s, n])

    dk, dv, gpb = ref["dk"], ref["dv"], ref["gpb"]
    turns = 0
    for g in range(G):
        for qb in reversed(range(NQ)):
            K = (qb + 1) * QB
            rows = pl.ds(qb * QB, QB)
            keys = pl.ds(0, K)
            lanes = pl.ds(g * GW, GW)
            go = gx[rows, lanes]
            prod = go.astype(F32) * mo[rows, lanes].astype(F32)
            qv = qb_[g, rows, :]
            kv = kb_[g, keys, :]
            vv = vb_[g, keys, :]
            outs = []
            dk_sum = dv_sum = None
            for a in range(HG):
                delta = jnp.sum(only(prod, a), axis=-1, keepdims=True)
                goa = only(go, a)
                prob = probs[g * HG + a, rows, keys]
                gprob = dot(goa, vv, NT)
                gs = (prob.astype(F32) * (gprob - delta)).astype(BF)
                outs.append(dot(gs, kv))
                dk_part = dot(gs, only(qv, a), TN)
                dv_part = dot(prob, goa, TN)
                dk_sum = dk_part if dk_sum is None else dk_sum + dk_part
                dv_sum = dv_part if dv_sum is None else dv_sum + dv_part
            gpb[rows, lanes] = (pick(outs) * scale).astype(BF)
            if qb == NQ - 1:
                dk[keys, :] = dk_sum
                dv[keys, :] = dv_sum
            else:
                dk[keys, :] = dk[keys, :] + dk_sum
                dv[keys, :] = dv[keys, :] + dv_sum
            if turns == 1:
                pass_on(out_ref, ref["fo"], ref["ro"])
            reduces["down"].tick()
            reduces["up"].tick()
            reduces["out"].tick()
            turns += 1
        gpb[:, pl.ds(HW + g * GW, GW)] = dk[...].astype(BF)
        gpb[:, pl.ds(2 * HW + g * GW, GW)] = dv[...].astype(BF)

    gns, gnr = ref["gns"], ref["gnr"]
    for p in range(1, T):
        s = lax.rem(t + p, T)
        gns[p - 1] = dot(gpb[row_ds(s * R, R, 64), :], wqkv[...], NT).astype(BF)
        copy = remote(gns.at[p - 1], gnr.at[p - 1], ref["sn"].at[p - 1], ref["rn"].at[p - 1], {"tensor": s})
        copy.start()
        sends.append(copy.wait_send)
    ref["qkv_acc"][0] = dot(nb[...], gpb[...], TN).astype(BF)
    reduces["qkv"].tick()
    own = dot(gpb[row_ds(t * R, R, 64), :], wqkv[...], NT)
    for p in range(1, T):
        arrived(gnr.at[p - 1], ref["rn"].at[p - 1])
        own = own + gnr[p - 1].astype(F32)
    xhat, rstd = norm_parts(xb[row_ds(t * R, R, 64), :].astype(F32))
    sv[0, 0:1, 0:D] = jnp.sum(own * xhat, axis=0, keepdims=True)
    sv[0, 1:2, 0:D] = jnp.sum(own, axis=0, keepdims=True)
    igb = ref["igb"]
    igb[...] = (gmid[...] + norm_back(own, vec[0:1, :], xhat, rstd)).astype(BF)
    for k in range(FO):
        give_back(igb, ig_ref, ref["si"], ref["ri"], k)

    rsv = ref["rsv"]
    everyone = [(a, b) for a, n in (("ctx", N), ("dp", DP), ("tensor", T)) for b in bits_of(n)]
    for n, (axis, bit) in enumerate(everyone):
        copy = remote(
            sv.at[n], rsv.at[n], ref["sv_ss"].at[n], ref["sv_rs"].at[n],
            {axis: flip(place[axis], bit)},
        )
        copy.start()
        reduces["qkv"].tick()
        copy.wait()
        sv[n + 1] = sv[n] + rsv[n]
    pass_on(ig_ref, ref["fi"], ref["ri"])
    last = sv[len(everyone)]
    part = D // T
    gains = last[0:4, 0:part]
    bias = last[4:5, 0:FFh]
    for s in range(1, T):
        gains = jnp.where(t == s, last[0:4, s * part : (s + 1) * part], gains)
        bias = jnp.where(t == s, last[4 + s : 5 + s, 0:FFh], bias)
    ref["gains"][...] = gains
    ref["bias_out"][...] = bias

    for name in ("down", "up", "out", "qkv"):
        reduces[name].drain()
    take_rest(out_ref, ref["ro"])
    take_rest(ig_ref, ref["ri"])
    for done in sends:
        done()


def body(
    sizes,
    inputs,
    cotangent,
    live_frames,
    gain_attn,
    shift_attn,
    w_qkv,
    w_out,
    gain_mlp,
    shift_mlp,
    w_up,
    up_bias,
    w_down,
):
    N, T, DP = sizes["ctx"], sizes["tensor"], sizes["dp"]
    C, _, _, tok, D = inputs.shape
    heads, head_dim = w_qkv.shape[1], w_qkv.shape[2] // 3
    HW = heads * head_dim
    GW = min(128, HW)
    FFh = w_up.shape[1]
    L = 2 * N * tok
    R = L // T
    cfg = dict(
        N=N, T=T, DP=DP, L=L, R=R, FO=2 * N // T, tok=tok, D=D, HW=HW, GW=GW, G=HW // GW,
        FFh=FFh, QB=256, head_dim=head_dim,
    )
    G = cfg["G"]
    core, rest = [("ctx", 1)], [("ctx", b) for b in bits_of(N)[1:]]
    over_dp = [("dp", b) for b in bits_of(DP)]
    over_t = [("tensor", b) for b in reversed(bits_of(T))]
    cfg["plans"] = plans = {
        "down": plan_levels(T, FFh, core + over_dp + over_t + rest),
        "up": plan_levels(T, D, core + over_t + over_dp + rest),
        "out": plan_levels(T, HW, core + over_t + over_dp + rest),
        "qkv": plan_levels(1, D, core + over_dp + rest),
    }
    widths = {"down": D, "up": FFh, "out": D, "qkv": 3 * HW}
    leads = {"down": (T, FFh), "up": (T, D), "out": (T, HW), "qkv": (1, D)}

    x = inputs.reshape(C, 2, tok, D)
    cot = cotangent.reshape(C, 2, tok, D)
    wq = w_qkv.reshape(D, heads, 3, head_dim).transpose(0, 2, 1, 3).reshape(D, 3 * HW)
    vec = jnp.stack([gain_attn, shift_attn, gain_mlp, shift_mlp] * 2)
    bias = jnp.broadcast_to(up_bias[None], (8, FFh))

    vm = pl.BlockSpec(memory_space=pltpu.VMEM)
    hbm = pl.BlockSpec(memory_space=pl.ANY)
    ins = [
        ("x", x, hbm),
        ("cot", cot, hbm),
        ("live", live_frames, pl.BlockSpec(memory_space=pltpu.SMEM)),
        ("vec", vec, vm),
        ("w_qkv", wq, vm),
        ("w_out", w_out, hbm),
        ("w_up", w_up, hbm),
        ("w_down", w_down, hbm),
        ("bias", bias, vm),
    ]
    S = jax.ShapeDtypeStruct
    outs = [
        ("out", S((C, 2, tok, D), BF)),
        ("ig", S((C, 2, tok, D), BF)),
        ("down_fin", S((FFh, D), BF)),
        ("up_fin", S((D, FFh), BF)),
        ("out_fin", S((HW, D), BF)),
        ("qkv_fin", S((D, 3 * HW), BF)),
        ("gains", S((4, D // T), F32)),
        ("bias_out", S((1, FFh), F32)),
    ]
    W = max(D, FFh)
    SR = -(-(4 + T) // 8) * 8
    n_all = len(bits_of(N)) + len(bits_of(DP)) + len(bits_of(T))
    RC = min(256, R)
    piece = min(cfg["QB"], R)
    FO = cfg["FO"]
    dma = pltpu.SemaphoreType.DMA
    V = pltpu.VMEM
    scratch = dict(
        xb=V((L, D), BF), rx=dma((2 * N,)), sx=dma((N, 2)), fx=dma((T, FO)),
        cb=V((R, D), BF), rc=dma((FO,)), sc=dma((N, 2)),
        w_out_full=V((T, HW, D), BF), w_up_full=V((T, D, FFh), BF),
        w_down_full=V((T, FFh, D), BF), bias_full=V((T, 8, FFh), F32),
        rw=dma((4, 4, T)), sw=dma((4, 4, T)), lw=dma((4,)),
        nb=V((L, D), BF), q=V((G, L, GW), BF), k=V((G, L, GW), BF), v=V((G, L, GW), BF),
        probs=V((heads, L, L), BF), mo=V((L, HW), BF), mr=V((T, R, HW), BF),
        rm=dma((T, R // piece, G)), sm=dma((L // piece, G)),
        second=V((R, D), BF), act=V((T, R, FFh), BF), gpre=V((T, R, FFh), BF),
        mlow=V((R, D), BF), gmid=V((R, D), F32), gst=V((T, R, HW), BF), gx=V((L, HW), BF),
        sg=dma((T, R // RC)), rg=dma((T, R // RC)),
        ob=V((R, D), BF), so=dma((FO,)), ro=dma((N, 2)), fo=dma((T, N, 2)),
        igb=V((R, D), BF), si=dma((FO,)), ri=dma((N, 2)), fi=dma((T, N, 2)),
        mlp_sum=V((RC, D), F32), sec_sum=V((RC, D), F32),
        sv=V((n_all + 1, SR, W), F32), rsv=V((n_all, SR, W), F32),
        sv_ss=dma((n_all,)), sv_rs=dma((n_all,)),
        dk=V((L, GW), F32), dv=V((L, GW), F32), gpb=V((L, 3 * HW), BF),
        gns=V((max(T - 1, 1), R, D), BF), gnr=V((max(T - 1, 1), R, D), BF),
        sn=dma((T,)), rn=dma((T,)),
    )
    for name, levels in plans.items():
        scratch[name + "_acc"] = V(leads[name] + (widths[name],), BF)
        scratch[name + "_ss"] = dma((2 * len(levels),))
        scratch[name + "_rs"] = dma((2 * len(levels),))
        for n, (_, _, _, lead, rows) in enumerate(levels):
            scratch[f"{name}_buf{n}"] = V((lead, rows, widths[name]), BF)
    names = [n for n, *_ in ins] + [n for n, _ in outs] + list(scratch)
    results = pl.pallas_call(
        functools.partial(kernel, cfg, names),
        out_shape=[s for _, s in outs],
        in_specs=[s for _, _, s in ins],
        out_specs=[vm] * len(outs),
        scratch_shapes=list(scratch.values()),
        compiler_params=pltpu.CompilerParams(
            collective_id=0, has_side_effects=True, vmem_limit_bytes=60 * 2**20
        ),
    )(*[a for _, a, _ in ins])
    got = dict(zip([n for n, _ in outs], results))
    grad_qkv = (
        got["qkv_fin"]
        .reshape(D, 3, heads, head_dim)
        .transpose(0, 2, 1, 3)
        .reshape(w_qkv.shape)
        .astype(F32)
    )
    gains = got["gains"]
    return (
        got["out"].reshape(inputs.shape),
        got["ig"].reshape(inputs.shape),
        gains[0],
        gains[1],
        grad_qkv,
        got["out_fin"].astype(F32),
        gains[2],
        gains[3],
        got["up_fin"].astype(F32),
        got["bias_out"][0],
        got["down_fin"].astype(F32),
    )


def solution(mesh):
    return jax.shard_map(
        functools.partial(body, dict(mesh.shape)),
        mesh=mesh,
        in_specs=(
            P("dp", None, "ctx", None, None),
            P("dp", None, "ctx", None, None),
            P("dp"),
            P(),
            P(),
            P(None, "tensor", None),
            P("tensor", None),
            P(),
            P(),
            P(None, "tensor"),
            P("tensor"),
            P("tensor", None),
        ),
        out_specs=(
            P("dp", None, "ctx", None, None),
            P("dp", None, "ctx", None, None),
            P("tensor"),
            P("tensor"),
            P(None, "tensor", None),
            P("tensor", None),
            P("tensor"),
            P("tensor"),
            P(None, "tensor"),
            P("tensor"),
            P("tensor", None),
        ),
        check_vma=False,
    )
```

```python
import functools
from types import SimpleNamespace

import jax
import jax.numpy as jnp
from jax import lax
from jax.experimental import pallas as pl
from jax.experimental.pallas import tpu as pltpu
from jax.sharding import PartitionSpec as P

PATCH = 64
EPSILON = 1e-05
MESH = pl.DeviceIdType.MESH
BF = jnp.bfloat16
F32 = jnp.float32

NN = (((1,), (0,)), ((), ()))
NT = (((1,), (1,)), ((), ()))
TN = (((0,), (0,)), ((), ()))


def dot(a, b, dims=NN):
    return lax.dot_general(a, b, dims, preferred_element_type=F32)


def bits_of(size):
    found, bit = [], 1
    while bit < size:
        found.append(bit)
        bit *= 2
    return found


def flip(index, bit):
    return index + bit - 2 * bit * ((index // bit) % 2)


def bit_of(index, bit):
    return (index // bit) % 2


def row_ds(start, size, unit=16):
    return pl.ds(pl.multiple_of(start, unit), size)


def remote(src, dst, send_sem, recv_sem, where):
    return pltpu.make_async_remote_copy(
        src_ref=src,
        dst_ref=dst,
        send_sem=send_sem,
        recv_sem=recv_sem,
        device_id=where,
        device_id_type=MESH,
    )


def arrived(dst, sem):
    pltpu.make_async_copy(dst, dst, sem).wait()


def norm_parts(values):
    mean = jnp.mean(values, axis=-1, keepdims=True)
    centered = values - mean
    var = jnp.mean(centered * centered, axis=-1, keepdims=True)
    rstd = lax.rsqrt(var + EPSILON)
    return centered * rstd, rstd


def norm_back(grad, gain, xhat, rstd):
    scaled = grad * gain
    first = jnp.mean(scaled, axis=-1, keepdims=True)
    second = jnp.mean(scaled * xhat, axis=-1, keepdims=True)
    return rstd * (scaled - first - xhat * second)


def plan_levels(lead, rows, order):
    levels = []
    for axis, bit, *forced in order:
        if forced:
            kind = forced[0]
            rows = rows // 2 if kind == "p" else rows
        elif axis == "tensor":
            lead //= 2
            kind = "t"
        elif rows % 32 == 0:
            rows //= 2
            kind = "r"
        else:
            kind = "f"
        levels.append((axis, bit, kind, lead, rows))
    return levels


ORDERS = {
    "down0": "yxzZ",
    "down1": "xzyZ",
    "up0": "zyxZ",
    "up1": "yxzZ",
    "out": "xyzR",
    "qkv0": "yxzZ",
    "qkv1": "xyzZ",
}
CHUNKS = tuple(ORDERS)
VECTORS, OUTPUT, INPUT_GRAD, MARK = range(7, 11)
ORDER = tuple(CHUNKS[n] for n in (2, 3, 0, 1))
SCRIPT = (
    10, 3, 2, 0, 1, 4, 10, 10, 10, 8, 10, 8, 5, 10, 10, 8, 10, 3, 10, 8, 1, 6, 10, 4, 2, 7, 0,
    3, 1, 6, 9, 0, 9, 5, 7, 9, 3, 9, 0, 5, 7, 4, 3, 5, 7, 2, 4, 0, 1, 3, 6, 5, 2, 4, 0, 6, 1, 3,
    5, 3, 2, 0, 4, 1, 0, 5, 6, 4, 5, 2, 7, 6, 1, 1, 4, 4, 2, 2, 6, 6,
)


class Reduce:
    def __init__(self, levels, acc, fin, bufs, ss, rs, place):
        self.levels, self.acc, self.fin = levels, acc, fin
        self.bufs, self.ss, self.rs, self.place = bufs, ss, rs, place
        self.lead, self.rows = acc.shape[0], acc.shape[1]
        self.toff, self.roff = 0, 0
        self.marks = []
        self.copy = None
        self.steps = []
        count = len(levels)
        for n in range(count):
            self.steps.append(functools.partial(self.step, n))
        self.steps.append(self.turn)

    def send(self, n):
        axis, bit, kind, lead, rows = self.levels[n]
        mine = bit_of(self.place[axis], bit)
        self.marks.append((self.toff, self.roff, self.lead, self.rows))
        toff, roff = self.toff, self.roff
        dst = self.bufs[n]
        if kind == "p":
            toff = mine
            roff = self.roff + (1 - mine) * rows
            self.roff = self.roff + mine * rows
            dst = self.acc.at[pl.ds(toff, 1), row_ds(roff, rows)]
            self.copy = remote(
                dst, dst, self.ss.at[n], self.rs.at[n], {axis: flip(self.place[axis], bit)}
            )
            self.lead, self.rows = lead, rows
            self.copy.start()
            return
        if kind == "t":
            toff = self.toff + (1 - mine) * lead
            self.toff = self.toff + mine * lead
        elif kind == "r":
            roff = self.roff + (1 - mine) * rows
            self.roff = self.roff + mine * rows
        self.lead, self.rows = lead, rows
        self.copy = remote(
            self.acc.at[pl.ds(toff, lead), row_ds(roff, rows)],
            dst,
            self.ss.at[n],
            self.rs.at[n],
            {axis: flip(self.place[axis], bit)},
        )
        self.copy.start()

    def absorb(self, n):
        self.copy.wait()
        if self.levels[n][2] == "p":
            return
        buf = self.bufs[n]
        part = 32 if self.rows % 32 == 0 else 16
        for a in range(self.lead):

            def add(b, _):
                off = pl.multiple_of(b * part, 16)
                at = row_ds(self.roff + off, part)
                old = self.acc[self.toff + a, at, :].astype(F32)
                new = buf[a, pl.ds(off, part), :].astype(F32)
                self.acc[self.toff + a, at, :] = (old + new).astype(BF)
                return 0

            lax.fori_loop(0, self.rows // part, add, 0)

    def step(self, n):
        if n > 0:
            self.absorb(n - 1)
        self.send(n)

    def turn(self):
        count = len(self.levels)
        self.absorb(count - 1)
        at = row_ds(self.roff, self.rows)
        self.fin[at, :] = self.acc[self.toff, at, :]
        back = [n for n in reversed(range(count)) if self.levels[n][2] in "pr"]
        for k, n in enumerate(back):
            if k == 0:
                self.gather(n, True)
            else:
                self.steps.append(functools.partial(self.gather, n, False))
        self.steps.append(self.close)

    def gather(self, n, first):
        if not first:
            self.copy.wait()
        axis, bit, kind, lead, rows = self.levels[n]
        part = self.fin.at[row_ds(self.roff, rows)]
        count = len(self.levels)
        self.copy = remote(
            part,
            part,
            self.ss.at[count + n],
            self.rs.at[count + n],
            {axis: flip(self.place[axis], bit)},
        )
        self.copy.start()
        self.roff = self.marks[n][1]

    def close(self):
        self.copy.wait()

    def tick(self):
        if self.steps:
            self.steps.pop(0)()
            return True
        return False

    def drain(self):
        while self.tick():
            pass


def spread_kernel(cfg, names, *refs):
    ref = SimpleNamespace(**dict(zip(names, refs)))
    N, T, DP = cfg.N, cfg.T, cfg.DP
    L, R, FO, tok = cfg.L, cfg.R, cfg.FO, cfg.tok
    D, HW, GW, G, FFh, QB = cfg.D, cfg.HW, cfg.GW, cfg.G, cfg.FFh, cfg.QB
    head_dim = cfg.head_dim
    HG = GW // head_dim
    scale = head_dim ** (-0.5)
    d = lax.axis_index("dp")
    i = lax.axis_index("ctx")
    t = lax.axis_index("tensor")
    place = {"dp": d, "ctx": i, "tensor": t}
    x_in, cot_in = ref.x, ref.cot
    sends = []

    bar = pltpu.get_barrier_semaphore()
    peers = [{"ctx": lax.rem(i + p, N)} for p in range(1, N)]
    peers += [{"tensor": lax.rem(t + p, T)} for p in range(1, T)]
    peers += [{"dp": flip(d, b)} for b in bits_of(DP)]
    for peer in peers:
        pl.semaphore_signal(bar, inc=1, device_id=peer, device_id_type=MESH)
    pl.semaphore_wait(bar, len(peers))

    frames = (i, 2 * N - 1 - i)

    def owns(h):
        return frames[h] // FO == t

    xb, rx, sx, fx = ref.xb, ref.rx, ref.sx, ref.fx
    for p in range(N):
        c = lax.rem(i + p, N)
        for h in (0, 1):
            to = xb.at[row_ds(frames[h] * tok, tok)]

            @pl.when(owns(h))
            def _(p=p, c=c, h=h, to=to):
                if p == 0:
                    pltpu.make_async_copy(x_in.at[c, h], to, rx.at[frames[h]]).start()
                else:
                    remote(
                        x_in.at[c, h], to, sx.at[p, h], rx.at[frames[h]], {"ctx": c}
                    ).start()

            if p > 0:

                def done(p=p, c=c, h=h, to=to):
                    @pl.when(owns(h))
                    def _():
                        remote(
                            x_in.at[c, h], to, sx.at[p, h], rx.at[frames[h]], {"ctx": c}
                        ).wait_send()

                sends.append(done)

    def near(k):
        return t * FO + lax.rem(i + k, FO)

    for k in range(FO):
        f = near(k)
        part = xb.at[row_ds(f * tok, tok)]
        arrived(part, rx.at[f])
        for p in range(1, T):
            copy = remote(
                part, part, fx.at[p, k], rx.at[f], {"tensor": lax.rem(t + p, T)}
            )
            copy.start()
            sends.append(copy.wait_send)

    cb, rc, sc = ref.cb, ref.rc, ref.sc
    for p in range(N):
        c = lax.rem(i + p, N)
        for h in (0, 1):
            slot = lax.rem(frames[h], FO)
            to = cb.at[row_ds(slot * tok, tok)]

            @pl.when(owns(h))
            def _(p=p, c=c, h=h, to=to, slot=slot):
                if p == 0:
                    pltpu.make_async_copy(cot_in.at[c, h], to, rc.at[slot]).start()
                else:
                    remote(cot_in.at[c, h], to, sc.at[p, h], rc.at[slot], {"ctx": c}).start()

            if p > 0:

                def done(p=p, c=c, h=h, to=to, slot=slot):
                    @pl.when(owns(h))
                    def _():
                        remote(
                            cot_in.at[c, h], to, sc.at[p, h], rc.at[slot], {"ctx": c}
                        ).wait_send()

                sends.append(done)

    share = 2 * lax.rem(d, 2) + lax.rem(i, 2)
    wide = ("w_out", "w_up", "w_down")
    full = {n: getattr(ref, n + "_full") for n in wide + ("bias",)}
    rw, sw, lw = ref.rw, ref.sw, ref.lw
    own_copies = []
    for n, name in enumerate(wide + ("bias",)):
        copy = pltpu.make_async_copy(getattr(ref, name), full[name].at[t], lw.at[n])
        copy.start()
        own_copies.append(copy)
    for p in range(1, T):
        to = {"tensor": lax.rem(t + p, T)}
        copy = remote(ref.bias, full["bias"].at[t], sw.at[3, 0, p], rw.at[3, 0, t], to)
        copy.start()
        sends.append(copy.wait_send)
    for n, name in enumerate(wide):
        quarter = getattr(ref, name).shape[0] // 4
        at = row_ds(share * quarter, quarter)
        for p in range(1, T):
            to = {"tensor": lax.rem(t + p, T)}
            copy = remote(
                getattr(ref, name).at[at], full[name].at[t, at], sw.at[n, 0, p], rw.at[n, 0, t], to
            )
            copy.start()
            sends.append(copy.wait_send)

    other_dp = 2 * (1 - lax.rem(d, 2)) + lax.rem(i, 2)
    other_core = 2 * lax.rem(d, 2) + 1 - lax.rem(i, 2)
    other_both = 2 * (1 - lax.rem(d, 2)) + 1 - lax.rem(i, 2)

    def weight_part(name, s, which):
        quarter = getattr(ref, name).shape[0] // 4
        return full[name].at[s, row_ds(which * quarter, quarter)]

    def weights_second(n, name):
        for p in range(1, T):
            s = lax.rem(t + p, T)
            part = weight_part(name, s, share)
            arrived(part, rw.at[n, 0, s])
            for stage, to in ((1, {"dp": flip(d, 1)}), (2, {"ctx": flip(i, 1)})):
                copy = remote(part, part, sw.at[n, stage, p], rw.at[n, stage, s], to)
                copy.start()
                sends.append(copy.wait_send)

    def weights_third(n, name):
        for p in range(1, T):
            s = lax.rem(t + p, T)
            part = weight_part(name, s, other_dp)
            arrived(part, rw.at[n, 1, s])
            copy = remote(
                part, part, sw.at[n, 3, p], rw.at[n, 3, s], {"ctx": flip(i, 1)}
            )
            copy.start()
            sends.append(copy.wait_send)

    def weights_ready(n, name):
        own_copies[n].wait()
        for p in range(1, T):
            s = lax.rem(t + p, T)
            if name == "bias":
                arrived(full[name].at[s], rw.at[n, 0, s])
            else:
                arrived(weight_part(name, s, other_core), rw.at[n, 2, s])
                arrived(weight_part(name, s, other_both), rw.at[n, 3, s])

    RB = min(256, R)
    nb, qb_, kb_, vb_ = ref.nb, ref.q, ref.k, ref.v
    vec = (ref.gain_attn, ref.shift_attn, ref.gain_mlp, ref.shift_mlp)
    wqkv = ref.w_qkv

    def project(start):
        rows = row_ds(start, RB, 64)
        xhat, _ = norm_parts(xb[rows, :].astype(F32))
        normed = (xhat * vec[0][...] + vec[1][...]).astype(BF)
        nb[rows, :] = normed
        packed = dot(normed, wqkv[...])
        for g in range(G):
            lo = g * GW
            qb_[g, rows, :] = (packed[:, lo : lo + GW].astype(BF).astype(F32) * scale).astype(BF)
            kb_[g, rows, :] = packed[:, HW + lo : HW + lo + GW].astype(BF)
            vb_[g, rows, :] = packed[:, 2 * HW + lo : 2 * HW + lo + GW].astype(BF)

    for k in range(R // RB):
        project(t * R + k * RB)
    for p in range(1, T):
        s = lax.rem(t + p, T)
        for k in range(FO):
            f = s * FO + k
            arrived(xb.at[row_ds(f * tok, tok)], rx.at[f])
        for k in range(R // RB):
            project(s * R + k * RB)

    for n, name in enumerate(wide):
        weights_second(n, name)

    live = ref.live[i]
    probs, mo, mr = ref.probs, ref.mo, ref.mr
    rm, sm = ref.rm, ref.sm
    piece = min(QB, R)
    NQ = L // QB
    lane = lax.broadcasted_iota(jnp.int32, (QB, GW), 1) // head_dim

    def pick(parts):
        out = parts[0]
        for a in range(1, HG):
            out = jnp.where(lane == a, parts[a], out)
        return out

    def only(values, a):
        if HG == 1:
            return values
        return jnp.where(lane == a, values, jnp.zeros_like(values))

    def hand_over(qb, g):
        for b in range(QB // piece):
            row = qb * QB + b * piece
            s = row // R
            slot = (row - s * R) // piece
            src = mo.at[pl.ds(row, piece), pl.ds(g * GW, GW)]
            dst = mr.at[t, pl.ds(row - s * R, piece), pl.ds(g * GW, GW)]
            index = row // piece

            @pl.when(s == t)
            def _():
                mr[t, pl.ds(row - s * R, piece), pl.ds(g * GW, GW)] = mo[
                    pl.ds(row, piece), pl.ds(g * GW, GW)
                ]

            @pl.when(s != t)
            def _():
                remote(src, dst, sm.at[index, g], rm.at[t, slot, g], {"tensor": s}).start()

            def done(s=s, src=src, dst=dst, index=index, slot=slot):
                @pl.when(s != t)
                def _():
                    remote(
                        src, dst, sm.at[index, g], rm.at[t, slot, g], {"tensor": s}
                    ).wait_send()

            sends.append(done)

    pumps = [functools.partial(weights_third, n, name) for n, name in enumerate(wide)]
    def mask_shift(qb):
        K = (qb + 1) * QB
        row_frame = (qb * QB + lax.broadcasted_iota(jnp.int32, (QB, K), 0)) // PATCH
        col_frame = lax.broadcasted_iota(jnp.int32, (QB, K), 1) // PATCH
        allowed = (col_frame <= row_frame) & (col_frame < live)
        return jnp.where(allowed, 0.0, -1e30)

    def attend_block(qb, g, shift):
        K = (qb + 1) * QB
        rows = pl.ds(qb * QB, QB)
        qv = qb_[g, rows, :]
        kv = kb_[g, pl.ds(0, K), :]
        vv = vb_[g, pl.ds(0, K), :]
        outs = []
        for a in range(HG):
            scores = dot(only(qv, a), kv, NT) + shift
            top = jnp.max(scores, axis=-1, keepdims=True)
            weights = jnp.exp(scores - top)
            total = jnp.sum(weights, axis=-1, keepdims=True)
            prob = (weights * (1.0 / total)).astype(BF)
            probs[g * HG + a, rows, pl.ds(0, K)] = prob
            outs.append(dot(prob, vv))
        mo[rows, pl.ds(g * GW, GW)] = pick(outs).astype(BF)

    for qb in reversed(range(NQ)):
        shift = mask_shift(qb)
        for g in range(G):
            attend_block(qb, g, shift)
            hand_over(qb, g)
        if pumps:
            pumps.pop(0)()
    while pumps:
        pumps.pop(0)()

    for n, name in enumerate(wide + ("bias",)):
        weights_ready(n, name)
    for p in range(1, T):
        s = lax.rem(t + p, T)
        for slot in range(R // piece):
            for g in range(G):
                arrived(
                    mr.at[s, pl.ds(slot * piece, piece), pl.ds(g * GW, GW)], rm.at[s, slot, g]
                )
    for k in range(FO):
        arrived(cb.at[pl.ds(k * tok, tok)], rc.at[k])

    wof, wuf, wdf, bf_ = full["w_out"], full["w_up"], full["w_down"], full["bias"]
    second, act, gpre = ref.second, ref.act, ref.gpre
    mlow, gmid, gst, gx = ref.mlow, ref.gmid, ref.gst, ref.gx
    ob, out_ref, ig_ref = ref.ob, ref.out, ref.ig
    sv = ref.sv
    mlp_sum, sec_sum = ref.mlp_sum, ref.sec_sum
    RC = min(256, R)
    FT = min(512, FFh)
    c0 = 0.7978845608028654
    sv[0] = jnp.zeros_like(sv[0])

    def frame_home(k):
        f = t * FO + k
        high = f // N
        j = f * (1 - high) + (2 * N - 1 - f) * high
        return j, high

    def give_back(buf, dst_ref, ss, rs, k):
        j, h = frame_home(k)
        src = buf.at[pl.ds(k * tok, tok)]

        @pl.when(j == i)
        def _():
            pltpu.make_async_copy(src, dst_ref.at[i, h], rs.at[i, h]).start()

        @pl.when(j != i)
        def _():
            remote(src, dst_ref.at[i, h], ss.at[k], rs.at[i, h], {"ctx": j}).start()

        def done():
            @pl.when(j != i)
            def _():
                remote(src, dst_ref.at[i, h], ss.at[k], rs.at[i, h], {"ctx": j}).wait_send()

        sends.append(done)

    def pass_on(dst_ref, fs, rs):
        for p in range(N):
            c = lax.rem(i + p, N)
            for h in (0, 1):
                part = dst_ref.at[c, h]

                @pl.when(owns(h))
                def _(p=p, c=c, h=h, part=part):
                    arrived(part, rs.at[c, h])
                    for q in range(1, T):
                        remote(
                            part, part, fs.at[q, p, h], rs.at[c, h], {"tensor": lax.rem(t + q, T)}
                        ).start()

                def done(p=p, c=c, h=h, part=part):
                    @pl.when(owns(h))
                    def _():
                        for q in range(1, T):
                            remote(
                                part,
                                part,
                                fs.at[q, p, h],
                                rs.at[c, h],
                                {"tensor": lax.rem(t + q, T)},
                            ).wait_send()

                sends.append(done)

    def take_rest(dst_ref, rs):
        for c in range(N):
            for h in (0, 1):

                @pl.when(frames[h] // FO != t)
                def _(c=c, h=h):
                    arrived(dst_ref.at[c, h], rs.at[c, h])

    sg, rg = ref.sg, ref.rg
    def feed_forward(rc_index):
        rows = pl.ds(rc_index * RC, RC)
        attn = dot(mr[0, rows, :], wof[0])
        for s in range(1, T):
            attn = attn + dot(mr[s, rows, :], wof[s])
        middle = xb[row_ds(t * R + rc_index * RC, RC, 64), :].astype(F32) + attn
        xhat, rstd = norm_parts(middle)
        sec = (xhat * vec[2][...] + vec[3][...]).astype(BF)
        second[rows, :] = sec
        cot = cb[rows, :]
        for s in range(T):
            for j in range(FFh // FT):
                cols = pl.ds(j * FT, FT)
                pre = dot(sec, wuf[s, :, cols]) + bf_[s, 0:1, cols]
                gact = dot(cot, wdf[s, cols, :], NT)
                sq = pre * pre
                th = jnp.tanh(c0 * pre * (1.0 + 0.044715 * sq))
                half = 0.5 * (1.0 + th)
                a = (pre * half).astype(BF)
                slope = half + 0.5 * pre * (1.0 - th * th) * (c0 * (1.0 + 0.134145 * sq))
                gp = (gact * slope).astype(BF)
                act[s, rows, cols] = a
                gpre[s, rows, cols] = gp
                sv[0, 4 + s : 5 + s, cols] = sv[0, 4 + s : 5 + s, cols] + jnp.sum(
                    gp.astype(F32), axis=0, keepdims=True
                )
                up = dot(a, wdf[s, cols, :])
                back = dot(gp, wuf[s, :, cols], NT)
                if s == 0 and j == 0:
                    mlp_sum[...] = up
                    sec_sum[...] = back
                else:
                    mlp_sum[...] = mlp_sum[...] + up
                    sec_sum[...] = sec_sum[...] + back
        ob[rows, :] = (middle + mlp_sum[...]).astype(BF)
        gsec = sec_sum[...]
        sv[0, 2:3, 0:D] = sv[0, 2:3, 0:D] + jnp.sum(gsec * xhat, axis=0, keepdims=True)
        sv[0, 3:4, 0:D] = sv[0, 3:4, 0:D] + jnp.sum(gsec, axis=0, keepdims=True)
        gm = cot.astype(F32) + norm_back(gsec, vec[2][...], xhat, rstd)
        gmid[rows, :] = gm
        low = gm.astype(BF)
        mlow[rows, :] = low
        for s in range(T):
            gst[s, rows, :] = dot(low, wof[s], NT).astype(BF)

    for rc_index in range(R // RC):
        rows = pl.ds(rc_index * RC, RC)
        feed_forward(rc_index)
        for s in range(T):
            src = gst.at[s, rows]
            dst = gx.at[row_ds(t * R + rc_index * RC, RC, 64)]

            @pl.when(s == t)
            def _():
                gx[row_ds(t * R + rc_index * RC, RC, 64), :] = gst[s, rows, :]

            @pl.when(s != t)
            def _():
                remote(
                    src, dst, sg.at[s, rc_index], rg.at[t, rc_index], {"tensor": s}
                ).start()

            def done(s=s, src=src, dst=dst, rc_index=rc_index):
                @pl.when(s != t)
                def _():
                    remote(
                        src, dst, sg.at[s, rc_index], rg.at[t, rc_index], {"tensor": s}
                    ).wait_send()

            sends.append(done)
        for k in range(rc_index * RC // tok, (rc_index + 1) * RC // tok):
            give_back(ob, out_ref, ref.so, ref.ro, k)

    reduces = {}
    for name in cfg.plans:
        levels = cfg.plans[name]
        bufs = [getattr(ref, name + "_buf" + str(n)) for n in range(len(levels))]
        reduces[name] = Reduce(
            levels, getattr(ref, name + "_acc"), getattr(ref, name + "_fin"), bufs, getattr(ref, name + "_ss"),
            getattr(ref, name + "_rs"), place,
        )
    cot = cb[...]
    for s in range(T):
        ref.down_acc[s] = dot(act[s], cot, TN).astype(BF)
    reduces["down"].tick()
    for s in range(T):
        ref.up_acc[s] = dot(second[...], gpre[s], TN).astype(BF)
    reduces["up"].tick()
    for s in range(T):
        ref.out_acc[s] = dot(mr[s], mlow[...], TN).astype(BF)
    reduces["out"].tick()

    for p in range(1, T):
        s = lax.rem(t + p, T)
        for n in range(R // RC):
            arrived(gx.at[row_ds(s * R + n * RC, RC, 64)], rg.at[s, n])

    dk, dv, gpb = ref.dk, ref.dv, ref.gpb

    def attend_back_block(g, qb):
        K = (qb + 1) * QB
        rows = pl.ds(qb * QB, QB)
        keys = pl.ds(0, K)
        lanes = pl.ds(g * GW, GW)
        go = gx[rows, lanes]
        prod = go.astype(F32) * mo[rows, lanes].astype(F32)
        qv = qb_[g, rows, :]
        kv = kb_[g, keys, :]
        vv = vb_[g, keys, :]
        outs = []
        dk_sum = dv_sum = None
        for a in range(HG):
            delta = jnp.sum(only(prod, a), axis=-1, keepdims=True)
            goa = only(go, a)
            prob = probs[g * HG + a, rows, keys]
            gprob = dot(goa, vv, NT)
            gs = (prob.astype(F32) * (gprob - delta)).astype(BF)
            outs.append(dot(gs, kv))
            dk_part = dot(gs, only(qv, a), TN)
            dv_part = dot(prob, goa, TN)
            dk_sum = dk_part if dk_sum is None else dk_sum + dk_part
            dv_sum = dv_part if dv_sum is None else dv_sum + dv_part
        gpb[rows, lanes] = (pick(outs) * scale).astype(BF)
        if qb == NQ - 1:
            dk[keys, :] = dk_sum
            dv[keys, :] = dv_sum
        else:
            dk[keys, :] = dk[keys, :] + dk_sum
            dv[keys, :] = dv[keys, :] + dv_sum

    turns = 0
    for g in range(G):
        for qb in reversed(range(NQ)):
            attend_back_block(g, qb)
            if turns == 1:
                pass_on(out_ref, ref.fo, ref.ro)
            reduces["down"].tick()
            reduces["up"].tick()
            reduces["out"].tick()
            turns += 1
        gpb[:, pl.ds(HW + g * GW, GW)] = dk[...].astype(BF)
        gpb[:, pl.ds(2 * HW + g * GW, GW)] = dv[...].astype(BF)

    gns, gnr = ref.gns, ref.gnr
    for p in range(1, T):
        s = lax.rem(t + p, T)
        gns[p - 1] = dot(gpb[row_ds(s * R, R, 64), :], wqkv[...], NT).astype(BF)
        copy = remote(gns.at[p - 1], gnr.at[p - 1], ref.sn.at[p - 1], ref.rn.at[p - 1], {"tensor": s})
        copy.start()
        sends.append(copy.wait_send)
    ref.qkv_acc[0] = dot(nb[...], gpb[...], TN).astype(BF)
    reduces["qkv"].tick()
    own = dot(gpb[row_ds(t * R, R, 64), :], wqkv[...], NT)
    for p in range(1, T):
        arrived(gnr.at[p - 1], ref.rn.at[p - 1])
        own = own + gnr[p - 1].astype(F32)
    xhat, rstd = norm_parts(xb[row_ds(t * R, R, 64), :].astype(F32))
    sv[0, 0:1, 0:D] = jnp.sum(own * xhat, axis=0, keepdims=True)
    sv[0, 1:2, 0:D] = jnp.sum(own, axis=0, keepdims=True)
    igb = ref.igb
    igb[...] = (gmid[...] + norm_back(own, vec[0][...], xhat, rstd)).astype(BF)
    for k in range(FO):
        give_back(igb, ig_ref, ref.si, ref.ri, k)

    rsv = ref.rsv
    everyone = [(a, b) for a, n in (("ctx", N), ("dp", DP), ("tensor", T)) for b in bits_of(n)]
    for n, (axis, bit) in enumerate(everyone):
        copy = remote(
            sv.at[n], rsv.at[n], ref.sv_ss.at[n], ref.sv_rs.at[n],
            {axis: flip(place[axis], bit)},
        )
        copy.start()
        reduces["qkv"].tick()
        copy.wait()
        sv[n + 1] = sv[n] + rsv[n]
    pass_on(ig_ref, ref.fi, ref.ri)
    last = sv[len(everyone)]
    part = D // T
    gains = last[0:4, 0:part]
    bias = last[4:5, 0:FFh]
    for s in range(1, T):
        gains = jnp.where(t == s, last[0:4, s * part : (s + 1) * part], gains)
        bias = jnp.where(t == s, last[4 + s : 5 + s, 0:FFh], bias)
    for n, got in enumerate((ref.grad_ga, ref.grad_sa, ref.grad_gm, ref.grad_sm)):
        got[...] = gains[n : n + 1, :]
    ref.bias_out[...] = bias

    for name in ("down", "up", "out", "qkv"):
        reduces[name].drain()
    take_rest(out_ref, ref.ro)
    take_rest(ig_ref, ref.ri)
    for done in sends:
        done()


def chip_kernel(cfg, names, *refs):
    ref = SimpleNamespace(**dict(zip(names, refs)))
    N, T, DP = cfg.N, cfg.T, cfg.DP
    L, R, FO, tok = cfg.L, cfg.R, cfg.FO, cfg.tok
    D, HW, GW, G, FFh, QB = cfg.D, cfg.HW, cfg.GW, cfg.G, cfg.FFh, cfg.QB
    head_dim = cfg.head_dim
    Z = N // 2
    HG = GW // head_dim
    scale = head_dim ** (-0.5)
    d = lax.axis_index("dp")
    i = lax.axis_index("ctx")
    t = lax.axis_index("tensor")
    z, kap = i // 2, lax.rem(i, 2)
    clip = 2 * z + t
    mate, mirror, beside = {"ctx": flip(i, 1)}, {"tensor": 1 - t}, {"dp": flip(d, 1)}
    place = {"dp": d, "ctx": i, "tensor": t}
    x_in, cot_in = ref.x, ref.cot
    sends = []

    def go(src, dst, send_sem, recv_sem, where):
        copy = remote(src, dst, send_sem, recv_sem, where)
        copy.start()
        sends.append(copy.wait_send)

    def go_if(cond, *args):
        @pl.when(cond)
        def _():
            remote(*args).start()

        def done():
            @pl.when(cond)
            def _():
                remote(*args).wait_send()

        sends.append(done)

    bar = pltpu.get_barrier_semaphore()
    peers = [{"ctx": lax.rem(i + p, N)} for p in range(1, N)]
    peers += [mirror] + [{"dp": flip(d, b)} for b in bits_of(DP)]
    for peer in peers:
        pl.semaphore_signal(bar, inc=1, device_id=peer, device_id_type=MESH)

    wqkv, rq = ref.wq, ref.rq
    blocks = []
    for n in range(HW // head_dim):
        for b in range(3):
            src = ref.w_qkv.at[n, pl.ds(b * head_dim, head_dim)]
            dst = wqkv.at[pl.ds(b * HW + n * head_dim, head_dim)]
            blocks.append((src, dst, ref.bq.at[3 * n + b]))

    @pl.when(kap == t)
    def _():
        for block in blocks:
            pltpu.make_async_copy(*block).start()
        for block in blocks:
            pltpu.make_async_copy(*block).wait()

    pl.semaphore_wait(bar, len(peers))

    frames = (i, 2 * N - 1 - i)

    def deal(src_ref, dst_ref, spot, ss, rs):
        for p in range(Z):
            zz = lax.rem(z + p, Z)
            for h in (0, 1):
                src = src_ref.at[2 * zz + t, h]
                dst = dst_ref.at[row_ds(spot(h) * tok, tok)]
                to = {"ctx": 2 * zz + h}
                sem = rs.at[spot(h)]
                if p == 0:

                    @pl.when(kap == h)
                    def _(src=src, dst=dst, sem=sem):
                        pltpu.make_async_copy(src, dst, sem).start()

                    go_if(kap != h, src, dst, ss.at[p, h], sem, to)
                else:
                    go(src, dst, ss.at[p, h], sem, to)

    xb, rx = ref.xb, ref.rx
    deal(x_in, xb, lambda h: frames[h], ref.sx, rx)
    cb, rc = ref.cb, ref.rc
    deal(cot_in, cb, lambda h: frames[h] - h * FO, ref.sc, rc)

    half = 3 * HW // 2
    first_half = row_ds(lax.rem(d, 2) * half, half)
    other_half = row_ds((1 - lax.rem(d, 2)) * half, half)
    go_if(
        kap == t, wqkv.at[first_half], wqkv.at[first_half], ref.sq.at[0], rq.at[1],
        mirror,
    )

    share = 2 * lax.rem(d, 2) + kap
    other_dp = 2 * (1 - lax.rem(d, 2)) + kap
    other_core = 2 * lax.rem(d, 2) + 1 - kap
    other_both = 2 * (1 - lax.rem(d, 2)) + 1 - kap
    wide = ("w_out", "w_up", "w_down")
    full = {n: getattr(ref, n + "_full") for n in wide + ("bias",)}
    rw, sw, lw = ref.rw, ref.sw, ref.lw
    own_copies = {}
    for n, name in enumerate(wide + ("bias",)):
        own_copies[name] = pltpu.make_async_copy(getattr(ref, name), full[name].at[t], lw.at[n])
        own_copies[name].start()

    def weight_part(name, s, which):
        quarter = getattr(ref, name).shape[0] // 4
        return full[name].at[s, row_ds(which * quarter, quarter)]

    for n, name in enumerate(wide):
        quarter = getattr(ref, name).shape[0] // 4
        src = getattr(ref, name).at[row_ds(share * quarter, quarter)]
        go(src, weight_part(name, t, share), sw.at[n, 0], rw.at[n, 0], mirror)
    go(ref.bias, full["bias"].at[t], sw.at[3, 0], rw.at[3, 0], mirror)

    def weights_second(name):
        n = wide.index(name)
        part = weight_part(name, 1 - t, share)
        arrived(part, rw.at[n, 0])
        go(part, part, sw.at[n, 1], rw.at[n, 1], beside)
        go(part, part, sw.at[n, 2], rw.at[n, 2], mate)

    def weights_third(name):
        n = wide.index(name)
        part = weight_part(name, 1 - t, other_dp)
        arrived(part, rw.at[n, 1])
        go(part, part, sw.at[n, 3], rw.at[n, 3], mate)

    def weights_ready(name):
        n = wide.index(name)
        arrived(weight_part(name, 1 - t, other_core), rw.at[n, 2])
        arrived(weight_part(name, 1 - t, other_both), rw.at[n, 3])

    RB = min(256, R)
    nb, qb_, kb_, vb_ = ref.nb, ref.q, ref.k, ref.v
    vec = (ref.gain_attn, ref.shift_attn, ref.gain_mlp, ref.shift_mlp)

    def project(start):
        rows = row_ds(start, RB, 64)
        xhat, _ = norm_parts(xb[rows, :].astype(F32))
        normed = (xhat * vec[0][...] + vec[1][...]).astype(BF)
        nb[rows, :] = normed
        packed = dot(normed, wqkv[...], NT)
        for g in range(G):
            lo = g * GW
            qb_[g, rows, :] = (packed[:, lo : lo + GW].astype(BF).astype(F32) * scale).astype(BF)
            kb_[g, rows, :] = packed[:, HW + lo : HW + lo + GW].astype(BF)
            vb_[g, rows, :] = packed[:, 2 * HW + lo : 2 * HW + lo + GW].astype(BF)

    @pl.when(kap != t)
    def _():
        arrived(wqkv.at[first_half], rq.at[1])

    go_if(
        kap != t, wqkv.at[first_half], wqkv.at[first_half], ref.sq.at[1], rq.at[2], beside
    )
    weights_second("w_out")
    for p in range(Z):
        for core in (0, 1):
            j = 2 * lax.rem(z + p, Z) + core
            f = j * (1 - kap) + (2 * N - 1 - j) * kap
            part = xb.at[row_ds(f * tok, tok)]
            arrived(part, rx.at[f])
            go(part, part, ref.fx.at[p, core], rx.at[f], mate)

    @pl.when(kap != t)
    def _():
        arrived(wqkv.at[other_half], rq.at[2])

    for k in range(R // RB):
        project(kap * R + k * RB)
    for k in range(FO):
        f = (1 - kap) * FO + k
        arrived(xb.at[row_ds(f * tok, tok)], rx.at[f])
    for k in range(R // RB):
        project((1 - kap) * R + k * RB)

    live = ref.live[clip]
    probs, mo, mr = ref.probs, ref.mo, ref.mr
    rm, sm = ref.rm, ref.sm
    NQ = L // QB
    lane = lax.broadcasted_iota(jnp.int32, (QB, GW), 1) // head_dim

    def pick(parts):
        out = parts[0]
        for a in range(1, HG):
            out = jnp.where(lane == a, parts[a], out)
        return out

    def only(values, a):
        if HG == 1:
            return values
        return jnp.where(lane == a, values, jnp.zeros_like(values))

    def hand_over(qb, g):
        row = qb * QB
        s = row // R
        off = row - s * R
        lanes = pl.ds(g * GW, GW)
        src = mo.at[pl.ds(row, QB), lanes]
        dst = mr.at[kap, pl.ds(off, QB), lanes]

        @pl.when(kap == s)
        def _():
            mr[kap, pl.ds(off, QB), lanes] = mo[pl.ds(row, QB), lanes]

        go_if(kap != s, src, dst, sm.at[qb, g], rm.at[off // QB, g], mate)

    def mask_shift(qb):
        K = (qb + 1) * QB
        row_frame = (qb * QB + lax.broadcasted_iota(jnp.int32, (QB, K), 0)) // PATCH
        col_frame = lax.broadcasted_iota(jnp.int32, (QB, K), 1) // PATCH
        allowed = (col_frame <= row_frame) & (col_frame < live)
        return jnp.where(allowed, 0.0, -1e30)

    def attend_block(qb, g, shift):
        K = (qb + 1) * QB
        rows = pl.ds(qb * QB, QB)
        qv = qb_[g, rows, :]
        kv = kb_[g, pl.ds(0, K), :]
        vv = vb_[g, pl.ds(0, K), :]
        outs = []
        for a in range(HG):
            scores = dot(only(qv, a), kv, NT) + shift
            top = jnp.max(scores, axis=-1, keepdims=True)
            weights = jnp.exp(scores - top)
            total = jnp.sum(weights, axis=-1, keepdims=True)
            prob = (weights * (1.0 / total)).astype(BF)
            probs[g * HG + a, rows, pl.ds(0, K)] = prob
            outs.append(dot(prob, vv))
        mo[rows, pl.ds(g * GW, GW)] = pick(outs).astype(BF)

    pumps = {
        (0, 0): functools.partial(weights_second, "w_up"),
        (1, 1): functools.partial(weights_second, "w_down"),
        (2, 0): functools.partial(weights_third, "w_out"),
    }
    for qb in range(NQ):
        shift = mask_shift(qb)
        for g in range(G):
            attend_block(qb, g, shift)
            hand_over(qb, g)
            if (qb, g) in pumps:
                pumps[qb, g]()

    wof, wuf, wdf, bf_ = full["w_out"], full["w_up"], full["w_down"], full["bias"]
    second, act, gpre = ref.second, ref.act, ref.gpre
    mlow, gmid, gst, gx = ref.mlow, ref.gmid, ref.gst, ref.gx
    ob, out_ref, ig_ref = ref.ob, ref.out, ref.ig
    mid, bsum, sv = ref.mid, ref.bsum, ref.sv
    mlp_sum, sec_sum = ref.mlp_sum, ref.sec_sum
    RC = min(256, R)
    FT = min(512, FFh)
    c0 = 0.7978845608028654

    def middle_rows(c):
        rows = pl.ds(c * RC, RC)
        attn = dot(mr[0, rows, :], wof[0])
        for s in range(1, T):
            attn = attn + dot(mr[s, rows, :], wof[s])
        middle = xb[row_ds(kap * R + c * RC, RC, 64), :].astype(F32) + attn
        mid[rows, :] = middle
        xhat, _ = norm_parts(middle)
        second[rows, :] = (xhat * vec[2][...] + vec[3][...]).astype(BF)

    def feed_forward(s, c, first):
        rows = pl.ds(c * RC, RC)
        sec = second[rows, :]
        cot = cb[rows, :]
        for j in range(FFh // FT):
            cols = pl.ds(j * FT, FT)
            pre = dot(sec, wuf[s, :, cols]) + bf_[s, 0:1, cols]
            gact = dot(cot, wdf[s, cols, :], NT)
            sq = pre * pre
            th = jnp.tanh(c0 * pre * (1.0 + 0.044715 * sq))
            half = 0.5 * (1.0 + th)
            a = (pre * half).astype(BF)
            slope = half + 0.5 * pre * (1.0 - th * th) * (c0 * (1.0 + 0.134145 * sq))
            gp = (gact * slope).astype(BF)
            act[s, rows, cols] = a
            gpre[s, rows, cols] = gp
            sums = jnp.sum(gp.astype(F32), axis=0, keepdims=True)
            bsum[s, 0:1, cols] = sums if c == 0 else bsum[s, 0:1, cols] + sums
            up = dot(a, wdf[s, cols, :])
            back = dot(gp, wuf[s, :, cols], NT)
            if first and j == 0:
                mlp_sum[rows, :] = up
                sec_sum[rows, :] = back
            else:
                mlp_sum[rows, :] = mlp_sum[rows, :] + up
                sec_sum[rows, :] = sec_sum[rows, :] + back

    def finish_rows(c):
        rows = pl.ds(c * RC, RC)
        middle = mid[rows, :]
        xhat, rstd = norm_parts(middle)
        ob[rows, :] = (middle + mlp_sum[rows, :]).astype(BF)
        gsec = sec_sum[rows, :]
        gain_sum = jnp.sum(gsec * xhat, axis=0, keepdims=True)
        shift_sum = jnp.sum(gsec, axis=0, keepdims=True)
        if c > 0:
            gain_sum = gain_sum + sv[0, 2:3, 0:D]
            shift_sum = shift_sum + sv[0, 3:4, 0:D]
        sv[0, 2:3, 0:D] = gain_sum
        sv[0, 3:4, 0:D] = shift_sum
        gm = cb[rows, :].astype(F32) + norm_back(gsec, vec[2][...], xhat, rstd)
        gmid[rows, :] = gm
        low = gm.astype(BF)
        mlow[rows, :] = low
        for s in range(T):
            gst[s, rows, :] = dot(low, wof[s], NT).astype(BF)

    def give_back(buf, dst_ref, ss, rs, k):
        f = kap * FO + k
        j = f * (1 - kap) + (2 * N - 1 - f) * kap
        src = buf.at[pl.ds(k * tok, tok)]
        dst, sem = dst_ref.at[clip, kap], rs.at[clip, kap]

        @pl.when(j == i)
        def _():
            pltpu.make_async_copy(src, dst, sem).start()

        go_if(j != i, src, dst, ss.at[k], sem, {"ctx": j})

    def pass_on(dst_ref, fs, rs, p):
        for h in (0, 1):
            cc = 2 * lax.rem(z + p, Z) + t
            part = dst_ref.at[cc, h]
            arrived(part, rs.at[cc, h])
            go(part, part, fs.at[p, h], rs.at[cc, h], mirror)

    def take_rest(dst_ref, rs):
        for p in range(Z):
            for h in (0, 1):
                cc = 2 * p + 1 - t
                arrived(dst_ref.at[cc, h], rs.at[cc, h])

    down_fin, up_fin = ref.down_fin, ref.up_fin
    fins = {
        "down0": down_fin.at[pl.ds(0, FFh // 2)],
        "down1": down_fin.at[pl.ds(FFh // 2, FFh // 2)],
        "up0": up_fin.at[pl.ds(0, D // 2)],
        "up1": up_fin.at[pl.ds(D // 2, D // 2)],
        "out": ref.out_fin,
        "qkv0": ref.qkv_fin.at[0],
        "qkv1": ref.qkv_fin.at[1],
    }
    reduces = {}
    for name, levels in cfg.plans.items():
        bufs = [getattr(ref, name + "_buf" + str(n), None) for n in range(len(levels))]
        reduces[name] = Reduce(
            levels, getattr(ref, name + "_acc"), fins[name], bufs, getattr(ref, name + "_ss"),
            getattr(ref, name + "_rs"), place,
        )

    def grad_wide(name, s):
        k = int(name[-1])
        if name[0] == "d":
            cols = pl.ds(k * (FFh // 2), FFh // 2)
            getattr(ref, name + "_acc")[s] = dot(act[s, :, cols], cb[...], TN).astype(BF)
        else:
            cols = pl.ds(k * (D // 2), D // 2)
            getattr(ref, name + "_acc")[s] = dot(second[:, cols], gpre[s], TN).astype(BF)

    rsv = ref.rsv
    everyone = [("ctx", b) for b in bits_of(N)] + [("dp", b) for b in bits_of(DP)]
    everyone += [("tensor", b) for b in bits_of(T)]
    vec_copy = []

    def vec_step():
        n = len(vec_copy)
        if n > 0:
            vec_copy[-1].wait()
            sv[n] = sv[n - 1] + rsv[n - 1]
        if n < len(everyone):
            axis, bit = everyone[n]
            copy = remote(
                sv.at[n], rsv.at[n], ref.sv_ss.at[n], ref.sv_rs.at[n],
                {axis: flip(place[axis], bit)},
            )
            copy.start()
            vec_copy.append(copy)
        else:
            vec_copy.append(None)

    out_done, ig_done = [], []
    script = list(cfg.script)

    def run_script():
        while script:
            item = script.pop(0)
            if item == MARK:
                return
            if item == VECTORS:
                vec_step()
            elif item == OUTPUT:
                pass_on(out_ref, ref.fo, ref.ro, len(out_done))
                out_done.append(item)
            elif item == INPUT_GRAD:
                pass_on(ig_ref, ref.fi, ref.ri, len(ig_done))
                ig_done.append(item)
            else:
                reduces[CHUNKS[item]].tick()

    for name in wide + ("bias",):
        own_copies[name].wait()
    arrived(full["bias"].at[1 - t], rw.at[3, 0])
    weights_ready("w_out")
    for k in range(FO):
        arrived(cb.at[pl.ds(k * tok, tok)], rc.at[k])
    for c in range(R // RC):
        for g in range(G):
            rows, lanes = pl.ds(c * RC, RC), pl.ds(g * GW, GW)
            arrived(mr.at[1 - kap, rows, lanes], rm.at[c, g])
        middle_rows(c)
        feed_forward(t, c, True)
        if c == 0:
            weights_third("w_up")
    for name in cfg.order:
        grad_wide(name, t)
    weights_third("w_down")
    weights_ready("w_up")
    weights_ready("w_down")
    for c in range(R // RC):
        feed_forward(1 - t, c, False)
    sv[0, 4:5, 0:FFh] = bsum[0, 0:1, :]
    sv[0, 5:6, 0:FFh] = bsum[1, 0:1, :]
    sg, rg = ref.sg, ref.rg
    for c in range(R // RC):
        finish_rows(c)
        rows = pl.ds(c * RC, RC)
        home = row_ds(kap * R + c * RC, RC, 64)
        gx[home, :] = gst[kap, rows, :]
        go(gst.at[1 - kap, rows], gx.at[home], sg.at[c], rg.at[c], mate)
    for k in range(FO):
        give_back(ob, out_ref, ref.so, ref.ro, k)

    for name in cfg.order:
        grad_wide(name, 1 - t)
        reduces[name].tick()
    for s in range(T):
        ref.out_acc[s] = dot(mr[s], mlow[...], TN).astype(BF)
    reduces["out"].tick()
    for c in range(R // RC):
        arrived(gx.at[row_ds((1 - kap) * R + c * RC, RC, 64)], rg.at[c])

    dk, dv, gpb = ref.dk, ref.dv, ref.gpb

    def attend_back_block(g, qb):
        K = (qb + 1) * QB
        rows = pl.ds(qb * QB, QB)
        keys = pl.ds(0, K)
        lanes = pl.ds(g * GW, GW)
        grad = gx[rows, lanes]
        prod = grad.astype(F32) * mo[rows, lanes].astype(F32)
        qv = qb_[g, rows, :]
        kv = kb_[g, keys, :]
        vv = vb_[g, keys, :]
        outs = []
        dk_sum = dv_sum = None
        for a in range(HG):
            delta = jnp.sum(only(prod, a), axis=-1, keepdims=True)
            goa = only(grad, a)
            prob = probs[g * HG + a, rows, keys]
            gprob = dot(goa, vv, NT)
            gs = (prob.astype(F32) * (gprob - delta)).astype(BF)
            outs.append(dot(gs, kv))
            dk_part = dot(gs, only(qv, a), TN)
            dv_part = dot(prob, goa, TN)
            dk_sum = dk_part if dk_sum is None else dk_sum + dk_part
            dv_sum = dv_part if dv_sum is None else dv_sum + dv_part
        gpb[rows, lanes] = (pick(outs) * scale).astype(BF)
        if qb == NQ - 1:
            dk[keys, :] = dk_sum
            dv[keys, :] = dv_sum
        else:
            dk[keys, :] = dk[keys, :] + dk_sum
            dv[keys, :] = dv[keys, :] + dv_sum

    run_script()
    for g in range(G):
        for qb in reversed(range(NQ)):
            attend_back_block(g, qb)
            if qb == 0:
                gpb[:, pl.ds(HW + g * GW, GW)] = dk[...].astype(BF)
                gpb[:, pl.ds(2 * HW + g * GW, GW)] = dv[...].astype(BF)
                for b in range(3):
                    getattr(ref, "qkv" + str(g) + "_acc")[kap, pl.ds(b * GW, GW), :] = dot(
                        gpb[:, pl.ds(b * HW + g * GW, GW)], nb[...], TN
                    ).astype(BF)
                reduces["qkv" + str(g)].tick()
            run_script()

    gns, gnr = ref.gns, ref.gnr
    gns[...] = dot(gpb[row_ds((1 - kap) * R, R, 64), :], wqkv[...]).astype(BF)
    go(gns, gnr, ref.sn.at[0], ref.rn.at[0], mate)
    run_script()
    own = dot(gpb[row_ds(kap * R, R, 64), :], wqkv[...])
    arrived(gnr, ref.rn.at[0])
    own = own + gnr[...].astype(F32)
    xhat, rstd = norm_parts(xb[row_ds(kap * R, R, 64), :].astype(F32))
    sv[0, 0:1, 0:D] = jnp.sum(own * xhat, axis=0, keepdims=True)
    sv[0, 1:2, 0:D] = jnp.sum(own, axis=0, keepdims=True)
    igb = ref.igb
    igb[...] = (gmid[...] + norm_back(own, vec[0][...], xhat, rstd)).astype(BF)
    for k in range(FO):
        give_back(igb, ig_ref, ref.si, ref.ri, k)
    vec_step()
    run_script()
    last = sv[len(everyone)]
    part = D // T
    gains = last[0:4, 0:part]
    bias = last[4:5, 0:FFh]
    for s in range(1, T):
        gains = jnp.where(t == s, last[0:4, s * part : (s + 1) * part], gains)
        bias = jnp.where(t == s, last[4 + s : 5 + s, 0:FFh], bias)
    for n, got in enumerate((ref.grad_ga, ref.grad_sa, ref.grad_gm, ref.grad_sm)):
        got[...] = gains[n : n + 1, :]
    ref.bias_out[...] = bias

    take_rest(out_ref, ref.ro)
    take_rest(ig_ref, ref.ri)
    for done in sends:
        done()


def finish_kernel(sizes, *refs):
    D, HW, FFh, GW, G, head_dim = sizes
    ins, outs, scratch = refs[:11], refs[11:22], refs[22:]
    out, ig, ga, sa, qkv, wo, gm, sm, up, bias, down = ins
    b_out, b_ig, b_qkv, b_wo, b_up, b_down, f_qkv, f_wo, f_up, f_down, sem = scratch
    moves = []

    def move(n, src, dst):
        copy = pltpu.make_async_copy(src, dst, sem.at[n])
        copy.start()
        moves.append(copy)
        return copy

    half = down.shape[0] // 2
    reads = [
        move(0, down.at[pl.ds(0, half)], b_down.at[pl.ds(0, half)]),
        move(1, down.at[pl.ds(half, half)], b_down.at[pl.ds(half, half)]),
        move(2, up.at[pl.ds(0, D // 2)], b_up.at[pl.ds(0, D // 2)]),
        move(3, up.at[pl.ds(D // 2, D // 2)], b_up.at[pl.ds(D // 2, D // 2)]),
        move(4, wo, b_wo),
        move(5, qkv, b_qkv),
        move(11, out, b_out),
        move(12, ig, b_ig),
    ]
    parts = (
        (b_down, f_down, outs[10], 0, half),
        (b_down, f_down, outs[10], half, half),
        (b_up, f_up, outs[8], 0, D // 2),
        (b_up, f_up, outs[8], D // 2, D // 2),
        (b_wo, f_wo, outs[5], 0, HW),
    )
    for n, (src, mid, dst, off, rows) in enumerate(parts):
        reads[n].wait()
        at = pl.ds(off, rows)
        mid[at, :] = src[at, :].astype(F32)
        move(6 + n, mid.at[at], dst.at[at])
    for n, (src, dst) in enumerate(((ga, 2), (sa, 3), (gm, 6), (sm, 7), (bias, 9))):
        outs[dst][...] = src[...]
    reads[6].wait()
    move(14, b_out, outs[0])
    reads[7].wait()
    move(15, b_ig, outs[1])
    reads[5].wait()
    for g in range(G):
        for a in range(GW // head_dim):
            for b in range(3):
                f_qkv[g * (GW // head_dim) + a, pl.ds(b * head_dim, head_dim), :] = b_qkv[
                    g, pl.ds(b * GW + a * head_dim, head_dim), :
                ].astype(F32)
    move(13, f_qkv, outs[4])
    for copy in moves[len(reads) :]:
        copy.wait()


def finish(got, layout, qkv_shape, sizes, T):
    D, HW, FFh, GW, G, head_dim = sizes
    vm = pl.BlockSpec(memory_space=pltpu.VMEM)
    hbm = pl.BlockSpec(memory_space=pl.ANY)
    S, V = jax.ShapeDtypeStruct, pltpu.VMEM
    small = S((1, D // T), F32)
    by_head = (qkv_shape[1], qkv_shape[2], qkv_shape[0])
    results = pl.pallas_call(
        functools.partial(finish_kernel, sizes),
        out_shape=[
            S(got.out.shape, BF), S(got.ig.shape, BF), small, small, S(by_head, F32),
            S((HW, D), F32), small, small, S((D, FFh), F32), S((1, FFh), F32), S((FFh, D), F32),
        ],
        in_specs=[hbm, hbm, vm, vm, hbm, hbm, vm, vm, hbm, vm, hbm],
        out_specs=[hbm, hbm, vm, vm, hbm, hbm, vm, vm, hbm, vm, hbm],
        scratch_shapes=[
            V(got.out.shape, BF), V(got.ig.shape, BF), V((G, 3 * GW, D), BF), V((HW, D), BF), V((D, FFh), BF), V((FFh, D), BF),
            V(by_head, F32), V((HW, D), F32), V((D, FFh), F32), V((FFh, D), F32),
            pltpu.SemaphoreType.DMA((16,)),
        ],
        compiler_params=pltpu.CompilerParams(vmem_limit_bytes=60 * 2**20),
    )(
        got.out, got.ig, got.grad_ga, got.grad_sa, got.qkv_fin, got.out_fin, got.grad_gm,
        got.grad_sm, got.up_fin, got.bias_out, got.down_fin,
    )
    out, ig, ga, sa, qkv, wo, gm, sm, up, bias, down = results
    return (
        out.reshape(layout), ig.reshape(layout), ga[0], sa[0], qkv.transpose(2, 0, 1), wo, gm[0], sm[0], up, bias[0],
        down,
    )


def body(
    sizes,
    inputs,
    cotangent,
    live_frames,
    gain_attn,
    shift_attn,
    w_qkv,
    w_out,
    gain_mlp,
    shift_mlp,
    w_up,
    up_bias,
    w_down,
):
    N, T, DP = sizes["ctx"], sizes["tensor"], sizes["dp"]
    C, _, _, tok, D = inputs.shape
    heads, head_dim = w_qkv.shape[1], w_qkv.shape[2] // 3
    HW = heads * head_dim
    GW = min(128, HW)
    FFh = w_up.shape[1]
    L = 2 * N * tok
    by_chip = T == 2 and HW == 256 and N >= 8 and N % 2 == 0 and C == N and DP == 2 and L % 512 == 0
    S_ = 2 if by_chip else T
    R = L // S_
    cfg = SimpleNamespace(
        N=N, T=T, DP=DP, L=L, R=R, FO=2 * N // S_, tok=tok, D=D, HW=HW, GW=GW, G=HW // GW,
        FFh=FFh, QB=256, head_dim=head_dim,
    )
    G = cfg.G
    core, rest = [("ctx", 1)], [("ctx", b) for b in bits_of(N)[1:]]
    over_dp = [("dp", b) for b in bits_of(DP)]
    over_t = [("tensor", b) for b in reversed(bits_of(T))]
    if by_chip:
        steps = {
            "x": over_dp, "y": over_t, "z": rest[:1], "Z": rest[1:-1] + [rest[-1] + ("f",)],
            "R": rest[1:], "X": [over_dp[-1] + ("f",)],
        }
        cfg.plans = plans = {}
        cfg.script, cfg.order = SCRIPT, ORDER
        leads, widths = {}, {}
        for name, order in ORDERS.items():
            begin = [("ctx", 1, "p")] if name[0] == "q" else core
            if name[0] == "d":
                leads[name], widths[name] = (T, FFh // 2), D
            elif name[0] == "u":
                leads[name], widths[name] = (T, D // 2), FFh
            elif name[0] == "o":
                leads[name], widths[name] = (T, HW), D
            else:
                leads[name], widths[name] = (T, 3 * GW), D
            plans[name] = plan_levels(*leads[name], begin + sum((steps[c] for c in order), []))
    else:
        cfg.plans = plans = {
            "down": plan_levels(T, FFh, core + over_dp + over_t + rest),
            "up": plan_levels(T, D, core + over_t + over_dp + rest),
            "out": plan_levels(T, HW, core + over_t + over_dp + rest),
            "qkv": plan_levels(1, D, core + over_dp + rest),
        }
        leads = {"down": (T, FFh), "up": (T, D), "out": (T, HW), "qkv": (1, D)}
        widths = {"down": D, "up": FFh, "out": D, "qkv": 3 * HW}

    x = inputs.reshape(C, 2, tok, D)
    cot = cotangent.reshape(C, 2, tok, D)
    wq = w_qkv.transpose(1, 2, 0)
    if not by_chip:
        wq = w_qkv.reshape(D, heads, 3, head_dim).transpose(0, 2, 1, 3).reshape(D, 3 * HW)

    vm = pl.BlockSpec(memory_space=pltpu.VMEM)
    hbm = pl.BlockSpec(memory_space=pl.ANY)
    ins = dict(
        x=(x, hbm),
        cot=(cot, hbm),
        live=(live_frames, pl.BlockSpec(memory_space=pltpu.SMEM)),
        gain_attn=(gain_attn.reshape(1, D), vm),
        shift_attn=(shift_attn.reshape(1, D), vm),
        gain_mlp=(gain_mlp.reshape(1, D), vm),
        shift_mlp=(shift_mlp.reshape(1, D), vm),
        w_qkv=(wq, hbm if by_chip else vm),
        w_out=(w_out, hbm),
        w_up=(w_up, hbm),
        w_down=(w_down, hbm),
        bias=(up_bias.reshape(1, FFh), vm),
    )
    S = jax.ShapeDtypeStruct
    outs = dict(
        out=S((C, 2, tok, D), BF),
        ig=S((C, 2, tok, D), BF),
        down_fin=S((FFh, D), BF),
        up_fin=S((D, FFh), BF),
        out_fin=S((HW, D), BF),
        qkv_fin=S((G, 3 * GW, D) if by_chip else (D, 3 * HW), BF),
        grad_ga=S((1, D // T), F32),
        grad_sa=S((1, D // T), F32),
        grad_gm=S((1, D // T), F32),
        grad_sm=S((1, D // T), F32),
        bias_out=S((1, FFh), F32),
    )
    W = max(D, FFh)
    SR = -(-(4 + T) // 8) * 8
    n_all = len(bits_of(N)) + len(bits_of(DP)) + len(bits_of(T))
    RC = min(256, R)
    piece = min(cfg.QB, R)
    FO = cfg.FO
    dma = pltpu.SemaphoreType.DMA
    V = pltpu.VMEM
    scratch = dict(
        xb=V((L, D), BF), rx=dma((2 * N,)),
        cb=V((R, D), BF), rc=dma((FO,)),
        w_out_full=V((T, HW, D), BF), w_up_full=V((T, D, FFh), BF),
        w_down_full=V((T, FFh, D), BF), bias_full=V((T, 1, FFh), F32), lw=dma((4,)),
        nb=V((L, D), BF), q=V((G, L, GW), BF), k=V((G, L, GW), BF), v=V((G, L, GW), BF),
        probs=V((heads, L, L), BF), mo=V((L, HW), BF), mr=V((S_, R, HW), BF),
        second=V((R, D), BF), act=V((T, R, FFh), BF), gpre=V((T, R, FFh), BF),
        mlow=V((R, D), BF), gmid=V((R, D), F32), gst=V((T, R, HW), BF), gx=V((L, HW), BF),
        ob=V((R, D), BF), so=dma((FO,)), ro=dma((N, 2)),
        igb=V((R, D), BF), si=dma((FO,)), ri=dma((N, 2)),
        sv=V((n_all + 1, SR, W), F32), rsv=V((n_all, SR, W), F32),
        sv_ss=dma((n_all,)), sv_rs=dma((n_all,)),
        dk=V((L, GW), F32), dv=V((L, GW), F32), gpb=V((L, 3 * HW), BF),
    )
    if by_chip:
        scratch.update(
            sx=dma((N // 2, 2)), fx=dma((N // 2, 2)), sc=dma((N // 2, 2)),
            wq=V((3 * HW, D), BF), rq=dma((3,)), bq=dma((3 * heads,)), sq=dma((2,)),
            rw=dma((4, 4)), sw=dma((4, 4)), rm=dma((R // 256, G)), sm=dma((L // 256, G)),
            mid=V((R, D), F32), bsum=V((T, 8, FFh), F32),
            mlp_sum=V((R, D), F32), sec_sum=V((R, D), F32),
            sg=dma((R // RC,)), rg=dma((R // RC,)),
            fo=dma((N // 2, 2)), fi=dma((N // 2, 2)),
            gns=V((R, D), BF), gnr=V((R, D), BF), sn=dma((1,)), rn=dma((1,)),
        )
    else:
        scratch.update(
            sx=dma((N, 2)), fx=dma((T, FO)), sc=dma((N, 2)), rw=dma((4, 4, T)), sw=dma((4, 4, T)),
            rm=dma((T, R // piece, G)), sm=dma((L // piece, G)),
            sg=dma((T, R // RC)), rg=dma((T, R // RC)), fo=dma((T, N, 2)), fi=dma((T, N, 2)),
            mlp_sum=V((RC, D), F32), sec_sum=V((RC, D), F32),
            gns=V((max(T - 1, 1), R, D), BF), gnr=V((max(T - 1, 1), R, D), BF),
            sn=dma((T,)), rn=dma((T,)),
        )
    for name, levels in plans.items():
        scratch[name + "_acc"] = V(leads[name] + (widths[name],), BF)
        scratch[name + "_ss"] = dma((2 * len(levels),))
        scratch[name + "_rs"] = dma((2 * len(levels),))
        for n, (_, _, kind, lead, rows) in enumerate(levels):
            if kind == "p":
                continue
            scratch[name + "_buf" + str(n)] = V((lead, rows, widths[name]), BF)
    names = list(ins) + list(outs) + list(scratch)
    results = pl.pallas_call(
        functools.partial(chip_kernel if by_chip else spread_kernel, cfg, names),
        out_shape=list(outs.values()),
        in_specs=[s for _, s in ins.values()],
        out_specs=[vm] * len(outs),
        scratch_shapes=list(scratch.values()),
        compiler_params=pltpu.CompilerParams(
            collective_id=0, has_side_effects=True, vmem_limit_bytes=60 * 2**20
        ),
    )(*[a for a, _ in ins.values()])
    got = SimpleNamespace(**dict(zip(outs, results)))
    if by_chip:
        return finish(got, inputs.shape, w_qkv.shape, (D, HW, FFh, GW, G, head_dim), T)
    grad_qkv = got.qkv_fin.reshape(D, 3, heads, head_dim).transpose(0, 2, 1, 3)
    return (
        got.out.reshape(inputs.shape),
        got.ig.reshape(inputs.shape),
        got.grad_ga[0],
        got.grad_sa[0],
        grad_qkv.reshape(w_qkv.shape).astype(F32),
        got.out_fin.astype(F32),
        got.grad_gm[0],
        got.grad_sm[0],
        got.up_fin.astype(F32),
        got.bias_out[0],
        got.down_fin.astype(F32),
    )


def solution(mesh):
    return jax.shard_map(
        functools.partial(body, dict(mesh.shape)),
        mesh=mesh,
        in_specs=(
            P("dp", None, "ctx", None, None),
            P("dp", None, "ctx", None, None),
            P("dp"),
            P(),
            P(),
            P(None, "tensor", None),
            P("tensor", None),
            P(),
            P(),
            P(None, "tensor"),
            P("tensor"),
            P("tensor", None),
        ),
        out_specs=(
            P("dp", None, "ctx", None, None),
            P("dp", None, "ctx", None, None),
            P("tensor"),
            P("tensor"),
            P(None, "tensor", None),
            P("tensor", None),
            P("tensor"),
            P("tensor"),
            P(None, "tensor"),
            P("tensor"),
            P("tensor", None),
        ),
        check_vma=False,
    )
```

```python
import functools
from types import SimpleNamespace

import jax
import jax.numpy as jnp
from jax import lax
from jax.experimental import pallas as pl
from jax.experimental.pallas import tpu as pltpu
from jax.sharding import PartitionSpec as P

PATCH = 64
EPSILON = 1e-05
MESH = pl.DeviceIdType.MESH
BF = jnp.bfloat16
F32 = jnp.float32

NN = (((1,), (0,)), ((), ()))
NT = (((1,), (1,)), ((), ()))
TN = (((0,), (0,)), ((), ()))


def dot(a, b, dims=NN):
    return lax.dot_general(a, b, dims, preferred_element_type=F32)


def bits_of(size):
    found, bit = [], 1
    while bit < size:
        found.append(bit)
        bit *= 2
    return found


def flip(index, bit):
    return index + bit - 2 * bit * ((index // bit) % 2)


def bit_of(index, bit):
    return (index // bit) % 2


def row_ds(start, size, unit=16):
    return pl.ds(pl.multiple_of(start, unit), size)


def remote(src, dst, send_sem, recv_sem, where):
    return pltpu.make_async_remote_copy(
        src_ref=src,
        dst_ref=dst,
        send_sem=send_sem,
        recv_sem=recv_sem,
        device_id=where,
        device_id_type=MESH,
    )


def arrived(dst, sem):
    pltpu.make_async_copy(dst, dst, sem).wait()


def norm_parts(values):
    mean = jnp.mean(values, axis=-1, keepdims=True)
    centered = values - mean
    var = jnp.mean(centered * centered, axis=-1, keepdims=True)
    rstd = lax.rsqrt(var + EPSILON)
    return centered * rstd, rstd


def norm_back(grad, gain, xhat, rstd):
    scaled = grad * gain
    first = jnp.mean(scaled, axis=-1, keepdims=True)
    second = jnp.mean(scaled * xhat, axis=-1, keepdims=True)
    return rstd * (scaled - first - xhat * second)


def plan_levels(lead, rows, order):
    levels = []
    for axis, bit, *forced in order:
        if forced:
            kind = forced[0]
            rows = rows // 2 if kind == "p" else rows
        elif axis == "tensor":
            lead //= 2
            kind = "t"
        elif rows % 32 == 0:
            rows //= 2
            kind = "r"
        else:
            kind = "f"
        levels.append((axis, bit, kind, lead, rows))
    return levels


ORDERS = {
    "down0": "zxyZ",
    "down1": "yxzZ",
    "up0": "yzxZ",
    "up1": "xyzZ",
    "out": "yxzZ",
    "qkv0": "yxzZ",
    "qkv1": "yxzZ",
}
CHUNKS = tuple(ORDERS)
VECTORS, OUTPUT, INPUT_GRAD, MARK = range(7, 11)
ORDER = tuple(CHUNKS[n] for n in (0, 2, 1, 3))
SCRIPT = (
    10, 0, 10, 2, 3, 1, 10, 10, 10, 10, 10, 10, 10, 10, 10, 2, 5, 6, 10, 1, 3, 5, 4, 1, 2, 9, 6,
    5, 2, 0, 9, 3, 5, 7, 1, 4, 6, 3, 0, 4, 5, 0, 9, 9, 2, 1, 4, 6, 8, 5, 3, 8, 1, 7, 0, 4, 2, 8,
    5, 3, 6, 4, 1, 8, 7, 0, 6, 7, 5, 2, 4, 1, 3, 0, 6, 4, 3, 2, 0, 7, 6,
)


class Reduce:
    def __init__(self, levels, acc, fin, bufs, ss, rs, place):
        self.levels, self.acc, self.fin = levels, acc, fin
        self.bufs, self.ss, self.rs, self.place = bufs, ss, rs, place
        self.lead, self.rows = acc.shape[0], acc.shape[1]
        self.toff, self.roff = 0, 0
        self.marks = []
        self.copy = self.result = None
        self.steps = []
        count = len(levels)
        for n in range(count):
            self.steps.append(functools.partial(self.step, n))
        self.steps.append(self.turn)

    def send(self, n):
        axis, bit, kind, lead, rows = self.levels[n]
        mine = bit_of(self.place[axis], bit)
        self.marks.append((self.toff, self.roff, self.lead, self.rows))
        toff, roff = self.toff, self.roff
        dst = self.bufs[n]
        if kind == "p":
            toff = mine
            roff = self.roff + (1 - mine) * rows
            self.roff = self.roff + mine * rows
            dst = self.acc.at[pl.ds(toff, 1), row_ds(roff, rows)]
            self.copy = remote(
                dst, dst, self.ss.at[n], self.rs.at[n], {axis: flip(self.place[axis], bit)}
            )
            self.lead, self.rows = lead, rows
            self.copy.start()
            return
        if kind == "t":
            toff = self.toff + (1 - mine) * lead
            self.toff = self.toff + mine * lead
        elif kind == "r":
            roff = self.roff + (1 - mine) * rows
            self.roff = self.roff + mine * rows
        self.lead, self.rows = lead, rows
        self.copy = remote(
            self.acc.at[pl.ds(toff, lead), row_ds(roff, rows)],
            dst,
            self.ss.at[n],
            self.rs.at[n],
            {axis: flip(self.place[axis], bit)},
        )
        self.copy.start()

    def absorb(self, n):
        self.copy.wait()
        if self.levels[n][2] == "p":
            return
        buf = self.bufs[n]
        part = 32 if self.rows % 32 == 0 else 16
        for a in range(self.lead):

            def add(b, _):
                off = pl.multiple_of(b * part, 16)
                at = row_ds(self.roff + off, part)
                old = self.acc[self.toff + a, at, :].astype(F32)
                new = buf[a, pl.ds(off, part), :].astype(F32)
                self.acc[self.toff + a, at, :] = (old + new).astype(BF)
                return 0

            lax.fori_loop(0, self.rows // part, add, 0)

    def step(self, n):
        if n > 0:
            self.absorb(n - 1)
        self.send(n)

    def turn(self):
        count = len(self.levels)
        self.absorb(count - 1)
        at = row_ds(self.roff, self.rows)
        self.fin[at, :] = self.acc[self.toff, at, :]
        back = [n for n in reversed(range(count)) if self.levels[n][2] in "pr"]
        for k, n in enumerate(back):
            if k == 0:
                self.gather(n, True)
            else:
                self.steps.append(functools.partial(self.gather, n, False))
        self.steps.append(self.close)

    def gather(self, n, first):
        if not first:
            self.copy.wait()
        axis, bit, kind, lead, rows = self.levels[n]
        part = self.fin.at[row_ds(self.roff, rows)]
        count = len(self.levels)
        self.copy = remote(
            part,
            part,
            self.ss.at[count + n],
            self.rs.at[count + n],
            {axis: flip(self.place[axis], bit)},
        )
        self.copy.start()
        self.roff = self.marks[n][1]

    def close(self):
        self.copy.wait()
        if self.result is not None:
            self.result.start()

    def tick(self):
        if self.steps:
            self.steps.pop(0)()
            return True
        return False

    def drain(self):
        while self.tick():
            pass


def spread_kernel(cfg, names, *refs):
    ref = SimpleNamespace(**dict(zip(names, refs)))
    N, T, DP = cfg.N, cfg.T, cfg.DP
    L, R, FO, tok = cfg.L, cfg.R, cfg.FO, cfg.tok
    D, HW, GW, G, FFh, QB = cfg.D, cfg.HW, cfg.GW, cfg.G, cfg.FFh, cfg.QB
    head_dim = cfg.head_dim
    HG = GW // head_dim
    scale = head_dim ** (-0.5)
    d = lax.axis_index("dp")
    i = lax.axis_index("ctx")
    t = lax.axis_index("tensor")
    place = {"dp": d, "ctx": i, "tensor": t}
    x_in, cot_in = ref.x, ref.cot
    sends = []

    bar = pltpu.get_barrier_semaphore()
    peers = [{"ctx": lax.rem(i + p, N)} for p in range(1, N)]
    peers += [{"tensor": lax.rem(t + p, T)} for p in range(1, T)]
    peers += [{"dp": flip(d, b)} for b in bits_of(DP)]
    for peer in peers:
        pl.semaphore_signal(bar, inc=1, device_id=peer, device_id_type=MESH)
    pl.semaphore_wait(bar, len(peers))

    frames = (i, 2 * N - 1 - i)

    def owns(h):
        return frames[h] // FO == t

    xb, rx, sx, fx = ref.xb, ref.rx, ref.sx, ref.fx
    for p in range(N):
        c = lax.rem(i + p, N)
        for h in (0, 1):
            to = xb.at[row_ds(frames[h] * tok, tok)]

            @pl.when(owns(h))
            def _(p=p, c=c, h=h, to=to):
                if p == 0:
                    pltpu.make_async_copy(x_in.at[c, h], to, rx.at[frames[h]]).start()
                else:
                    remote(
                        x_in.at[c, h], to, sx.at[p, h], rx.at[frames[h]], {"ctx": c}
                    ).start()

            if p > 0:

                def done(p=p, c=c, h=h, to=to):
                    @pl.when(owns(h))
                    def _():
                        remote(
                            x_in.at[c, h], to, sx.at[p, h], rx.at[frames[h]], {"ctx": c}
                        ).wait_send()

                sends.append(done)

    def near(k):
        return t * FO + lax.rem(i + k, FO)

    for k in range(FO):
        f = near(k)
        part = xb.at[row_ds(f * tok, tok)]
        arrived(part, rx.at[f])
        for p in range(1, T):
            copy = remote(
                part, part, fx.at[p, k], rx.at[f], {"tensor": lax.rem(t + p, T)}
            )
            copy.start()
            sends.append(copy.wait_send)

    cb, rc, sc = ref.cb, ref.rc, ref.sc
    for p in range(N):
        c = lax.rem(i + p, N)
        for h in (0, 1):
            slot = lax.rem(frames[h], FO)
            to = cb.at[row_ds(slot * tok, tok)]

            @pl.when(owns(h))
            def _(p=p, c=c, h=h, to=to, slot=slot):
                if p == 0:
                    pltpu.make_async_copy(cot_in.at[c, h], to, rc.at[slot]).start()
                else:
                    remote(cot_in.at[c, h], to, sc.at[p, h], rc.at[slot], {"ctx": c}).start()

            if p > 0:

                def done(p=p, c=c, h=h, to=to, slot=slot):
                    @pl.when(owns(h))
                    def _():
                        remote(
                            cot_in.at[c, h], to, sc.at[p, h], rc.at[slot], {"ctx": c}
                        ).wait_send()

                sends.append(done)

    share = 2 * lax.rem(d, 2) + lax.rem(i, 2)
    wide = ("w_out", "w_up", "w_down")
    full = {n: getattr(ref, n + "_full") for n in wide + ("bias",)}
    rw, sw, lw = ref.rw, ref.sw, ref.lw
    own_copies = []
    for n, name in enumerate(wide + ("bias",)):
        copy = pltpu.make_async_copy(getattr(ref, name), full[name].at[t], lw.at[n])
        copy.start()
        own_copies.append(copy)
    for p in range(1, T):
        to = {"tensor": lax.rem(t + p, T)}
        copy = remote(ref.bias, full["bias"].at[t], sw.at[3, 0, p], rw.at[3, 0, t], to)
        copy.start()
        sends.append(copy.wait_send)
    for n, name in enumerate(wide):
        quarter = getattr(ref, name).shape[0] // 4
        at = row_ds(share * quarter, quarter)
        for p in range(1, T):
            to = {"tensor": lax.rem(t + p, T)}
            copy = remote(
                getattr(ref, name).at[at], full[name].at[t, at], sw.at[n, 0, p], rw.at[n, 0, t], to
            )
            copy.start()
            sends.append(copy.wait_send)

    other_dp = 2 * (1 - lax.rem(d, 2)) + lax.rem(i, 2)
    other_core = 2 * lax.rem(d, 2) + 1 - lax.rem(i, 2)
    other_both = 2 * (1 - lax.rem(d, 2)) + 1 - lax.rem(i, 2)

    def weight_part(name, s, which):
        quarter = getattr(ref, name).shape[0] // 4
        return full[name].at[s, row_ds(which * quarter, quarter)]

    def weights_second(n, name):
        for p in range(1, T):
            s = lax.rem(t + p, T)
            part = weight_part(name, s, share)
            arrived(part, rw.at[n, 0, s])
            for stage, to in ((1, {"dp": flip(d, 1)}), (2, {"ctx": flip(i, 1)})):
                copy = remote(part, part, sw.at[n, stage, p], rw.at[n, stage, s], to)
                copy.start()
                sends.append(copy.wait_send)

    def weights_third(n, name):
        for p in range(1, T):
            s = lax.rem(t + p, T)
            part = weight_part(name, s, other_dp)
            arrived(part, rw.at[n, 1, s])
            copy = remote(
                part, part, sw.at[n, 3, p], rw.at[n, 3, s], {"ctx": flip(i, 1)}
            )
            copy.start()
            sends.append(copy.wait_send)

    def weights_ready(n, name):
        own_copies[n].wait()
        for p in range(1, T):
            s = lax.rem(t + p, T)
            if name == "bias":
                arrived(full[name].at[s], rw.at[n, 0, s])
            else:
                arrived(weight_part(name, s, other_core), rw.at[n, 2, s])
                arrived(weight_part(name, s, other_both), rw.at[n, 3, s])

    RB = min(256, R)
    nb, qb_, kb_, vb_ = ref.nb, ref.q, ref.k, ref.v
    vec = (ref.gain_attn, ref.shift_attn, ref.gain_mlp, ref.shift_mlp)
    wqkv = ref.w_qkv

    def project(start):
        rows = row_ds(start, RB, 64)
        xhat, _ = norm_parts(xb[rows, :].astype(F32))
        normed = (xhat * vec[0][...] + vec[1][...]).astype(BF)
        nb[rows, :] = normed
        packed = dot(normed, wqkv[...])
        for g in range(G):
            lo = g * GW
            qb_[g, rows, :] = (packed[:, lo : lo + GW].astype(BF).astype(F32) * scale).astype(BF)
            kb_[g, rows, :] = packed[:, HW + lo : HW + lo + GW].astype(BF)
            vb_[g, rows, :] = packed[:, 2 * HW + lo : 2 * HW + lo + GW].astype(BF)

    for k in range(R // RB):
        project(t * R + k * RB)
    for p in range(1, T):
        s = lax.rem(t + p, T)
        for k in range(FO):
            f = s * FO + k
            arrived(xb.at[row_ds(f * tok, tok)], rx.at[f])
        for k in range(R // RB):
            project(s * R + k * RB)

    for n, name in enumerate(wide):
        weights_second(n, name)

    live = ref.live[i]
    probs, mo, mr = ref.probs, ref.mo, ref.mr
    rm, sm = ref.rm, ref.sm
    piece = min(QB, R)
    NQ = L // QB
    lane = lax.broadcasted_iota(jnp.int32, (QB, GW), 1) // head_dim

    def pick(parts):
        out = parts[0]
        for a in range(1, HG):
            out = jnp.where(lane == a, parts[a], out)
        return out

    def only(values, a):
        if HG == 1:
            return values
        return jnp.where(lane == a, values, jnp.zeros_like(values))

    def hand_over(qb, g):
        for b in range(QB // piece):
            row = qb * QB + b * piece
            s = row // R
            slot = (row - s * R) // piece
            src = mo.at[pl.ds(row, piece), pl.ds(g * GW, GW)]
            dst = mr.at[t, pl.ds(row - s * R, piece), pl.ds(g * GW, GW)]
            index = row // piece

            @pl.when(s == t)
            def _():
                mr[t, pl.ds(row - s * R, piece), pl.ds(g * GW, GW)] = mo[
                    pl.ds(row, piece), pl.ds(g * GW, GW)
                ]

            @pl.when(s != t)
            def _():
                remote(src, dst, sm.at[index, g], rm.at[t, slot, g], {"tensor": s}).start()

            def done(s=s, src=src, dst=dst, index=index, slot=slot):
                @pl.when(s != t)
                def _():
                    remote(
                        src, dst, sm.at[index, g], rm.at[t, slot, g], {"tensor": s}
                    ).wait_send()

            sends.append(done)

    pumps = [functools.partial(weights_third, n, name) for n, name in enumerate(wide)]
    def mask_shift(qb):
        K = (qb + 1) * QB
        row_frame = (qb * QB + lax.broadcasted_iota(jnp.int32, (QB, K), 0)) // PATCH
        col_frame = lax.broadcasted_iota(jnp.int32, (QB, K), 1) // PATCH
        allowed = (col_frame <= row_frame) & (col_frame < live)
        return jnp.where(allowed, 0.0, -1e30)

    def attend_block(qb, g, shift):
        K = (qb + 1) * QB
        rows = pl.ds(qb * QB, QB)
        qv = qb_[g, rows, :]
        kv = kb_[g, pl.ds(0, K), :]
        vv = vb_[g, pl.ds(0, K), :]
        outs = []
        for a in range(HG):
            scores = dot(only(qv, a), kv, NT) + shift
            top = jnp.max(scores, axis=-1, keepdims=True)
            weights = jnp.exp(scores - top)
            total = jnp.sum(weights, axis=-1, keepdims=True)
            prob = (weights * (1.0 / total)).astype(BF)
            probs[g * HG + a, rows, pl.ds(0, K)] = prob
            outs.append(dot(prob, vv))
        mo[rows, pl.ds(g * GW, GW)] = pick(outs).astype(BF)

    for qb in reversed(range(NQ)):
        shift = mask_shift(qb)
        for g in range(G):
            attend_block(qb, g, shift)
            hand_over(qb, g)
        if pumps:
            pumps.pop(0)()
    while pumps:
        pumps.pop(0)()

    for n, name in enumerate(wide + ("bias",)):
        weights_ready(n, name)
    for p in range(1, T):
        s = lax.rem(t + p, T)
        for slot in range(R // piece):
            for g in range(G):
                arrived(
                    mr.at[s, pl.ds(slot * piece, piece), pl.ds(g * GW, GW)], rm.at[s, slot, g]
                )
    for k in range(FO):
        arrived(cb.at[pl.ds(k * tok, tok)], rc.at[k])

    wof, wuf, wdf, bf_ = full["w_out"], full["w_up"], full["w_down"], full["bias"]
    second, act, gpre = ref.second, ref.act, ref.gpre
    mlow, gmid, gst, gx = ref.mlow, ref.gmid, ref.gst, ref.gx
    ob, out_ref, ig_ref = ref.ob, ref.out, ref.ig
    sv = ref.sv
    mlp_sum, sec_sum = ref.mlp_sum, ref.sec_sum
    RC = min(256, R)
    FT = min(512, FFh)
    c0 = 0.7978845608028654
    sv[0] = jnp.zeros_like(sv[0])

    def frame_home(k):
        f = t * FO + k
        high = f // N
        j = f * (1 - high) + (2 * N - 1 - f) * high
        return j, high

    def give_back(buf, dst_ref, ss, rs, k):
        j, h = frame_home(k)
        src = buf.at[pl.ds(k * tok, tok)]

        @pl.when(j == i)
        def _():
            pltpu.make_async_copy(src, dst_ref.at[i, h], rs.at[i, h]).start()

        @pl.when(j != i)
        def _():
            remote(src, dst_ref.at[i, h], ss.at[k], rs.at[i, h], {"ctx": j}).start()

        def done():
            @pl.when(j != i)
            def _():
                remote(src, dst_ref.at[i, h], ss.at[k], rs.at[i, h], {"ctx": j}).wait_send()

        sends.append(done)

    def pass_on(dst_ref, fs, rs):
        for p in range(N):
            c = lax.rem(i + p, N)
            for h in (0, 1):
                part = dst_ref.at[c, h]

                @pl.when(owns(h))
                def _(p=p, c=c, h=h, part=part):
                    arrived(part, rs.at[c, h])
                    for q in range(1, T):
                        remote(
                            part, part, fs.at[q, p, h], rs.at[c, h], {"tensor": lax.rem(t + q, T)}
                        ).start()

                def done(p=p, c=c, h=h, part=part):
                    @pl.when(owns(h))
                    def _():
                        for q in range(1, T):
                            remote(
                                part,
                                part,
                                fs.at[q, p, h],
                                rs.at[c, h],
                                {"tensor": lax.rem(t + q, T)},
                            ).wait_send()

                sends.append(done)

    def take_rest(dst_ref, rs):
        for c in range(N):
            for h in (0, 1):

                @pl.when(frames[h] // FO != t)
                def _(c=c, h=h):
                    arrived(dst_ref.at[c, h], rs.at[c, h])

    sg, rg = ref.sg, ref.rg
    def feed_forward(rc_index):
        rows = pl.ds(rc_index * RC, RC)
        attn = dot(mr[0, rows, :], wof[0])
        for s in range(1, T):
            attn = attn + dot(mr[s, rows, :], wof[s])
        middle = xb[row_ds(t * R + rc_index * RC, RC, 64), :].astype(F32) + attn
        xhat, rstd = norm_parts(middle)
        sec = (xhat * vec[2][...] + vec[3][...]).astype(BF)
        second[rows, :] = sec
        cot = cb[rows, :]
        for s in range(T):
            for j in range(FFh // FT):
                cols = pl.ds(j * FT, FT)
                pre = dot(sec, wuf[s, :, cols]) + bf_[s, 0:1, cols]
                gact = dot(cot, wdf[s, cols, :], NT)
                sq = pre * pre
                th = jnp.tanh(c0 * pre * (1.0 + 0.044715 * sq))
                half = 0.5 * (1.0 + th)
                a = (pre * half).astype(BF)
                slope = half + 0.5 * pre * (1.0 - th * th) * (c0 * (1.0 + 0.134145 * sq))
                gp = (gact * slope).astype(BF)
                act[s, rows, cols] = a
                gpre[s, rows, cols] = gp
                sv[0, 4 + s : 5 + s, cols] = sv[0, 4 + s : 5 + s, cols] + jnp.sum(
                    gp.astype(F32), axis=0, keepdims=True
                )
                up = dot(a, wdf[s, cols, :])
                back = dot(gp, wuf[s, :, cols], NT)
                if s == 0 and j == 0:
                    mlp_sum[...] = up
                    sec_sum[...] = back
                else:
                    mlp_sum[...] = mlp_sum[...] + up
                    sec_sum[...] = sec_sum[...] + back
        ob[rows, :] = (middle + mlp_sum[...]).astype(BF)
        gsec = sec_sum[...]
        sv[0, 2:3, 0:D] = sv[0, 2:3, 0:D] + jnp.sum(gsec * xhat, axis=0, keepdims=True)
        sv[0, 3:4, 0:D] = sv[0, 3:4, 0:D] + jnp.sum(gsec, axis=0, keepdims=True)
        gm = cot.astype(F32) + norm_back(gsec, vec[2][...], xhat, rstd)
        gmid[rows, :] = gm
        low = gm.astype(BF)
        mlow[rows, :] = low
        for s in range(T):
            gst[s, rows, :] = dot(low, wof[s], NT).astype(BF)

    for rc_index in range(R // RC):
        rows = pl.ds(rc_index * RC, RC)
        feed_forward(rc_index)
        for s in range(T):
            src = gst.at[s, rows]
            dst = gx.at[row_ds(t * R + rc_index * RC, RC, 64)]

            @pl.when(s == t)
            def _():
                gx[row_ds(t * R + rc_index * RC, RC, 64), :] = gst[s, rows, :]

            @pl.when(s != t)
            def _():
                remote(
                    src, dst, sg.at[s, rc_index], rg.at[t, rc_index], {"tensor": s}
                ).start()

            def done(s=s, src=src, dst=dst, rc_index=rc_index):
                @pl.when(s != t)
                def _():
                    remote(
                        src, dst, sg.at[s, rc_index], rg.at[t, rc_index], {"tensor": s}
                    ).wait_send()

            sends.append(done)
        for k in range(rc_index * RC // tok, (rc_index + 1) * RC // tok):
            give_back(ob, out_ref, ref.so, ref.ro, k)

    reduces = {}
    for name in cfg.plans:
        levels = cfg.plans[name]
        bufs = [getattr(ref, name + "_buf" + str(n)) for n in range(len(levels))]
        reduces[name] = Reduce(
            levels, getattr(ref, name + "_acc"), getattr(ref, name + "_fin"), bufs, getattr(ref, name + "_ss"),
            getattr(ref, name + "_rs"), place,
        )
    cot = cb[...]
    for s in range(T):
        ref.down_acc[s] = dot(act[s], cot, TN).astype(BF)
    reduces["down"].tick()
    for s in range(T):
        ref.up_acc[s] = dot(second[...], gpre[s], TN).astype(BF)
    reduces["up"].tick()
    for s in range(T):
        ref.out_acc[s] = dot(mr[s], mlow[...], TN).astype(BF)
    reduces["out"].tick()

    for p in range(1, T):
        s = lax.rem(t + p, T)
        for n in range(R // RC):
            arrived(gx.at[row_ds(s * R + n * RC, RC, 64)], rg.at[s, n])

    dk, dv, gpb = ref.dk, ref.dv, ref.gpb

    def attend_back_block(g, qb):
        K = (qb + 1) * QB
        rows = pl.ds(qb * QB, QB)
        keys = pl.ds(0, K)
        lanes = pl.ds(g * GW, GW)
        go = gx[rows, lanes]
        prod = go.astype(F32) * mo[rows, lanes].astype(F32)
        qv = qb_[g, rows, :]
        kv = kb_[g, keys, :]
        vv = vb_[g, keys, :]
        outs = []
        dk_sum = dv_sum = None
        for a in range(HG):
            delta = jnp.sum(only(prod, a), axis=-1, keepdims=True)
            goa = only(go, a)
            prob = probs[g * HG + a, rows, keys]
            gprob = dot(goa, vv, NT)
            gs = (prob.astype(F32) * (gprob - delta)).astype(BF)
            outs.append(dot(gs, kv))
            dk_part = dot(gs, only(qv, a), TN)
            dv_part = dot(prob, goa, TN)
            dk_sum = dk_part if dk_sum is None else dk_sum + dk_part
            dv_sum = dv_part if dv_sum is None else dv_sum + dv_part
        gpb[rows, lanes] = (pick(outs) * scale).astype(BF)
        if qb == NQ - 1:
            dk[keys, :] = dk_sum
            dv[keys, :] = dv_sum
        else:
            dk[keys, :] = dk[keys, :] + dk_sum
            dv[keys, :] = dv[keys, :] + dv_sum

    turns = 0
    for g in range(G):
        for qb in reversed(range(NQ)):
            attend_back_block(g, qb)
            if turns == 1:
                pass_on(out_ref, ref.fo, ref.ro)
            reduces["down"].tick()
            reduces["up"].tick()
            reduces["out"].tick()
            turns += 1
        gpb[:, pl.ds(HW + g * GW, GW)] = dk[...].astype(BF)
        gpb[:, pl.ds(2 * HW + g * GW, GW)] = dv[...].astype(BF)

    gns, gnr = ref.gns, ref.gnr
    for p in range(1, T):
        s = lax.rem(t + p, T)
        gns[p - 1] = dot(gpb[row_ds(s * R, R, 64), :], wqkv[...], NT).astype(BF)
        copy = remote(gns.at[p - 1], gnr.at[p - 1], ref.sn.at[p - 1], ref.rn.at[p - 1], {"tensor": s})
        copy.start()
        sends.append(copy.wait_send)
    ref.qkv_acc[0] = dot(nb[...], gpb[...], TN).astype(BF)
    reduces["qkv"].tick()
    own = dot(gpb[row_ds(t * R, R, 64), :], wqkv[...], NT)
    for p in range(1, T):
        arrived(gnr.at[p - 1], ref.rn.at[p - 1])
        own = own + gnr[p - 1].astype(F32)
    xhat, rstd = norm_parts(xb[row_ds(t * R, R, 64), :].astype(F32))
    sv[0, 0:1, 0:D] = jnp.sum(own * xhat, axis=0, keepdims=True)
    sv[0, 1:2, 0:D] = jnp.sum(own, axis=0, keepdims=True)
    igb = ref.igb
    igb[...] = (gmid[...] + norm_back(own, vec[0][...], xhat, rstd)).astype(BF)
    for k in range(FO):
        give_back(igb, ig_ref, ref.si, ref.ri, k)

    rsv = ref.rsv
    everyone = [(a, b) for a, n in (("ctx", N), ("dp", DP), ("tensor", T)) for b in bits_of(n)]
    for n, (axis, bit) in enumerate(everyone):
        copy = remote(
            sv.at[n], rsv.at[n], ref.sv_ss.at[n], ref.sv_rs.at[n],
            {axis: flip(place[axis], bit)},
        )
        copy.start()
        reduces["qkv"].tick()
        copy.wait()
        sv[n + 1] = sv[n] + rsv[n]
    pass_on(ig_ref, ref.fi, ref.ri)
    last = sv[len(everyone)]
    part = D // T
    gains = last[0:4, 0:part]
    bias = last[4:5, 0:FFh]
    for s in range(1, T):
        gains = jnp.where(t == s, last[0:4, s * part : (s + 1) * part], gains)
        bias = jnp.where(t == s, last[4 + s : 5 + s, 0:FFh], bias)
    for n, got in enumerate((ref.grad_ga, ref.grad_sa, ref.grad_gm, ref.grad_sm)):
        got[...] = gains[n : n + 1, :]
    ref.bias_out[...] = bias

    for name in ("down", "up", "out", "qkv"):
        reduces[name].drain()
    take_rest(out_ref, ref.ro)
    take_rest(ig_ref, ref.ri)
    for done in sends:
        done()


def chip_kernel(cfg, names, *refs):
    ref = SimpleNamespace(**dict(zip(names, refs)))
    N, T, DP = cfg.N, cfg.T, cfg.DP
    L, R, FO, tok = cfg.L, cfg.R, cfg.FO, cfg.tok
    D, HW, GW, G, FFh, QB = cfg.D, cfg.HW, cfg.GW, cfg.G, cfg.FFh, cfg.QB
    head_dim = cfg.head_dim
    Z = N // 2
    HG = GW // head_dim
    scale = head_dim ** (-0.5)
    d = lax.axis_index("dp")
    i = lax.axis_index("ctx")
    t = lax.axis_index("tensor")
    z, kap = i // 2, lax.rem(i, 2)
    clip = 2 * z + t
    mate, mirror, beside = {"ctx": flip(i, 1)}, {"tensor": 1 - t}, {"dp": flip(d, 1)}
    place = {"dp": d, "ctx": i, "tensor": t}
    x_in, cot_in = ref.x, ref.cot
    sends = []

    def go(src, dst, send_sem, recv_sem, where):
        copy = remote(src, dst, send_sem, recv_sem, where)
        copy.start()
        sends.append(copy.wait_send)

    def go_if(cond, *args):
        @pl.when(cond)
        def _():
            remote(*args).start()

        def done():
            @pl.when(cond)
            def _():
                remote(*args).wait_send()

        sends.append(done)

    bar = pltpu.get_barrier_semaphore()
    peers = [{"ctx": lax.rem(i + p, N)} for p in range(1, N)]
    peers += [mirror] + [{"dp": flip(d, b)} for b in bits_of(DP)]
    for peer in peers:
        pl.semaphore_signal(bar, inc=1, device_id=peer, device_id_type=MESH)

    wqkv, rq = ref.wq, ref.rq
    blocks = []
    for n in range(HW // head_dim):
        for b in range(3):
            src = ref.w_qkv.at[n, pl.ds(b * head_dim, head_dim)]
            dst = wqkv.at[pl.ds(b * HW + n * head_dim, head_dim)]
            blocks.append((src, dst, ref.bq.at[3 * n + b]))

    @pl.when(kap == t)
    def _():
        for block in blocks:
            pltpu.make_async_copy(*block).start()
        for block in blocks:
            pltpu.make_async_copy(*block).wait()

    pl.semaphore_wait(bar, len(peers))

    frames = (i, 2 * N - 1 - i)
    hops = [0, Z // 2] + [p for p in range(1, Z) if p != Z // 2]

    def deal(src_ref, dst_ref, spot, ss, rs):
        for p in hops:
            zz = lax.rem(z + p, Z)
            for h in (0, 1):
                src = src_ref.at[2 * zz + t, h]
                dst = dst_ref.at[row_ds(spot(h) * tok, tok)]
                to = {"ctx": 2 * zz + h}
                sem = rs.at[spot(h)]
                if p == 0:

                    @pl.when(kap == h)
                    def _(src=src, dst=dst, sem=sem):
                        pltpu.make_async_copy(src, dst, sem).start()

                    go_if(kap != h, src, dst, ss.at[p, h], sem, to)
                else:
                    go(src, dst, ss.at[p, h], sem, to)

    xb, rx = ref.xb, ref.rx
    deal(x_in, xb, lambda h: frames[h], ref.sx, rx)
    cb, rc = ref.cb, ref.rc
    deal(cot_in, cb, lambda h: frames[h] - h * FO, ref.sc, rc)

    half = 3 * HW // 2
    first_half = row_ds(lax.rem(d, 2) * half, half)
    other_half = row_ds((1 - lax.rem(d, 2)) * half, half)
    go_if(
        kap == t, wqkv.at[first_half], wqkv.at[first_half], ref.sq.at[0], rq.at[1],
        mirror,
    )

    share = 2 * lax.rem(d, 2) + kap
    other_dp = 2 * (1 - lax.rem(d, 2)) + kap
    other_core = 2 * lax.rem(d, 2) + 1 - kap
    other_both = 2 * (1 - lax.rem(d, 2)) + 1 - kap
    wide = ("w_out", "w_up", "w_down")
    full = {n: getattr(ref, n + "_full") for n in wide + ("bias",)}
    rw, sw, lw = ref.rw, ref.sw, ref.lw
    own_copies = {}
    for n, name in enumerate(wide + ("bias",)):
        own_copies[name] = pltpu.make_async_copy(getattr(ref, name), full[name].at[t], lw.at[n])
        own_copies[name].start()

    def weight_part(name, s, which):
        quarter = getattr(ref, name).shape[0] // 4
        return full[name].at[s, row_ds(which * quarter, quarter)]

    for n, name in enumerate(wide):
        quarter = getattr(ref, name).shape[0] // 4
        src = getattr(ref, name).at[row_ds(share * quarter, quarter)]
        go(src, weight_part(name, t, share), sw.at[n, 0], rw.at[n, 0], mirror)
    go(ref.bias, full["bias"].at[t], sw.at[3, 0], rw.at[3, 0], mirror)

    def weights_second(name):
        n = wide.index(name)
        part = weight_part(name, 1 - t, share)
        arrived(part, rw.at[n, 0])
        go(part, part, sw.at[n, 1], rw.at[n, 1], beside)
        go(part, part, sw.at[n, 2], rw.at[n, 2], mate)

    def weights_third(name):
        n = wide.index(name)
        part = weight_part(name, 1 - t, other_dp)
        arrived(part, rw.at[n, 1])
        go(part, part, sw.at[n, 3], rw.at[n, 3], mate)

    def weights_ready(name):
        n = wide.index(name)
        arrived(weight_part(name, 1 - t, other_core), rw.at[n, 2])
        arrived(weight_part(name, 1 - t, other_both), rw.at[n, 3])

    RB = 2 * tok
    nb, qa, ka, va = ref.nb, ref.q, ref.k, ref.v
    live = ref.live[clip]
    vec = (ref.gain_attn, ref.shift_attn, ref.gain_mlp, ref.shift_mlp)

    def project(start):
        rows = row_ds(start, RB, 64)
        xhat, _ = norm_parts(xb[rows, :].astype(F32))
        normed = (xhat * vec[0][...] + vec[1][...]).astype(BF)
        nb[rows, :] = normed
        packed = dot(normed, wqkv[...], NT)
        side = lax.broadcasted_iota(jnp.int32, (RB, GW), 1)
        frame = (start + lax.broadcasted_iota(jnp.int32, (RB, GW), 0)) // PATCH
        for n in range(G * HG):
            g, h = n // HG, n % HG
            mine = side // head_dim == h
            other = side - (1 - h) * head_dim
            lo = g * GW
            query = packed[:, lo : lo + GW].astype(BF).astype(F32) * scale
            key = packed[:, HW + lo : HW + lo + GW]
            value = packed[:, 2 * HW + lo : 2 * HW + lo + GW]
            hidden = (other < L // PATCH) & ((frame > other) | (frame >= live))
            qa[n, rows, :] = jnp.where(mine, query, jnp.where(frame == other, 1.0, 0.0)).astype(BF)
            ka[n, rows, :] = jnp.where(mine, key, jnp.where(hidden, -1e30, 0.0)).astype(BF)
            va[n, rows, :] = jnp.where(mine, value, 1.0).astype(BF)

    @pl.when(kap != t)
    def _():
        arrived(wqkv.at[first_half], rq.at[1])

    go_if(
        kap != t, wqkv.at[first_half], wqkv.at[first_half], ref.sq.at[1], rq.at[2], beside
    )
    weights_second("w_out")
    def first_row(p, core):
        far = 2 * lax.rem(z + Z - p, Z)
        return (far * (1 - core) + (2 * N - 2 - far) * core) * tok

    for p in hops:
        for n in range(2):
            row = first_row(p, kap) + n * tok
            part = xb.at[row_ds(row, tok)]
            arrived(part, rx.at[row // tok])
            go(part, part, ref.fx.at[p, n], rx.at[row // tok], mate)
        if p == 0:

            @pl.when(kap != t)
            def _():
                arrived(wqkv.at[other_half], rq.at[2])

        if p != hops[-1]:
            project(first_row(p, kap))
    for p in hops:
        if p == hops[-1]:
            project(first_row(p, kap))
        for n in range(2):
            row = first_row(p, 1 - kap) + n * tok
            arrived(xb.at[row_ds(row, tok)], rx.at[row // tok])
        project(first_row(p, 1 - kap))

    probs, mo, mr = ref.probs, ref.mo, ref.mr
    rm, sm = ref.rm, ref.sm
    NQ = L // QB
    lane = lax.broadcasted_iota(jnp.int32, (QB, GW), 1)

    def pick(first, second):
        return jnp.where(lane < head_dim, first, second)

    def hand_over(qb, g):
        row = qb * QB
        s = row // R
        off = row - s * R
        lanes = pl.ds(g * GW, GW)
        src = mo.at[pl.ds(row, QB), lanes]
        dst = mr.at[kap, pl.ds(off, QB), lanes]

        @pl.when(kap == s)
        def _():
            mr[kap, pl.ds(off, QB), lanes] = mo[pl.ds(row, QB), lanes]

        go_if(kap != s, src, dst, sm.at[qb, g], rm.at[off // QB, g], mate)

    def attend_block(qb, g):
        K = (qb + 1) * QB
        rows, keys = pl.ds(qb * QB, QB), pl.ds(0, K)
        outs, sums = [], []
        for n in range(g * HG, (g + 1) * HG):
            scores = dot(qa[n, rows, :], ka[n, keys, :], NT)
            top = jnp.max(scores, axis=-1, keepdims=True)
            weights = jnp.exp(scores - top).astype(BF)
            probs[n, rows, keys] = weights
            both = dot(weights, va[n, keys, :])
            outs.append(both)
            sums.append(pltpu.roll(both, head_dim, 1))
        inverse = 1.0 / pick(*sums)
        lanes = pl.ds(g * GW, GW)
        ref.inv[rows, lanes] = inverse
        mo[rows, lanes] = (pick(*outs) * inverse).astype(BF)

    pumps = {
        (0, 0): functools.partial(weights_second, "w_up"),
        (2, 0): functools.partial(weights_second, "w_down"),
        (2, 1): functools.partial(weights_third, "w_out"),
    }
    for qb in range(NQ):
        for g in range(G):
            attend_block(qb, g)
            hand_over(qb, g)
            if (qb, g) in pumps:
                pumps[qb, g]()

    wof, wuf, wdf, bf_ = full["w_out"], full["w_up"], full["w_down"], full["bias"]
    second, act, gpre = ref.second, ref.act, ref.gpre
    mlow, gmid, gst, gx = ref.mlow, ref.gmid, ref.gst, ref.gx
    ob, out_ref, ig_ref = ref.ob, ref.out, ref.ig
    mid, bsum, sv = ref.mid, ref.bsum, ref.sv
    mlp_sum, sec_sum = ref.mlp_sum, ref.sec_sum
    RC = min(256, R)
    FT = 2 * FFh // len(cfg.order)
    c0 = 0.7978845608028654

    def middle_rows(c):
        rows = pl.ds(c * RC, RC)
        attn = dot(mr[0, rows, :], wof[0])
        for s in range(1, T):
            attn = attn + dot(mr[s, rows, :], wof[s])
        middle = xb[row_ds(kap * R + c * RC, RC, 64), :].astype(F32) + attn
        mid[rows, :] = middle
        xhat, _ = norm_parts(middle)
        second[rows, :] = (xhat * vec[2][...] + vec[3][...]).astype(BF)

    def feed_forward(s, c, tiles, first):
        rows = pl.ds(c * RC, RC)
        sec = second[rows, :]
        cot = cb[rows, :]
        for j in tiles:
            cols = pl.ds(j * FT, FT)
            pre = dot(sec, wuf[s, :, cols]) + bf_[s, 0:1, cols]
            gact = dot(cot, wdf[s, cols, :], NT)
            sq = pre * pre
            th = jnp.tanh(c0 * pre * (1.0 + 0.044715 * sq))
            half = 0.5 * (1.0 + th)
            a = (pre * half).astype(BF)
            slope = half + 0.5 * pre * (1.0 - th * th) * (c0 * (1.0 + 0.134145 * sq))
            gp = (gact * slope).astype(BF)
            act[s, rows, cols] = a
            gpre[s, rows, cols] = gp
            sums = jnp.sum(gp.astype(F32), axis=0, keepdims=True)
            bsum[s, 0:1, cols] = sums if c == 0 else bsum[s, 0:1, cols] + sums
            up = dot(a, wdf[s, cols, :])
            back = dot(gp, wuf[s, :, cols], NT)
            if first and j == 0:
                mlp_sum[rows, :] = up
                sec_sum[rows, :] = back
            else:
                mlp_sum[rows, :] = mlp_sum[rows, :] + up
                sec_sum[rows, :] = sec_sum[rows, :] + back

    def finish_rows(c):
        rows = pl.ds(c * RC, RC)
        middle = mid[rows, :]
        xhat, rstd = norm_parts(middle)
        ob[rows, :] = (middle + mlp_sum[rows, :]).astype(BF)
        gsec = sec_sum[rows, :]
        gain_sum = jnp.sum(gsec * xhat, axis=0, keepdims=True)
        shift_sum = jnp.sum(gsec, axis=0, keepdims=True)
        if c > 0:
            gain_sum = gain_sum + sv[0, 2:3, 0:D]
            shift_sum = shift_sum + sv[0, 3:4, 0:D]
        sv[0, 2:3, 0:D] = gain_sum
        sv[0, 3:4, 0:D] = shift_sum
        gm = cb[rows, :].astype(F32) + norm_back(gsec, vec[2][...], xhat, rstd)
        gmid[rows, :] = gm
        low = gm.astype(BF)
        mlow[rows, :] = low
        for s in range(T):
            gst[s, rows, :] = dot(low, wof[s], NT).astype(BF)

    def give_back(buf, dst_ref, ss, rs, k):
        j = 2 * lax.rem(z + hops[k // 2], Z) + k % 2
        f = j * (1 - kap) + (2 * N - 1 - j) * kap
        src = buf.at[row_ds((f - kap * FO) * tok, tok)]
        dst, sem = dst_ref.at[clip, kap], rs.at[clip, kap]

        @pl.when(j == i)
        def _():
            pltpu.make_async_copy(src, dst, sem).start()

        go_if(j != i, src, dst, ss.at[k], sem, {"ctx": j})

    def pass_on(dst_ref, fs, rs, p):
        for h in (0, 1):
            cc = 2 * lax.rem(z + Z - hops[p], Z) + t
            part = dst_ref.at[cc, h]
            arrived(part, rs.at[cc, h])
            go(part, part, fs.at[p, h], rs.at[cc, h], mirror)

    def take_rest(dst_ref, rs):
        for p in range(Z):
            for h in (0, 1):
                cc = 2 * p + 1 - t
                arrived(dst_ref.at[cc, h], rs.at[cc, h])

    reduces = {}
    for name, levels in cfg.plans.items():
        bufs = [getattr(ref, name + "_buf" + str(n), None) for n in range(len(levels))]
        reduces[name] = Reduce(
            levels, getattr(ref, name + "_acc"), getattr(ref, name + "_fin"), bufs,
            getattr(ref, name + "_ss"), getattr(ref, name + "_rs"), place,
        )
        to, sem = getattr(ref, name + "_sum"), ref.end.at[len(reduces) - 1]
        reduces[name].result = pltpu.make_async_copy(reduces[name].fin, to, sem)

    def grad_wide(name, s):
        cols = pl.ds(int(name[-1]) * FT, FT)
        if name[0] == "d":
            getattr(ref, name + "_acc")[s] = dot(act[s, :, cols], cb[...], TN).astype(BF)
        else:
            getattr(ref, name + "_acc")[s] = dot(second[...], gpre[s, :, cols], TN).astype(BF)

    rsv = ref.rsv
    everyone = [("ctx", b) for b in bits_of(N)] + [("dp", b) for b in bits_of(DP)]
    everyone += [("tensor", b) for b in bits_of(T)]
    vec_copy = []

    def vec_step():
        n = len(vec_copy)
        if n > 0:
            vec_copy[-1].wait()
            sv[n] = sv[n - 1] + rsv[n - 1]
        if n < len(everyone):
            axis, bit = everyone[n]
            copy = remote(
                sv.at[n], rsv.at[n], ref.sv_ss.at[n], ref.sv_rs.at[n],
                {axis: flip(place[axis], bit)},
            )
            copy.start()
            vec_copy.append(copy)
        else:
            vec_copy.append(None)

    out_done, ig_done = [], []
    script = list(cfg.script)

    def run_script():
        while script:
            item = script.pop(0)
            if item == MARK:
                return
            if item == VECTORS:
                vec_step()
            elif item == OUTPUT:
                pass_on(out_ref, ref.fo, ref.ro, len(out_done))
                out_done.append(item)
            elif item == INPUT_GRAD:
                pass_on(ig_ref, ref.fi, ref.ri, len(ig_done))
                ig_done.append(item)
            else:
                reduces[CHUNKS[item]].tick()

    for name in wide + ("bias",):
        own_copies[name].wait()
    arrived(full["bias"].at[1 - t], rw.at[3, 0])
    weights_ready("w_out")
    for k in range(FO):
        arrived(cb.at[pl.ds(k * tok, tok)], rc.at[k])
    for c in range(R // RC):
        for g in range(G):
            rows, lanes = pl.ds(c * RC, RC), pl.ds(g * GW, GW)
            arrived(mr.at[1 - kap, rows, lanes], rm.at[c, g])
        middle_rows(c)
        feed_forward(t, c, range(FFh // FT), True)
        weights_third("w_up" if c == 0 else "w_down")
    for name in cfg.order:
        grad_wide(name, t)
    weights_ready("w_up")
    weights_ready("w_down")
    for j in range(FFh // FT):
        for c in range(R // RC):
            feed_forward(1 - t, c, (j,), False)
        run_script()
        for name in cfg.order:
            if name[-1] == str(j):
                grad_wide(name, 1 - t)
                reduces[name].tick()
    sv[0, 4:5, 0:FFh] = bsum[0, 0:1, :]
    sv[0, 5:6, 0:FFh] = bsum[1, 0:1, :]
    sg, rg = ref.sg, ref.rg
    for c in range(R // RC):
        finish_rows(c)
        rows = pl.ds(c * RC, RC)
        home = row_ds(kap * R + c * RC, RC, 64)
        gx[home, :] = gst[kap, rows, :]
        go(gst.at[1 - kap, rows], gx.at[home], sg.at[c], rg.at[c], mate)
    for k in range(FO):
        give_back(ob, out_ref, ref.so, ref.ro, k)

    for s in range(T):
        ref.out_acc[s] = dot(mr[s], mlow[...], TN).astype(BF)
    reduces["out"].tick()
    run_script()
    for c in range(R // RC):
        arrived(gx.at[row_ds((1 - kap) * R + c * RC, RC, 64)], rg.at[c])

    dk, dv, gpb = ref.dk, ref.dv, ref.gpb

    def attend_back_block(g, qb):
        K = (qb + 1) * QB
        rows = pl.ds(qb * QB, QB)
        keys = pl.ds(0, K)
        lanes = pl.ds(g * GW, GW)
        grad = gx[rows, lanes].astype(F32) * ref.inv[rows, lanes]
        prod = grad * mo[rows, lanes].astype(F32)
        outs = []
        for n in range(g * HG, (g + 1) * HG):
            h = n - g * HG
            mine = lane // head_dim == h
            other = lane - (1 - h) * head_dim
            delta = jnp.sum(jnp.where(mine, prod, 0.0), axis=-1, keepdims=True)
            high = delta.astype(BF).astype(F32)
            rest = jnp.where(other == 0, -high, jnp.where(other == 1, high - delta, 0.0))
            grads = jnp.where(mine, grad, rest).astype(BF)
            prob = probs[n, rows, keys]
            gs = (prob.astype(F32) * dot(grads, va[n, keys, :], NT)).astype(BF)
            outs.append(dot(gs, ka[n, keys, :]))
            dk_part = dot(gs, qa[n, rows, :], TN)
            dv_part = dot(prob, grads, TN)
            if qb == NQ - 1:
                dk[h, keys, :] = dk_part
                dv[h, keys, :] = dv_part
            else:
                dk[h, keys, :] = dk[h, keys, :] + dk_part
                dv[h, keys, :] = dv[h, keys, :] + dv_part
        gpb[rows, lanes] = (pick(*outs) * scale).astype(BF)

    def key_parts(g):
        first = lax.broadcasted_iota(jnp.int32, (L, GW), 1) < head_dim
        for b, acc in ((1, dk), (2, dv)):
            gpb[:, pl.ds(b * HW + g * GW, GW)] = jnp.where(first, acc[0], acc[1]).astype(BF)

    for g in range(G):
        for qb in reversed(range(NQ)):
            attend_back_block(g, qb)
            if qb == 0:
                key_parts(g)
                for b in range(3):
                    getattr(ref, "qkv" + str(g) + "_acc")[kap, pl.ds(b * GW, GW), :] = dot(
                        gpb[:, pl.ds(b * HW + g * GW, GW)], nb[...], TN
                    ).astype(BF)
                reduces["qkv" + str(g)].tick()
            run_script()

    gns, gnr = ref.gns, ref.gnr
    gns[...] = dot(gpb[row_ds((1 - kap) * R, R, 64), :], wqkv[...]).astype(BF)
    go(gns, gnr, ref.sn.at[0], ref.rn.at[0], mate)
    run_script()
    own = dot(gpb[row_ds(kap * R, R, 64), :], wqkv[...])
    arrived(gnr, ref.rn.at[0])
    own = own + gnr[...].astype(F32)
    xhat, rstd = norm_parts(xb[row_ds(kap * R, R, 64), :].astype(F32))
    sv[0, 0:1, 0:D] = jnp.sum(own * xhat, axis=0, keepdims=True)
    sv[0, 1:2, 0:D] = jnp.sum(own, axis=0, keepdims=True)
    igb = ref.igb
    igb[...] = (gmid[...] + norm_back(own, vec[0][...], xhat, rstd)).astype(BF)
    for k in range(FO):
        give_back(igb, ig_ref, ref.si, ref.ri, k)
    vec_step()
    run_script()
    last = sv[len(everyone)]
    part = D // T
    gains = last[0:4, 0:part]
    bias = last[4:5, 0:FFh]
    for s in range(1, T):
        gains = jnp.where(t == s, last[0:4, s * part : (s + 1) * part], gains)
        bias = jnp.where(t == s, last[4 + s : 5 + s, 0:FFh], bias)
    for n, got in enumerate((ref.grad_ga, ref.grad_sa, ref.grad_gm, ref.grad_sm)):
        got[...] = gains[n : n + 1, :]
    ref.bias_out[...] = bias

    take_rest(out_ref, ref.ro)
    take_rest(ig_ref, ref.ri)
    for chunk in reduces.values():
        chunk.result.wait()
    for done in sends:
        done()


def finish_kernel(sizes, *refs):
    D, HW, FFh, GW, G, head_dim, tiles = sizes
    count = 8 + 2 * tiles + G
    out, ig, ga, sa, gm, sm, bias, wo, *wide = refs[:count]
    outs = refs[count : count + 11]
    b_out, b_ig, b_wo, b_down, b_up, b_qkv, f_qkv, f_wo, f_up, f_down, sem = refs[count + 11 :]
    downs, ups, qkvs = wide[:tiles], wide[tiles : 2 * tiles], wide[2 * tiles :]
    moves = []

    def move(src, dst):
        copy = pltpu.make_async_copy(src, dst, sem.at[len(moves)])
        copy.start()
        moves.append(copy)
        return copy

    reads = [move(src, b_down.at[n]) for n, src in enumerate(downs)]
    reads += [move(src, b_up.at[n]) for n, src in enumerate(ups)]
    reads += [move(wo, b_wo)] + [move(src, b_qkv.at[g]) for g, src in enumerate(qkvs)]
    reads += [move(out, b_out), move(ig, b_ig)]
    part = FFh // tiles
    for n in range(tiles):
        reads[n].wait()
        at = pl.ds(n * part, part)
        f_down[at, :] = b_down[n].astype(F32)
        move(f_down.at[at], outs[10].at[at])
    for n in range(tiles):
        reads[tiles + n].wait()
        at = pl.ds(n * part, part)
        f_up[:, at] = b_up[n].astype(F32)
        move(f_up.at[:, at], outs[8].at[:, at])
    reads[2 * tiles].wait()
    f_wo[...] = b_wo[...].astype(F32)
    move(f_wo, outs[5])
    for n, src, dst in ((-2, b_out, 0), (-1, b_ig, 1)):
        reads[n].wait()
        move(src, outs[dst])
    for src, dst in ((ga, 2), (sa, 3), (gm, 6), (sm, 7), (bias, 9)):
        outs[dst][...] = src[...]
    pair = GW // head_dim
    for g in range(G):
        reads[2 * tiles + 1 + g].wait()
        for h in range(pair):
            for b in range(3):
                f_qkv[g * pair + h, pl.ds(b * head_dim, head_dim), :] = b_qkv[
                    g, pl.ds(b * GW + h * head_dim, head_dim), :
                ].astype(F32)
        at = pl.ds(g * pair, pair)
        move(f_qkv.at[at], outs[4].at[at])
    for copy in moves[len(reads) :]:
        copy.wait()


def finish(got, layout, qkv_shape, sizes, T):
    D, HW, FFh, GW, G, head_dim, tiles = sizes
    vm = pl.BlockSpec(memory_space=pltpu.VMEM)
    hbm = pl.BlockSpec(memory_space=pl.ANY)
    S, V = jax.ShapeDtypeStruct, pltpu.VMEM
    small = S((1, D // T), F32)
    by_head = (qkv_shape[1], qkv_shape[2], qkv_shape[0])
    results = pl.pallas_call(
        functools.partial(finish_kernel, sizes),
        out_shape=[
            S(got.out.shape, BF), S(got.ig.shape, BF), small, small, S(by_head, F32),
            S((HW, D), F32), small, small, S((D, FFh), F32), S((1, FFh), F32), S((FFh, D), F32),
        ],
        in_specs=[hbm] * 2 + [vm] * 5 + [hbm] * (1 + 2 * tiles + G),
        out_specs=[hbm, hbm, vm, vm, hbm, hbm, vm, vm, hbm, vm, hbm],
        scratch_shapes=[
            V(got.out.shape, BF), V(got.ig.shape, BF), V((HW, D), BF),
            V((tiles, FFh // tiles, D), BF), V((tiles, D, FFh // tiles), BF),
            V((G, 3 * GW, D), BF), V(by_head, F32), V((HW, D), F32), V((D, FFh), F32),
            V((FFh, D), F32), pltpu.SemaphoreType.DMA((8 + 4 * tiles + 2 * G,)),
        ],
        compiler_params=pltpu.CompilerParams(vmem_limit_bytes=60 * 2**20),
    )(
        got.out, got.ig, got.grad_ga, got.grad_sa, got.grad_gm, got.grad_sm, got.bias_out,
        got.out_sum, *[getattr(got, n + "_sum") for n in CHUNKS if n != "out"],
    )
    out, ig, ga, sa, qkv, wo, gm, sm, up, bias, down = results
    return (
        out.reshape(layout), ig.reshape(layout), ga[0], sa[0], qkv.transpose(2, 0, 1), wo, gm[0],
        sm[0], up, bias[0], down,
    )


def body(
    sizes,
    inputs,
    cotangent,
    live_frames,
    gain_attn,
    shift_attn,
    w_qkv,
    w_out,
    gain_mlp,
    shift_mlp,
    w_up,
    up_bias,
    w_down,
):
    N, T, DP = sizes["ctx"], sizes["tensor"], sizes["dp"]
    C, _, _, tok, D = inputs.shape
    heads, head_dim = w_qkv.shape[1], w_qkv.shape[2] // 3
    HW = heads * head_dim
    GW = min(128, HW)
    FFh = w_up.shape[1]
    L = 2 * N * tok
    by_chip = T == 2 and HW == 256 and head_dim == 64 and N == 8 and tok == PATCH and N % 2 == 0 and C == N and DP == 2 and FFh == 2 * D
    S_ = 2 if by_chip else T
    R = L // S_
    cfg = SimpleNamespace(
        N=N, T=T, DP=DP, L=L, R=R, FO=2 * N // S_, tok=tok, D=D, HW=HW, GW=GW, G=HW // GW,
        FFh=FFh, QB=256, head_dim=head_dim,
    )
    G = cfg.G
    core, rest = [("ctx", 1)], [("ctx", b) for b in bits_of(N)[1:]]
    over_dp = [("dp", b) for b in bits_of(DP)]
    over_t = [("tensor", b) for b in reversed(bits_of(T))]
    if by_chip:
        steps = {
            "x": over_dp, "y": over_t, "z": rest[:1], "Z": rest[1:-1] + [rest[-1] + ("f",)],
            "R": rest[1:], "X": [over_dp[-1] + ("f",)],
        }
        cfg.plans = plans = {}
        cfg.script, cfg.order = SCRIPT, ORDER
        leads, widths, tiles = {}, {}, len(ORDER) // 2
        for name, order in ORDERS.items():
            begin = [("ctx", 1, "p")] if name[0] == "q" else core
            if name[0] == "d":
                leads[name], widths[name] = (T, FFh // tiles), D
            elif name[0] == "u":
                leads[name], widths[name] = (T, D), FFh // tiles
            elif name[0] == "o":
                leads[name], widths[name] = (T, HW), D
            else:
                leads[name], widths[name] = (T, 3 * GW), D
            plans[name] = plan_levels(*leads[name], begin + sum((steps[c] for c in order), []))
    else:
        cfg.plans = plans = {
            "down": plan_levels(T, FFh, core + over_dp + over_t + rest),
            "up": plan_levels(T, D, core + over_t + over_dp + rest),
            "out": plan_levels(T, HW, core + over_t + over_dp + rest),
            "qkv": plan_levels(1, D, core + over_dp + rest),
        }
        leads = {"down": (T, FFh), "up": (T, D), "out": (T, HW), "qkv": (1, D)}
        widths = {"down": D, "up": FFh, "out": D, "qkv": 3 * HW}

    x = inputs.reshape(C, 2, tok, D)
    cot = cotangent.reshape(C, 2, tok, D)
    wq = w_qkv.transpose(1, 2, 0)
    if not by_chip:
        wq = w_qkv.reshape(D, heads, 3, head_dim).transpose(0, 2, 1, 3).reshape(D, 3 * HW)

    vm = pl.BlockSpec(memory_space=pltpu.VMEM)
    hbm = pl.BlockSpec(memory_space=pl.ANY)
    ins = dict(
        x=(x, hbm),
        cot=(cot, hbm),
        live=(live_frames, pl.BlockSpec(memory_space=pltpu.SMEM)),
        gain_attn=(gain_attn.reshape(1, D), vm),
        shift_attn=(shift_attn.reshape(1, D), vm),
        gain_mlp=(gain_mlp.reshape(1, D), vm),
        shift_mlp=(shift_mlp.reshape(1, D), vm),
        w_qkv=(wq, hbm if by_chip else vm),
        w_out=(w_out, hbm),
        w_up=(w_up, hbm),
        w_down=(w_down, hbm),
        bias=(up_bias.reshape(1, FFh), vm),
    )
    S = jax.ShapeDtypeStruct
    outs = dict(out=S((C, 2, tok, D), BF), ig=S((C, 2, tok, D), BF))
    if by_chip:
        for name in plans:
            outs[name + "_sum"] = S((leads[name][1], widths[name]), BF)
    else:
        outs.update(
            down_fin=S((FFh, D), BF), up_fin=S((D, FFh), BF), out_fin=S((HW, D), BF),
            qkv_fin=S((D, 3 * HW), BF),
        )
    large = len(outs)
    vector = S((1, D // T), F32)
    outs.update(
        grad_ga=vector, grad_sa=vector, grad_gm=vector, grad_sm=vector, bias_out=S((1, FFh), F32)
    )
    W = max(D, FFh)
    SR = -(-(4 + T) // 8) * 8
    n_all = len(bits_of(N)) + len(bits_of(DP)) + len(bits_of(T))
    RC = min(256, R)
    piece = min(cfg.QB, R)
    FO = cfg.FO
    dma = pltpu.SemaphoreType.DMA
    V = pltpu.VMEM
    scratch = dict(
        xb=V((L, D), BF), rx=dma((2 * N,)),
        cb=V((R, D), BF), rc=dma((FO,)),
        w_out_full=V((T, HW, D), BF), w_up_full=V((T, D, FFh), BF),
        w_down_full=V((T, FFh, D), BF), bias_full=V((T, 1, FFh), F32), lw=dma((4,)),
        nb=V((L, D), BF),
        probs=V((heads, L, L), BF), mo=V((L, HW), BF), mr=V((S_, R, HW), BF),
        second=V((R, D), BF), act=V((T, R, FFh), BF), gpre=V((T, R, FFh), BF),
        mlow=V((R, D), BF), gmid=V((R, D), F32), gst=V((T, R, HW), BF), gx=V((L, HW), BF),
        ob=V((R, D), BF), so=dma((FO,)), ro=dma((N, 2)),
        igb=V((R, D), BF), si=dma((FO,)), ri=dma((N, 2)),
        sv=V((n_all + 1, SR, W), F32), rsv=V((n_all, SR, W), F32),
        sv_ss=dma((n_all,)), sv_rs=dma((n_all,)),
        gpb=V((L, 3 * HW), BF),
    )
    if by_chip:
        scratch.update(
            q=V((heads, L, GW), BF), k=V((heads, L, GW), BF), v=V((heads, L, GW), BF),
            inv=V((L, HW), F32), dk=V((2, L, GW), F32), dv=V((2, L, GW), F32),
            sx=dma((N // 2, 2)), fx=dma((N // 2, 2)), sc=dma((N // 2, 2)),
            wq=V((3 * HW, D), BF), rq=dma((3,)), bq=dma((3 * heads,)), sq=dma((2,)),
            rw=dma((4, 4)), sw=dma((4, 4)), rm=dma((R // 256, G)), sm=dma((L // 256, G)),
            mid=V((R, D), F32), bsum=V((T, 8, FFh), F32),
            mlp_sum=V((R, D), F32), sec_sum=V((R, D), F32),
            sg=dma((R // RC,)), rg=dma((R // RC,)),
            fo=dma((N // 2, 2)), fi=dma((N // 2, 2)),
            gns=V((R, D), BF), gnr=V((R, D), BF), sn=dma((1,)), rn=dma((1,)), end=dma((len(plans),)),
        )
    else:
        scratch.update(
            q=V((G, L, GW), BF), k=V((G, L, GW), BF), v=V((G, L, GW), BF),
            dk=V((L, GW), F32), dv=V((L, GW), F32),
            sx=dma((N, 2)), fx=dma((T, FO)), sc=dma((N, 2)), rw=dma((4, 4, T)), sw=dma((4, 4, T)),
            rm=dma((T, R // piece, G)), sm=dma((L // piece, G)),
            sg=dma((T, R // RC)), rg=dma((T, R // RC)), fo=dma((T, N, 2)), fi=dma((T, N, 2)),
            mlp_sum=V((RC, D), F32), sec_sum=V((RC, D), F32),
            gns=V((max(T - 1, 1), R, D), BF), gnr=V((max(T - 1, 1), R, D), BF),
            sn=dma((T,)), rn=dma((T,)),
        )
    for name, levels in plans.items():
        scratch[name + "_acc"] = V(leads[name] + (widths[name],), BF)
        if by_chip:
            scratch[name + "_fin"] = V((leads[name][1], widths[name]), BF)
        scratch[name + "_ss"] = dma((2 * len(levels),))
        scratch[name + "_rs"] = dma((2 * len(levels),))
        for n, (_, _, kind, lead, rows) in enumerate(levels):
            if kind == "p":
                continue
            scratch[name + "_buf" + str(n)] = V((lead, rows, widths[name]), BF)
    names = list(ins) + list(outs) + list(scratch)
    results = pl.pallas_call(
        functools.partial(chip_kernel if by_chip else spread_kernel, cfg, names),
        out_shape=list(outs.values()),
        in_specs=[s for _, s in ins.values()],
        out_specs=[hbm if by_chip else vm] * large + [vm] * (len(outs) - large),
        scratch_shapes=list(scratch.values()),
        compiler_params=pltpu.CompilerParams(
            collective_id=0, has_side_effects=True, vmem_limit_bytes=60 * 2**20
        ),
    )(*[a for a, _ in ins.values()])
    got = SimpleNamespace(**dict(zip(outs, results)))
    if by_chip:
        return finish(got, inputs.shape, w_qkv.shape, (D, HW, FFh, GW, G, head_dim, tiles), T)
    grad_qkv = got.qkv_fin.reshape(D, 3, heads, head_dim).transpose(0, 2, 1, 3)
    return (
        got.out.reshape(inputs.shape),
        got.ig.reshape(inputs.shape),
        got.grad_ga[0],
        got.grad_sa[0],
        grad_qkv.reshape(w_qkv.shape).astype(F32),
        got.out_fin.astype(F32),
        got.grad_gm[0],
        got.grad_sm[0],
        got.up_fin.astype(F32),
        got.bias_out[0],
        got.down_fin.astype(F32),
    )


def solution(mesh):
    return jax.shard_map(
        functools.partial(body, dict(mesh.shape)),
        mesh=mesh,
        in_specs=(
            P("dp", None, "ctx", None, None),
            P("dp", None, "ctx", None, None),
            P("dp"),
            P(),
            P(),
            P(None, "tensor", None),
            P("tensor", None),
            P(),
            P(),
            P(None, "tensor"),
            P("tensor"),
            P("tensor", None),
        ),
        out_specs=(
            P("dp", None, "ctx", None, None),
            P("dp", None, "ctx", None, None),
            P("tensor"),
            P("tensor"),
            P(None, "tensor", None),
            P("tensor", None),
            P("tensor"),
            P("tensor"),
            P(None, "tensor"),
            P("tensor"),
            P("tensor", None),
        ),
        check_vma=False,
    )
```

```python
import functools
from types import SimpleNamespace

import jax
import jax.numpy as jnp
from jax import lax
from jax.experimental import pallas as pl
from jax.experimental.pallas import tpu as pltpu
from jax.sharding import PartitionSpec as P

PATCH = 64
EPSILON = 1e-05
MESH = pl.DeviceIdType.MESH
BF = jnp.bfloat16
F32 = jnp.float32

NN = (((1,), (0,)), ((), ()))
NT = (((1,), (1,)), ((), ()))
TN = (((0,), (0,)), ((), ()))


def dot(a, b, dims=NN):
    return lax.dot_general(a, b, dims, preferred_element_type=F32)


def bits_of(size):
    found, bit = [], 1
    while bit < size:
        found.append(bit)
        bit *= 2
    return found


def flip(index, bit):
    return index + bit - 2 * bit * ((index // bit) % 2)


def bit_of(index, bit):
    return (index // bit) % 2


def row_ds(start, size, unit=16):
    return pl.ds(pl.multiple_of(start, unit), size)


def remote(src, dst, send_sem, recv_sem, where):
    return pltpu.make_async_remote_copy(
        src_ref=src,
        dst_ref=dst,
        send_sem=send_sem,
        recv_sem=recv_sem,
        device_id=where,
        device_id_type=MESH,
    )


def arrived(dst, sem):
    pltpu.make_async_copy(dst, dst, sem).wait()


def norm_parts(values):
    mean = jnp.mean(values, axis=-1, keepdims=True)
    centered = values - mean
    var = jnp.mean(centered * centered, axis=-1, keepdims=True)
    rstd = lax.rsqrt(var + EPSILON)
    return centered * rstd, rstd


def norm_back(grad, gain, xhat, rstd):
    scaled = grad * gain
    first = jnp.mean(scaled, axis=-1, keepdims=True)
    second = jnp.mean(scaled * xhat, axis=-1, keepdims=True)
    return rstd * (scaled - first - xhat * second)


def plan_levels(lead, rows, order):
    levels = []
    for axis, bit, *forced in order:
        if forced:
            kind = forced[0]
            rows = rows // 2 if kind == "p" else rows
        elif axis == "tensor":
            lead //= 2
            kind = "t"
        elif rows % 32 == 0:
            rows //= 2
            kind = "r"
        else:
            kind = "f"
        levels.append((axis, bit, kind, lead, rows))
    return levels


ORDERS = {
    "down0": "zxyZ",
    "down1": "yxzZ",
    "up0": "yzxZ",
    "up1": "xyzZ",
    "out": "yxzZ",
    "qkv0": "yxzZ",
    "qkv1": "yxzZ",
}
CHUNKS = tuple(ORDERS)
VECTORS, OUTPUT, INPUT_GRAD, MARK = range(7, 11)
ORDER = tuple(CHUNKS[n] for n in (0, 2, 1, 3))
SCRIPT = (
    10, 0, 10, 2, 3, 1, 10, 10, 10, 10, 10, 10, 10, 10, 10, 2, 5, 6, 10, 1, 3, 5, 4, 1, 2, 9, 6,
    5, 2, 0, 9, 3, 5, 7, 1, 4, 6, 3, 0, 4, 5, 0, 9, 9, 2, 1, 4, 6, 8, 5, 3, 8, 1, 7, 0, 4, 2, 8,
    5, 3, 6, 4, 1, 8, 7, 0, 6, 7, 5, 2, 4, 1, 3, 0, 6, 4, 3, 2, 0, 7, 6,
)


class Reduce:
    def __init__(self, levels, acc, fin, bufs, ss, rs, place):
        self.levels, self.acc, self.fin = levels, acc, fin
        self.bufs, self.ss, self.rs, self.place = bufs, ss, rs, place
        self.lead, self.rows = acc.shape[0], acc.shape[1]
        self.toff, self.roff = 0, 0
        self.marks = []
        self.copy = self.result = None
        self.steps = []
        count = len(levels)
        for n in range(count):
            self.steps.append(functools.partial(self.step, n))
        self.steps.append(self.turn)

    def send(self, n):
        axis, bit, kind, lead, rows = self.levels[n]
        mine = bit_of(self.place[axis], bit)
        self.marks.append((self.toff, self.roff, self.lead, self.rows))
        toff, roff = self.toff, self.roff
        dst = self.bufs[n]
        if kind == "p":
            toff = mine
            roff = self.roff + (1 - mine) * rows
            self.roff = self.roff + mine * rows
            dst = self.acc.at[pl.ds(toff, 1), row_ds(roff, rows)]
            self.copy = remote(
                dst, dst, self.ss.at[n], self.rs.at[n], {axis: flip(self.place[axis], bit)}
            )
            self.lead, self.rows = lead, rows
            self.copy.start()
            return
        if kind == "t":
            toff = self.toff + (1 - mine) * lead
            self.toff = self.toff + mine * lead
        elif kind == "r":
            roff = self.roff + (1 - mine) * rows
            self.roff = self.roff + mine * rows
        self.lead, self.rows = lead, rows
        self.copy = remote(
            self.acc.at[pl.ds(toff, lead), row_ds(roff, rows)],
            dst,
            self.ss.at[n],
            self.rs.at[n],
            {axis: flip(self.place[axis], bit)},
        )
        self.copy.start()

    def absorb(self, n):
        self.copy.wait()
        if self.levels[n][2] == "p":
            return
        buf = self.bufs[n]
        part = 32 if self.rows % 32 == 0 else 16
        for a in range(self.lead):

            def add(b, _):
                off = pl.multiple_of(b * part, 16)
                at = row_ds(self.roff + off, part)
                old = self.acc[self.toff + a, at, :].astype(F32)
                new = buf[a, pl.ds(off, part), :].astype(F32)
                self.acc[self.toff + a, at, :] = (old + new).astype(BF)
                return 0

            lax.fori_loop(0, self.rows // part, add, 0)

    def step(self, n):
        if n > 0:
            self.absorb(n - 1)
        self.send(n)

    def turn(self):
        count = len(self.levels)
        self.absorb(count - 1)
        at = row_ds(self.roff, self.rows)
        self.fin[at, :] = self.acc[self.toff, at, :]
        back = [n for n in reversed(range(count)) if self.levels[n][2] in "pr"]
        for k, n in enumerate(back):
            if k == 0:
                self.gather(n, True)
            else:
                self.steps.append(functools.partial(self.gather, n, False))
        self.steps.append(self.close)

    def gather(self, n, first):
        if not first:
            self.copy.wait()
        axis, bit, kind, lead, rows = self.levels[n]
        part = self.fin.at[row_ds(self.roff, rows)]
        count = len(self.levels)
        self.copy = remote(
            part,
            part,
            self.ss.at[count + n],
            self.rs.at[count + n],
            {axis: flip(self.place[axis], bit)},
        )
        self.copy.start()
        self.roff = self.marks[n][1]

    def close(self):
        self.copy.wait()
        if self.result is not None:
            self.result.start()

    def tick(self):
        if self.steps:
            self.steps.pop(0)()
            return True
        return False

    def drain(self):
        while self.tick():
            pass


def spread_kernel(cfg, names, *refs):
    ref = SimpleNamespace(**dict(zip(names, refs)))
    N, T, DP = cfg.N, cfg.T, cfg.DP
    L, R, FO, tok = cfg.L, cfg.R, cfg.FO, cfg.tok
    D, HW, GW, G, FFh, QB = cfg.D, cfg.HW, cfg.GW, cfg.G, cfg.FFh, cfg.QB
    head_dim = cfg.head_dim
    HG = GW // head_dim
    scale = head_dim ** (-0.5)
    d = lax.axis_index("dp")
    i = lax.axis_index("ctx")
    t = lax.axis_index("tensor")
    place = {"dp": d, "ctx": i, "tensor": t}
    x_in, cot_in = ref.x, ref.cot
    sends = []

    bar = pltpu.get_barrier_semaphore()
    peers = [{"ctx": lax.rem(i + p, N)} for p in range(1, N)]
    peers += [{"tensor": lax.rem(t + p, T)} for p in range(1, T)]
    peers += [{"dp": flip(d, b)} for b in bits_of(DP)]
    for peer in peers:
        pl.semaphore_signal(bar, inc=1, device_id=peer, device_id_type=MESH)
    pl.semaphore_wait(bar, len(peers))

    frames = (i, 2 * N - 1 - i)

    def owns(h):
        return frames[h] // FO == t

    xb, rx, sx, fx = ref.xb, ref.rx, ref.sx, ref.fx
    for p in range(N):
        c = lax.rem(i + p, N)
        for h in (0, 1):
            to = xb.at[row_ds(frames[h] * tok, tok)]

            @pl.when(owns(h))
            def _(p=p, c=c, h=h, to=to):
                if p == 0:
                    pltpu.make_async_copy(x_in.at[c, h], to, rx.at[frames[h]]).start()
                else:
                    remote(
                        x_in.at[c, h], to, sx.at[p, h], rx.at[frames[h]], {"ctx": c}
                    ).start()

            if p > 0:

                def done(p=p, c=c, h=h, to=to):
                    @pl.when(owns(h))
                    def _():
                        remote(
                            x_in.at[c, h], to, sx.at[p, h], rx.at[frames[h]], {"ctx": c}
                        ).wait_send()

                sends.append(done)

    def near(k):
        return t * FO + lax.rem(i + k, FO)

    for k in range(FO):
        f = near(k)
        part = xb.at[row_ds(f * tok, tok)]
        arrived(part, rx.at[f])
        for p in range(1, T):
            copy = remote(
                part, part, fx.at[p, k], rx.at[f], {"tensor": lax.rem(t + p, T)}
            )
            copy.start()
            sends.append(copy.wait_send)

    cb, rc, sc = ref.cb, ref.rc, ref.sc
    for p in range(N):
        c = lax.rem(i + p, N)
        for h in (0, 1):
            slot = lax.rem(frames[h], FO)
            to = cb.at[row_ds(slot * tok, tok)]

            @pl.when(owns(h))
            def _(p=p, c=c, h=h, to=to, slot=slot):
                if p == 0:
                    pltpu.make_async_copy(cot_in.at[c, h], to, rc.at[slot]).start()
                else:
                    remote(cot_in.at[c, h], to, sc.at[p, h], rc.at[slot], {"ctx": c}).start()

            if p > 0:

                def done(p=p, c=c, h=h, to=to, slot=slot):
                    @pl.when(owns(h))
                    def _():
                        remote(
                            cot_in.at[c, h], to, sc.at[p, h], rc.at[slot], {"ctx": c}
                        ).wait_send()

                sends.append(done)

    share = 2 * lax.rem(d, 2) + lax.rem(i, 2)
    wide = ("w_out", "w_up", "w_down")
    full = {n: getattr(ref, n + "_full") for n in wide + ("bias",)}
    rw, sw, lw = ref.rw, ref.sw, ref.lw
    own_copies = []
    for n, name in enumerate(wide + ("bias",)):
        copy = pltpu.make_async_copy(getattr(ref, name), full[name].at[t], lw.at[n])
        copy.start()
        own_copies.append(copy)
    for p in range(1, T):
        to = {"tensor": lax.rem(t + p, T)}
        copy = remote(ref.bias, full["bias"].at[t], sw.at[3, 0, p], rw.at[3, 0, t], to)
        copy.start()
        sends.append(copy.wait_send)
    for n, name in enumerate(wide):
        quarter = getattr(ref, name).shape[0] // 4
        at = row_ds(share * quarter, quarter)
        for p in range(1, T):
            to = {"tensor": lax.rem(t + p, T)}
            copy = remote(
                getattr(ref, name).at[at], full[name].at[t, at], sw.at[n, 0, p], rw.at[n, 0, t], to
            )
            copy.start()
            sends.append(copy.wait_send)

    other_dp = 2 * (1 - lax.rem(d, 2)) + lax.rem(i, 2)
    other_core = 2 * lax.rem(d, 2) + 1 - lax.rem(i, 2)
    other_both = 2 * (1 - lax.rem(d, 2)) + 1 - lax.rem(i, 2)

    def weight_part(name, s, which):
        quarter = getattr(ref, name).shape[0] // 4
        return full[name].at[s, row_ds(which * quarter, quarter)]

    def weights_second(n, name):
        for p in range(1, T):
            s = lax.rem(t + p, T)
            part = weight_part(name, s, share)
            arrived(part, rw.at[n, 0, s])
            for stage, to in ((1, {"dp": flip(d, 1)}), (2, {"ctx": flip(i, 1)})):
                copy = remote(part, part, sw.at[n, stage, p], rw.at[n, stage, s], to)
                copy.start()
                sends.append(copy.wait_send)

    def weights_third(n, name):
        for p in range(1, T):
            s = lax.rem(t + p, T)
            part = weight_part(name, s, other_dp)
            arrived(part, rw.at[n, 1, s])
            copy = remote(
                part, part, sw.at[n, 3, p], rw.at[n, 3, s], {"ctx": flip(i, 1)}
            )
            copy.start()
            sends.append(copy.wait_send)

    def weights_ready(n, name):
        own_copies[n].wait()
        for p in range(1, T):
            s = lax.rem(t + p, T)
            if name == "bias":
                arrived(full[name].at[s], rw.at[n, 0, s])
            else:
                arrived(weight_part(name, s, other_core), rw.at[n, 2, s])
                arrived(weight_part(name, s, other_both), rw.at[n, 3, s])

    RB = min(256, R)
    nb, qb_, kb_, vb_ = ref.nb, ref.q, ref.k, ref.v
    vec = (ref.gain_attn, ref.shift_attn, ref.gain_mlp, ref.shift_mlp)
    wqkv = ref.w_qkv

    def project(start):
        rows = row_ds(start, RB, 64)
        xhat, _ = norm_parts(xb[rows, :].astype(F32))
        normed = (xhat * vec[0][...] + vec[1][...]).astype(BF)
        nb[rows, :] = normed
        packed = dot(normed, wqkv[...])
        for g in range(G):
            lo = g * GW
            qb_[g, rows, :] = (packed[:, lo : lo + GW].astype(BF).astype(F32) * scale).astype(BF)
            kb_[g, rows, :] = packed[:, HW + lo : HW + lo + GW].astype(BF)
            vb_[g, rows, :] = packed[:, 2 * HW + lo : 2 * HW + lo + GW].astype(BF)

    for k in range(R // RB):
        project(t * R + k * RB)
    for p in range(1, T):
        s = lax.rem(t + p, T)
        for k in range(FO):
            f = s * FO + k
            arrived(xb.at[row_ds(f * tok, tok)], rx.at[f])
        for k in range(R // RB):
            project(s * R + k * RB)

    for n, name in enumerate(wide):
        weights_second(n, name)

    live = ref.live[i]
    probs, mo, mr = ref.probs, ref.mo, ref.mr
    rm, sm = ref.rm, ref.sm
    piece = min(QB, R)
    NQ = L // QB
    lane = lax.broadcasted_iota(jnp.int32, (QB, GW), 1) // head_dim

    def pick(parts):
        out = parts[0]
        for a in range(1, HG):
            out = jnp.where(lane == a, parts[a], out)
        return out

    def only(values, a):
        if HG == 1:
            return values
        return jnp.where(lane == a, values, jnp.zeros_like(values))

    def hand_over(qb, g):
        for b in range(QB // piece):
            row = qb * QB + b * piece
            s = row // R
            slot = (row - s * R) // piece
            src = mo.at[pl.ds(row, piece), pl.ds(g * GW, GW)]
            dst = mr.at[t, pl.ds(row - s * R, piece), pl.ds(g * GW, GW)]
            index = row // piece

            @pl.when(s == t)
            def _():
                mr[t, pl.ds(row - s * R, piece), pl.ds(g * GW, GW)] = mo[
                    pl.ds(row, piece), pl.ds(g * GW, GW)
                ]

            @pl.when(s != t)
            def _():
                remote(src, dst, sm.at[index, g], rm.at[t, slot, g], {"tensor": s}).start()

            def done(s=s, src=src, dst=dst, index=index, slot=slot):
                @pl.when(s != t)
                def _():
                    remote(
                        src, dst, sm.at[index, g], rm.at[t, slot, g], {"tensor": s}
                    ).wait_send()

            sends.append(done)

    pumps = [functools.partial(weights_third, n, name) for n, name in enumerate(wide)]
    def mask_shift(qb):
        K = (qb + 1) * QB
        row_frame = (qb * QB + lax.broadcasted_iota(jnp.int32, (QB, K), 0)) // PATCH
        col_frame = lax.broadcasted_iota(jnp.int32, (QB, K), 1) // PATCH
        allowed = (col_frame <= row_frame) & (col_frame < live)
        return jnp.where(allowed, 0.0, -1e30)

    def attend_block(qb, g, shift):
        K = (qb + 1) * QB
        rows = pl.ds(qb * QB, QB)
        qv = qb_[g, rows, :]
        kv = kb_[g, pl.ds(0, K), :]
        vv = vb_[g, pl.ds(0, K), :]
        outs = []
        for a in range(HG):
            scores = dot(only(qv, a), kv, NT) + shift
            top = jnp.max(scores, axis=-1, keepdims=True)
            weights = jnp.exp(scores - top)
            total = jnp.sum(weights, axis=-1, keepdims=True)
            prob = (weights * (1.0 / total)).astype(BF)
            probs[g * HG + a, rows, pl.ds(0, K)] = prob
            outs.append(dot(prob, vv))
        mo[rows, pl.ds(g * GW, GW)] = pick(outs).astype(BF)

    for qb in reversed(range(NQ)):
        shift = mask_shift(qb)
        for g in range(G):
            attend_block(qb, g, shift)
            hand_over(qb, g)
        if pumps:
            pumps.pop(0)()
    while pumps:
        pumps.pop(0)()

    for n, name in enumerate(wide + ("bias",)):
        weights_ready(n, name)
    for p in range(1, T):
        s = lax.rem(t + p, T)
        for slot in range(R // piece):
            for g in range(G):
                arrived(
                    mr.at[s, pl.ds(slot * piece, piece), pl.ds(g * GW, GW)], rm.at[s, slot, g]
                )
    for k in range(FO):
        arrived(cb.at[pl.ds(k * tok, tok)], rc.at[k])

    wof, wuf, wdf, bf_ = full["w_out"], full["w_up"], full["w_down"], full["bias"]
    second, act, gpre = ref.second, ref.act, ref.gpre
    mlow, gmid, gst, gx = ref.mlow, ref.gmid, ref.gst, ref.gx
    ob, out_ref, ig_ref = ref.ob, ref.out, ref.ig
    sv = ref.sv
    mlp_sum, sec_sum = ref.mlp_sum, ref.sec_sum
    RC = min(256, R)
    FT = min(512, FFh)
    c0 = 0.7978845608028654
    sv[0] = jnp.zeros_like(sv[0])

    def frame_home(k):
        f = t * FO + k
        high = f // N
        j = f * (1 - high) + (2 * N - 1 - f) * high
        return j, high

    def give_back(buf, dst_ref, ss, rs, k):
        j, h = frame_home(k)
        src = buf.at[pl.ds(k * tok, tok)]

        @pl.when(j == i)
        def _():
            pltpu.make_async_copy(src, dst_ref.at[i, h], rs.at[i, h]).start()

        @pl.when(j != i)
        def _():
            remote(src, dst_ref.at[i, h], ss.at[k], rs.at[i, h], {"ctx": j}).start()

        def done():
            @pl.when(j != i)
            def _():
                remote(src, dst_ref.at[i, h], ss.at[k], rs.at[i, h], {"ctx": j}).wait_send()

        sends.append(done)

    def pass_on(dst_ref, fs, rs):
        for p in range(N):
            c = lax.rem(i + p, N)
            for h in (0, 1):
                part = dst_ref.at[c, h]

                @pl.when(owns(h))
                def _(p=p, c=c, h=h, part=part):
                    arrived(part, rs.at[c, h])
                    for q in range(1, T):
                        remote(
                            part, part, fs.at[q, p, h], rs.at[c, h], {"tensor": lax.rem(t + q, T)}
                        ).start()

                def done(p=p, c=c, h=h, part=part):
                    @pl.when(owns(h))
                    def _():
                        for q in range(1, T):
                            remote(
                                part,
                                part,
                                fs.at[q, p, h],
                                rs.at[c, h],
                                {"tensor": lax.rem(t + q, T)},
                            ).wait_send()

                sends.append(done)

    def take_rest(dst_ref, rs):
        for c in range(N):
            for h in (0, 1):

                @pl.when(frames[h] // FO != t)
                def _(c=c, h=h):
                    arrived(dst_ref.at[c, h], rs.at[c, h])

    sg, rg = ref.sg, ref.rg
    def feed_forward(rc_index):
        rows = pl.ds(rc_index * RC, RC)
        attn = dot(mr[0, rows, :], wof[0])
        for s in range(1, T):
            attn = attn + dot(mr[s, rows, :], wof[s])
        middle = xb[row_ds(t * R + rc_index * RC, RC, 64), :].astype(F32) + attn
        xhat, rstd = norm_parts(middle)
        sec = (xhat * vec[2][...] + vec[3][...]).astype(BF)
        second[rows, :] = sec
        cot = cb[rows, :]
        for s in range(T):
            for j in range(FFh // FT):
                cols = pl.ds(j * FT, FT)
                pre = dot(sec, wuf[s, :, cols]) + bf_[s, 0:1, cols]
                gact = dot(cot, wdf[s, cols, :], NT)
                sq = pre * pre
                th = jnp.tanh(c0 * pre * (1.0 + 0.044715 * sq))
                half = 0.5 * (1.0 + th)
                a = (pre * half).astype(BF)
                slope = half + 0.5 * pre * (1.0 - th * th) * (c0 * (1.0 + 0.134145 * sq))
                gp = (gact * slope).astype(BF)
                act[s, rows, cols] = a
                gpre[s, rows, cols] = gp
                sv[0, 4 + s : 5 + s, cols] = sv[0, 4 + s : 5 + s, cols] + jnp.sum(
                    gp.astype(F32), axis=0, keepdims=True
                )
                up = dot(a, wdf[s, cols, :])
                back = dot(gp, wuf[s, :, cols], NT)
                if s == 0 and j == 0:
                    mlp_sum[...] = up
                    sec_sum[...] = back
                else:
                    mlp_sum[...] = mlp_sum[...] + up
                    sec_sum[...] = sec_sum[...] + back
        ob[rows, :] = (middle + mlp_sum[...]).astype(BF)
        gsec = sec_sum[...]
        sv[0, 2:3, 0:D] = sv[0, 2:3, 0:D] + jnp.sum(gsec * xhat, axis=0, keepdims=True)
        sv[0, 3:4, 0:D] = sv[0, 3:4, 0:D] + jnp.sum(gsec, axis=0, keepdims=True)
        gm = cot.astype(F32) + norm_back(gsec, vec[2][...], xhat, rstd)
        gmid[rows, :] = gm
        low = gm.astype(BF)
        mlow[rows, :] = low
        for s in range(T):
            gst[s, rows, :] = dot(low, wof[s], NT).astype(BF)

    for rc_index in range(R // RC):
        rows = pl.ds(rc_index * RC, RC)
        feed_forward(rc_index)
        for s in range(T):
            src = gst.at[s, rows]
            dst = gx.at[row_ds(t * R + rc_index * RC, RC, 64)]

            @pl.when(s == t)
            def _():
                gx[row_ds(t * R + rc_index * RC, RC, 64), :] = gst[s, rows, :]

            @pl.when(s != t)
            def _():
                remote(
                    src, dst, sg.at[s, rc_index], rg.at[t, rc_index], {"tensor": s}
                ).start()

            def done(s=s, src=src, dst=dst, rc_index=rc_index):
                @pl.when(s != t)
                def _():
                    remote(
                        src, dst, sg.at[s, rc_index], rg.at[t, rc_index], {"tensor": s}
                    ).wait_send()

            sends.append(done)
        for k in range(rc_index * RC // tok, (rc_index + 1) * RC // tok):
            give_back(ob, out_ref, ref.so, ref.ro, k)

    reduces = {}
    for name in cfg.plans:
        levels = cfg.plans[name]
        bufs = [getattr(ref, name + "_buf" + str(n)) for n in range(len(levels))]
        reduces[name] = Reduce(
            levels, getattr(ref, name + "_acc"), getattr(ref, name + "_fin"), bufs, getattr(ref, name + "_ss"),
            getattr(ref, name + "_rs"), place,
        )
    cot = cb[...]
    for s in range(T):
        ref.down_acc[s] = dot(act[s], cot, TN).astype(BF)
    reduces["down"].tick()
    for s in range(T):
        ref.up_acc[s] = dot(second[...], gpre[s], TN).astype(BF)
    reduces["up"].tick()
    for s in range(T):
        ref.out_acc[s] = dot(mr[s], mlow[...], TN).astype(BF)
    reduces["out"].tick()

    for p in range(1, T):
        s = lax.rem(t + p, T)
        for n in range(R // RC):
            arrived(gx.at[row_ds(s * R + n * RC, RC, 64)], rg.at[s, n])

    dk, dv, gpb = ref.dk, ref.dv, ref.gpb

    def attend_back_block(g, qb):
        K = (qb + 1) * QB
        rows = pl.ds(qb * QB, QB)
        keys = pl.ds(0, K)
        lanes = pl.ds(g * GW, GW)
        go = gx[rows, lanes]
        prod = go.astype(F32) * mo[rows, lanes].astype(F32)
        qv = qb_[g, rows, :]
        kv = kb_[g, keys, :]
        vv = vb_[g, keys, :]
        outs = []
        dk_sum = dv_sum = None
        for a in range(HG):
            delta = jnp.sum(only(prod, a), axis=-1, keepdims=True)
            goa = only(go, a)
            prob = probs[g * HG + a, rows, keys]
            gprob = dot(goa, vv, NT)
            gs = (prob.astype(F32) * (gprob - delta)).astype(BF)
            outs.append(dot(gs, kv))
            dk_part = dot(gs, only(qv, a), TN)
            dv_part = dot(prob, goa, TN)
            dk_sum = dk_part if dk_sum is None else dk_sum + dk_part
            dv_sum = dv_part if dv_sum is None else dv_sum + dv_part
        gpb[rows, lanes] = (pick(outs) * scale).astype(BF)
        if qb == NQ - 1:
            dk[keys, :] = dk_sum
            dv[keys, :] = dv_sum
        else:
            dk[keys, :] = dk[keys, :] + dk_sum
            dv[keys, :] = dv[keys, :] + dv_sum

    turns = 0
    for g in range(G):
        for qb in reversed(range(NQ)):
            attend_back_block(g, qb)
            if turns == 1:
                pass_on(out_ref, ref.fo, ref.ro)
            reduces["down"].tick()
            reduces["up"].tick()
            reduces["out"].tick()
            turns += 1
        gpb[:, pl.ds(HW + g * GW, GW)] = dk[...].astype(BF)
        gpb[:, pl.ds(2 * HW + g * GW, GW)] = dv[...].astype(BF)

    gns, gnr = ref.gns, ref.gnr
    for p in range(1, T):
        s = lax.rem(t + p, T)
        gns[p - 1] = dot(gpb[row_ds(s * R, R, 64), :], wqkv[...], NT).astype(BF)
        copy = remote(gns.at[p - 1], gnr.at[p - 1], ref.sn.at[p - 1], ref.rn.at[p - 1], {"tensor": s})
        copy.start()
        sends.append(copy.wait_send)
    ref.qkv_acc[0] = dot(nb[...], gpb[...], TN).astype(BF)
    reduces["qkv"].tick()
    own = dot(gpb[row_ds(t * R, R, 64), :], wqkv[...], NT)
    for p in range(1, T):
        arrived(gnr.at[p - 1], ref.rn.at[p - 1])
        own = own + gnr[p - 1].astype(F32)
    xhat, rstd = norm_parts(xb[row_ds(t * R, R, 64), :].astype(F32))
    sv[0, 0:1, 0:D] = jnp.sum(own * xhat, axis=0, keepdims=True)
    sv[0, 1:2, 0:D] = jnp.sum(own, axis=0, keepdims=True)
    igb = ref.igb
    igb[...] = (gmid[...] + norm_back(own, vec[0][...], xhat, rstd)).astype(BF)
    for k in range(FO):
        give_back(igb, ig_ref, ref.si, ref.ri, k)

    rsv = ref.rsv
    everyone = [(a, b) for a, n in (("ctx", N), ("dp", DP), ("tensor", T)) for b in bits_of(n)]
    for n, (axis, bit) in enumerate(everyone):
        copy = remote(
            sv.at[n], rsv.at[n], ref.sv_ss.at[n], ref.sv_rs.at[n],
            {axis: flip(place[axis], bit)},
        )
        copy.start()
        reduces["qkv"].tick()
        copy.wait()
        sv[n + 1] = sv[n] + rsv[n]
    pass_on(ig_ref, ref.fi, ref.ri)
    last = sv[len(everyone)]
    part = D // T
    gains = last[0:4, 0:part]
    bias = last[4:5, 0:FFh]
    for s in range(1, T):
        gains = jnp.where(t == s, last[0:4, s * part : (s + 1) * part], gains)
        bias = jnp.where(t == s, last[4 + s : 5 + s, 0:FFh], bias)
    for n, got in enumerate((ref.grad_ga, ref.grad_sa, ref.grad_gm, ref.grad_sm)):
        got[...] = gains[n : n + 1, :]
    ref.bias_out[...] = bias

    for name in ("down", "up", "out", "qkv"):
        reduces[name].drain()
    take_rest(out_ref, ref.ro)
    take_rest(ig_ref, ref.ri)
    for done in sends:
        done()


def chip_kernel(cfg, names, *refs):
    ref = SimpleNamespace(**dict(zip(names, refs)))
    N, T, DP = cfg.N, cfg.T, cfg.DP
    L, R, FO, tok = cfg.L, cfg.R, cfg.FO, cfg.tok
    D, HW, GW, G, FFh, QB = cfg.D, cfg.HW, cfg.GW, cfg.G, cfg.FFh, cfg.QB
    head_dim = cfg.head_dim
    Z = N // 2
    HG = GW // head_dim
    scale = head_dim ** (-0.5)
    d = lax.axis_index("dp")
    i = lax.axis_index("ctx")
    t = lax.axis_index("tensor")
    z, kap = i // 2, lax.rem(i, 2)
    clip = 2 * z + t
    mate, mirror, beside = {"ctx": flip(i, 1)}, {"tensor": 1 - t}, {"dp": flip(d, 1)}
    place = {"dp": d, "ctx": i, "tensor": t}
    x_in, cot_in = ref.x, ref.cot
    sends = []

    def go(src, dst, send_sem, recv_sem, where):
        copy = remote(src, dst, send_sem, recv_sem, where)
        copy.start()
        sends.append(copy.wait_send)

    def go_if(cond, *args):
        @pl.when(cond)
        def _():
            remote(*args).start()

        def done():
            @pl.when(cond)
            def _():
                remote(*args).wait_send()

        sends.append(done)

    vec = [ref.vecs.at[n] for n in range(4)]
    vec_loads = []
    for n, src in enumerate((ref.gain_attn, ref.shift_attn, ref.gain_mlp, ref.shift_mlp)):
        vec_loads.append(pltpu.make_async_copy(src, vec[n], ref.vl.at[n]))
        vec_loads[-1].start()

    bar = pltpu.get_barrier_semaphore()
    peers = [{"ctx": lax.rem(i + p, N)} for p in (4, 3, 5, 2, 6, 1, 7)]
    peers += [mirror] + [{"dp": flip(d, b)} for b in bits_of(DP)]
    for peer in peers:
        pl.semaphore_signal(bar, inc=1, device_id=peer, device_id_type=MESH)

    wqkv, rq = ref.wq, ref.rq
    blocks = []
    for n in range(HW // head_dim):
        for b in range(3):
            src = ref.w_qkv.at[n, pl.ds(b * head_dim, head_dim)]
            dst = wqkv.at[pl.ds(b * HW + n * head_dim, head_dim)]
            blocks.append((src, dst, ref.bq.at[3 * n + b]))

    @pl.when(kap == t)
    def _():
        for block in blocks:
            pltpu.make_async_copy(*block).start()
        for block in blocks:
            pltpu.make_async_copy(*block).wait()

    pl.semaphore_wait(bar, len(peers))

    frames = (i, 2 * N - 1 - i)
    hops = [0, Z // 2] + [p for p in range(1, Z) if p != Z // 2]

    def deal(src_ref, dst_ref, spot, ss, rs):
        for p in hops:
            zz = lax.rem(z + p, Z)
            for h in (0, 1):
                src = src_ref.at[2 * zz + t, h]
                dst = dst_ref.at[row_ds(spot(h) * tok, tok)]
                to = {"ctx": 2 * zz + h}
                sem = rs.at[spot(h)]
                if p == 0:

                    @pl.when(kap == h)
                    def _(src=src, dst=dst, sem=sem):
                        pltpu.make_async_copy(src, dst, sem).start()

                    go_if(kap != h, src, dst, ss.at[p, h], sem, to)
                else:
                    go(src, dst, ss.at[p, h], sem, to)

    xb, rx = ref.xb, ref.rx
    deal(x_in, xb, lambda h: frames[h], ref.sx, rx)
    cb, rc = ref.cb, ref.rc
    deal(cot_in, cb, lambda h: frames[h] - h * FO, ref.sc, rc)

    half = 3 * HW // 2
    first_half = row_ds(lax.rem(d, 2) * half, half)
    other_half = row_ds((1 - lax.rem(d, 2)) * half, half)
    go_if(
        kap == t, wqkv.at[first_half], wqkv.at[first_half], ref.sq.at[0], rq.at[1],
        mirror,
    )

    share = 2 * lax.rem(d, 2) + kap
    other_dp = 2 * (1 - lax.rem(d, 2)) + kap
    other_core = 2 * lax.rem(d, 2) + 1 - kap
    other_both = 2 * (1 - lax.rem(d, 2)) + 1 - kap
    wide = ("w_out", "w_up", "w_down")
    full = {n: getattr(ref, n + "_full") for n in wide + ("bias",)}
    rw, sw, lw = ref.rw, ref.sw, ref.lw
    own_copies = {}
    for n, name in enumerate(wide + ("bias",)):
        own_copies[name] = pltpu.make_async_copy(getattr(ref, name), full[name].at[t], lw.at[n])
        own_copies[name].start()

    def weight_part(name, s, which):
        quarter = getattr(ref, name).shape[0] // 4
        return full[name].at[s, row_ds(which * quarter, quarter)]

    for n, name in enumerate(wide):
        quarter = getattr(ref, name).shape[0] // 4
        src = getattr(ref, name).at[row_ds(share * quarter, quarter)]
        go(src, weight_part(name, t, share), sw.at[n, 0], rw.at[n, 0], mirror)
    go(ref.bias, full["bias"].at[t], sw.at[3, 0], rw.at[3, 0], mirror)

    def weights_second(name):
        n = wide.index(name)
        part = weight_part(name, 1 - t, share)
        arrived(part, rw.at[n, 0])
        go(part, part, sw.at[n, 1], rw.at[n, 1], beside)
        go(part, part, sw.at[n, 2], rw.at[n, 2], mate)

    def weights_third(name):
        n = wide.index(name)
        part = weight_part(name, 1 - t, other_dp)
        arrived(part, rw.at[n, 1])
        go(part, part, sw.at[n, 3], rw.at[n, 3], mate)

    def weights_ready(name):
        n = wide.index(name)
        arrived(weight_part(name, 1 - t, other_core), rw.at[n, 2])
        arrived(weight_part(name, 1 - t, other_both), rw.at[n, 3])

    RB = 2 * tok
    nb, qa, ka, va = ref.nb, ref.q, ref.k, ref.v
    live = ref.live[clip]
    for load in vec_loads:
        load.wait()

    def project(start):
        rows = row_ds(start, RB, 64)
        xhat, _ = norm_parts(xb[rows, :].astype(F32))
        normed = (xhat * vec[0][...] + vec[1][...]).astype(BF)
        nb[rows, :] = normed
        packed = dot(normed, wqkv[...], NT)
        side = lax.broadcasted_iota(jnp.int32, (RB, GW), 1)
        frame = (start + lax.broadcasted_iota(jnp.int32, (RB, GW), 0)) // PATCH
        for n in range(G * HG):
            g, h = n // HG, n % HG
            mine = side // head_dim == h
            other = side - (1 - h) * head_dim
            lo = g * GW
            query = packed[:, lo : lo + GW].astype(BF).astype(F32) * scale
            key = packed[:, HW + lo : HW + lo + GW]
            value = packed[:, 2 * HW + lo : 2 * HW + lo + GW]
            hidden = (other < L // PATCH) & ((frame > other) | (frame >= live))
            qa[n, rows, :] = jnp.where(mine, query, jnp.where(frame == other, 1.0, 0.0)).astype(BF)
            ka[n, rows, :] = jnp.where(mine, key, jnp.where(hidden, -1e30, 0.0)).astype(BF)
            va[n, rows, :] = jnp.where(mine, value, 1.0).astype(BF)

    @pl.when(kap != t)
    def _():
        arrived(wqkv.at[first_half], rq.at[1])

    go_if(
        kap != t, wqkv.at[first_half], wqkv.at[first_half], ref.sq.at[1], rq.at[2], beside
    )
    weights_second("w_out")
    def first_row(p, core):
        far = 2 * lax.rem(z + Z - p, Z)
        return (far * (1 - core) + (2 * N - 2 - far) * core) * tok

    for p in hops:
        for n in range(2):
            row = first_row(p, kap) + n * tok
            part = xb.at[row_ds(row, tok)]
            arrived(part, rx.at[row // tok])
            go(part, part, ref.fx.at[p, n], rx.at[row // tok], mate)
        if p == 0:

            @pl.when(kap != t)
            def _():
                arrived(wqkv.at[other_half], rq.at[2])

        if p != hops[-1]:
            project(first_row(p, kap))
    for p in hops:
        if p == hops[-1]:
            project(first_row(p, kap))
        for n in range(2):
            row = first_row(p, 1 - kap) + n * tok
            arrived(xb.at[row_ds(row, tok)], rx.at[row // tok])
        project(first_row(p, 1 - kap))

    probs, mo, mr = ref.probs, ref.mo, ref.mr
    rm, sm = ref.rm, ref.sm
    NQ = L // QB
    lane = lax.broadcasted_iota(jnp.int32, (QB, GW), 1)

    def pick(first, second):
        return jnp.where(lane < head_dim, first, second)

    def hand_over(qb, g):
        row = qb * QB
        s = row // R
        off = row - s * R
        lanes = pl.ds(g * GW, GW)
        src = mo.at[pl.ds(row, QB), lanes]
        dst = mr.at[kap, pl.ds(off, QB), lanes]

        @pl.when(kap == s)
        def _():
            mr[kap, pl.ds(off, QB), lanes] = mo[pl.ds(row, QB), lanes]

        go_if(kap != s, src, dst, sm.at[qb, g], rm.at[off // QB, g], mate)

    def attend_block(qb, g):
        K = (qb + 1) * QB
        rows, keys = pl.ds(qb * QB, QB), pl.ds(0, K)
        outs, sums = [], []
        for n in range(g * HG, (g + 1) * HG):
            scores = dot(qa[n, rows, :], ka[n, keys, :], NT)
            top = jnp.max(scores, axis=-1, keepdims=True)
            weights = jnp.exp(scores - top).astype(BF)
            probs[n, rows, keys] = weights
            both = dot(weights, va[n, keys, :])
            outs.append(both)
            sums.append(pltpu.roll(both, head_dim, 1))
        inverse = 1.0 / pick(*sums)
        lanes = pl.ds(g * GW, GW)
        ref.inv[rows, lanes] = inverse
        mo[rows, lanes] = (pick(*outs) * inverse).astype(BF)

    pumps = {
        (0, 0): functools.partial(weights_second, "w_up"),
        (2, 0): functools.partial(weights_second, "w_down"),
        (2, 1): functools.partial(weights_third, "w_out"),
    }
    for qb in range(NQ):
        for g in range(G):
            attend_block(qb, g)
            hand_over(qb, g)
            if (qb, g) in pumps:
                pumps[qb, g]()

    wof, wuf, wdf, bf_ = full["w_out"], full["w_up"], full["w_down"], full["bias"]
    second, act, gpre = ref.second, ref.act, ref.gpre
    mlow, gmid, gst, gx = ref.mlow, ref.gmid, ref.gst, ref.gx
    ob, out_ref, ig_ref = ref.ob, ref.out, ref.ig
    mid, bsum, sv = ref.mid, ref.bsum, ref.sv
    mlp_sum, sec_sum = ref.mlp_sum, ref.sec_sum
    RC = min(256, R)
    FT = 2 * FFh // len(cfg.order)
    c0 = 0.7978845608028654

    def middle_rows(c):
        rows = pl.ds(c * RC, RC)
        attn = dot(mr[0, rows, :], wof[0])
        for s in range(1, T):
            attn = attn + dot(mr[s, rows, :], wof[s])
        middle = xb[row_ds(kap * R + c * RC, RC, 64), :].astype(F32) + attn
        mid[rows, :] = middle
        xhat, _ = norm_parts(middle)
        second[rows, :] = (xhat * vec[2][...] + vec[3][...]).astype(BF)

    def feed_forward(s, c, tiles, first):
        rows = pl.ds(c * RC, RC)
        sec = second[rows, :]
        cot = cb[rows, :]
        for j in tiles:
            cols = pl.ds(j * FT, FT)
            pre = dot(sec, wuf[s, :, cols]) + bf_[s, 0:1, cols]
            gact = dot(cot, wdf[s, cols, :], NT)
            sq = pre * pre
            th = jnp.tanh(c0 * pre * (1.0 + 0.044715 * sq))
            half = 0.5 * (1.0 + th)
            a = (pre * half).astype(BF)
            slope = half + 0.5 * pre * (1.0 - th * th) * (c0 * (1.0 + 0.134145 * sq))
            gp = (gact * slope).astype(BF)
            act[s, rows, cols] = a
            gpre[s, rows, cols] = gp
            sums = jnp.sum(gp.astype(F32), axis=0, keepdims=True)
            bsum[s, 0:1, cols] = sums if c == 0 else bsum[s, 0:1, cols] + sums
            up = dot(a, wdf[s, cols, :])
            back = dot(gp, wuf[s, :, cols], NT)
            if first and j == 0:
                mlp_sum[rows, :] = up
                sec_sum[rows, :] = back
            else:
                mlp_sum[rows, :] = mlp_sum[rows, :] + up
                sec_sum[rows, :] = sec_sum[rows, :] + back

    def finish_rows(c):
        rows = pl.ds(c * RC, RC)
        middle = mid[rows, :]
        xhat, rstd = norm_parts(middle)
        ob[rows, :] = (middle + mlp_sum[rows, :]).astype(BF)
        gsec = sec_sum[rows, :]
        gain_sum = jnp.sum(gsec * xhat, axis=0, keepdims=True)
        shift_sum = jnp.sum(gsec, axis=0, keepdims=True)
        if c > 0:
            gain_sum = gain_sum + sv[0, 2:3, 0:D]
            shift_sum = shift_sum + sv[0, 3:4, 0:D]
        sv[0, 2:3, 0:D] = gain_sum
        sv[0, 3:4, 0:D] = shift_sum
        gm = cb[rows, :].astype(F32) + norm_back(gsec, vec[2][...], xhat, rstd)
        gmid[rows, :] = gm
        low = gm.astype(BF)
        mlow[rows, :] = low
        for s in range(T):
            gst[s, rows, :] = dot(low, wof[s], NT).astype(BF)

    def give_back(buf, dst_ref, ss, rs, k):
        j = 2 * lax.rem(z + hops[k // 2], Z) + k % 2
        f = j * (1 - kap) + (2 * N - 1 - j) * kap
        src = buf.at[row_ds((f - kap * FO) * tok, tok)]
        dst, sem = dst_ref.at[clip, kap], rs.at[clip, kap]

        @pl.when(j == i)
        def _():
            pltpu.make_async_copy(src, dst, sem).start()

        go_if(j != i, src, dst, ss.at[k], sem, {"ctx": j})

    def pass_on(dst_ref, fs, rs, p):
        for h in (0, 1):
            cc = 2 * lax.rem(z + Z - hops[p], Z) + t
            part = dst_ref.at[cc, h]
            arrived(part, rs.at[cc, h])
            go(part, part, fs.at[p, h], rs.at[cc, h], mirror)

    def take_rest(dst_ref, rs):
        for p in range(Z):
            for h in (0, 1):
                cc = 2 * p + 1 - t
                arrived(dst_ref.at[cc, h], rs.at[cc, h])

    reduces = {}
    for name, levels in cfg.plans.items():
        bufs = [getattr(ref, name + "_buf" + str(n), None) for n in range(len(levels))]
        reduces[name] = Reduce(
            levels, getattr(ref, name + "_acc"), getattr(ref, name + "_fin"), bufs,
            getattr(ref, name + "_ss"), getattr(ref, name + "_rs"), place,
        )
        to, sem = getattr(ref, name + "_sum"), ref.end.at[len(reduces) - 1]
        reduces[name].result = pltpu.make_async_copy(reduces[name].fin, to, sem)

    def grad_wide(name, s):
        cols = pl.ds(int(name[-1]) * FT, FT)
        if name[0] == "d":
            getattr(ref, name + "_acc")[s] = dot(act[s, :, cols], cb[...], TN).astype(BF)
        else:
            getattr(ref, name + "_acc")[s] = dot(second[...], gpre[s, :, cols], TN).astype(BF)

    rsv = ref.rsv
    everyone = [("ctx", b) for b in bits_of(N)] + [("dp", b) for b in bits_of(DP)]
    everyone += [("tensor", b) for b in bits_of(T)]
    vec_copy = []

    def vec_step():
        n = len(vec_copy)
        if n > 0:
            vec_copy[-1].wait()
            sv[n] = sv[n - 1] + rsv[n - 1]
        if n < len(everyone):
            axis, bit = everyone[n]
            copy = remote(
                sv.at[n], rsv.at[n], ref.sv_ss.at[n], ref.sv_rs.at[n],
                {axis: flip(place[axis], bit)},
            )
            copy.start()
            vec_copy.append(copy)
        else:
            small_results()

    vec_out = []

    def small_results():
        last = sv[len(everyone)]
        part = D // T
        gains = last[0:4, 0:part]
        bias = last[4:5, 0:FFh]
        for s in range(1, T):
            gains = jnp.where(t == s, last[0:4, s * part : (s + 1) * part], gains)
            bias = jnp.where(t == s, last[4 + s : 5 + s, 0:FFh], bias)
        for n, to in enumerate((ref.grad_ga, ref.grad_sa, ref.grad_gm, ref.grad_sm)):
            ref.gain_sums[n] = gains[n : n + 1, :]
            vec_out.append(pltpu.make_async_copy(ref.gain_sums.at[n], to, ref.vo.at[n]))
        ref.bias_sums[...] = bias
        vec_out.append(pltpu.make_async_copy(ref.bias_sums, ref.bias_out, ref.vo.at[4]))
        for copy in vec_out:
            copy.start()

    out_done, ig_done = [], []
    script = list(cfg.script)

    def run_script():
        while script:
            item = script.pop(0)
            if item == MARK:
                return
            if item == VECTORS:
                vec_step()
            elif item == OUTPUT:
                pass_on(out_ref, ref.fo, ref.ro, len(out_done))
                out_done.append(item)
            elif item == INPUT_GRAD:
                pass_on(ig_ref, ref.fi, ref.ri, len(ig_done))
                ig_done.append(item)
            else:
                reduces[CHUNKS[item]].tick()

    for name in wide + ("bias",):
        own_copies[name].wait()
    arrived(full["bias"].at[1 - t], rw.at[3, 0])
    weights_ready("w_out")
    for k in range(FO):
        arrived(cb.at[pl.ds(k * tok, tok)], rc.at[k])
    for c in range(R // RC):
        for g in range(G):
            rows, lanes = pl.ds(c * RC, RC), pl.ds(g * GW, GW)
            arrived(mr.at[1 - kap, rows, lanes], rm.at[c, g])
        middle_rows(c)
        feed_forward(t, c, range(FFh // FT), True)
        weights_third("w_up" if c == 0 else "w_down")
    for name in cfg.order:
        if name[-1] == "0":
            grad_wide(name, t)
    weights_ready("w_up")
    weights_ready("w_down")
    for j in range(FFh // FT):
        for c in range(R // RC):
            feed_forward(1 - t, c, (j,), False)
        run_script()
        for name in cfg.order:
            if name[-1] == str(j):
                if j > 0:
                    grad_wide(name, t)
                grad_wide(name, 1 - t)
                reduces[name].tick()
    sv[0, 4:5, 0:FFh] = bsum[0, 0:1, :]
    sv[0, 5:6, 0:FFh] = bsum[1, 0:1, :]
    sg, rg = ref.sg, ref.rg
    for c in range(R // RC):
        finish_rows(c)
        rows = pl.ds(c * RC, RC)
        home = row_ds(kap * R + c * RC, RC, 64)
        gx[home, :] = gst[kap, rows, :]
        go(gst.at[1 - kap, rows], gx.at[home], sg.at[c], rg.at[c], mate)
    for k in range(FO):
        give_back(ob, out_ref, ref.so, ref.ro, k)

    for s in range(T):
        ref.out_acc[s] = dot(mr[s], mlow[...], TN).astype(BF)
    reduces["out"].tick()
    run_script()
    for c in range(R // RC):
        arrived(gx.at[row_ds((1 - kap) * R + c * RC, RC, 64)], rg.at[c])

    dk, dv, gpb = ref.dk, ref.dv, ref.gpb

    def attend_back_block(g, qb):
        K = (qb + 1) * QB
        rows = pl.ds(qb * QB, QB)
        keys = pl.ds(0, K)
        lanes = pl.ds(g * GW, GW)
        grad = gx[rows, lanes].astype(F32) * ref.inv[rows, lanes]
        prod = grad * mo[rows, lanes].astype(F32)
        outs = []
        for n in range(g * HG, (g + 1) * HG):
            h = n - g * HG
            mine = lane // head_dim == h
            other = lane - (1 - h) * head_dim
            delta = jnp.sum(jnp.where(mine, prod, 0.0), axis=-1, keepdims=True)
            high = delta.astype(BF).astype(F32)
            rest = jnp.where(other == 0, -high, jnp.where(other == 1, high - delta, 0.0))
            grads = jnp.where(mine, grad, rest).astype(BF)
            prob = probs[n, rows, keys]
            gs = (prob.astype(F32) * dot(grads, va[n, keys, :], NT)).astype(BF)
            outs.append(dot(gs, ka[n, keys, :]))
            dk_part = dot(gs, qa[n, rows, :], TN)
            dv_part = dot(prob, grads, TN)
            if qb == NQ - 1:
                dk[h, keys, :] = dk_part
                dv[h, keys, :] = dv_part
            else:
                dk[h, keys, :] = dk[h, keys, :] + dk_part
                dv[h, keys, :] = dv[h, keys, :] + dv_part
        gpb[rows, lanes] = (pick(*outs) * scale).astype(BF)

    def key_parts(g):
        first = lax.broadcasted_iota(jnp.int32, (L, GW), 1) < head_dim
        for b, acc in ((1, dk), (2, dv)):
            gpb[:, pl.ds(b * HW + g * GW, GW)] = jnp.where(first, acc[0], acc[1]).astype(BF)

    for g in range(G):
        for qb in reversed(range(NQ)):
            attend_back_block(g, qb)
            if qb == 0:
                key_parts(g)
                for b in range(3):
                    getattr(ref, "qkv" + str(g) + "_acc")[kap, pl.ds(b * GW, GW), :] = dot(
                        gpb[:, pl.ds(b * HW + g * GW, GW)], nb[...], TN
                    ).astype(BF)
                reduces["qkv" + str(g)].tick()
            run_script()

    gns, gnr = ref.gns, ref.gnr
    gns[...] = dot(gpb[row_ds((1 - kap) * R, R, 64), :], wqkv[...]).astype(BF)
    go(gns, gnr, ref.sn.at[0], ref.rn.at[0], mate)
    run_script()
    own = dot(gpb[row_ds(kap * R, R, 64), :], wqkv[...])
    arrived(gnr, ref.rn.at[0])
    own = own + gnr[...].astype(F32)
    xhat, rstd = norm_parts(xb[row_ds(kap * R, R, 64), :].astype(F32))
    sv[0, 0:1, 0:D] = jnp.sum(own * xhat, axis=0, keepdims=True)
    sv[0, 1:2, 0:D] = jnp.sum(own, axis=0, keepdims=True)
    igb = ref.igb
    igb[...] = (gmid[...] + norm_back(own, vec[0][...], xhat, rstd)).astype(BF)
    for k in range(FO):
        give_back(igb, ig_ref, ref.si, ref.ri, k)
    vec_step()
    run_script()
    take_rest(out_ref, ref.ro)
    take_rest(ig_ref, ref.ri)
    for chunk in reduces.values():
        chunk.result.wait()
    for copy in vec_out:
        copy.wait()
    for done in sends:
        done()


def finish_kernel(sizes, *refs):
    D, HW, FFh, GW, G, head_dim, tiles = sizes
    count = 8 + 2 * tiles + G
    out, ig, ga, sa, gm, sm, bias, wo, *wide = refs[:count]
    outs = refs[count : count + 11]
    (
        b_out, b_ig, b_wo, b_down, b_up, b_qkv, f_qkv, f_wo, f_up, f_down, b_vec, b_bias, sem,
    ) = refs[count + 11 :]
    downs, ups, qkvs = wide[:tiles], wide[tiles : 2 * tiles], wide[2 * tiles :]
    moves = []

    def move(src, dst):
        copy = pltpu.make_async_copy(src, dst, sem.at[len(moves)])
        copy.start()
        moves.append(copy)
        return copy

    reads = [move(src, b_down.at[n]) for n, src in enumerate(downs)]
    reads += [move(src, b_up.at[n]) for n, src in enumerate(ups)]
    reads += [move(wo, b_wo)] + [move(src, b_qkv.at[g]) for g, src in enumerate(qkvs)]
    vectors = ((ga, b_vec.at[0], 2), (sa, b_vec.at[1], 3), (gm, b_vec.at[2], 6))
    vectors += ((sm, b_vec.at[3], 7), (bias, b_bias, 9))
    small = len(reads)
    reads += [move(src, mid) for src, mid, _ in vectors]
    reads += [move(out, b_out), move(ig, b_ig)]
    part = FFh // tiles
    for n in range(tiles):
        reads[n].wait()
        at = pl.ds(n * part, part)
        f_down[at, :] = b_down[n].astype(F32)
        move(f_down.at[at], outs[10].at[at])
    for n in range(tiles):
        reads[tiles + n].wait()
        at = pl.ds(n * part, part)
        f_up[:, at] = b_up[n].astype(F32)
        move(f_up.at[:, at], outs[8].at[:, at])
    reads[2 * tiles].wait()
    f_wo[...] = b_wo[...].astype(F32)
    move(f_wo, outs[5])
    for n, src, dst in ((-2, b_out, 0), (-1, b_ig, 1)):
        reads[n].wait()
        move(src, outs[dst])
    for n, (_, mid, dst) in enumerate(vectors):
        reads[small + n].wait()
        move(mid, outs[dst])
    pair = GW // head_dim
    for g in range(G):
        reads[2 * tiles + 1 + g].wait()
        for h in range(pair):
            for b in range(3):
                f_qkv[g * pair + h, pl.ds(b * head_dim, head_dim), :] = b_qkv[
                    g, pl.ds(b * GW + h * head_dim, head_dim), :
                ].astype(F32)
        at = pl.ds(g * pair, pair)
        move(f_qkv.at[at], outs[4].at[at])
    for copy in moves[len(reads) :]:
        copy.wait()


def finish(got, layout, qkv_shape, sizes, T):
    D, HW, FFh, GW, G, head_dim, tiles = sizes
    hbm = pl.BlockSpec(memory_space=pl.ANY)
    S, V = jax.ShapeDtypeStruct, pltpu.VMEM
    small = S((1, D // T), F32)
    by_head = (qkv_shape[1], qkv_shape[2], qkv_shape[0])
    results = pl.pallas_call(
        functools.partial(finish_kernel, sizes),
        out_shape=[
            S(got.out.shape, BF), S(got.ig.shape, BF), small, small, S(by_head, F32),
            S((HW, D), F32), small, small, S((D, FFh), F32), S((1, FFh), F32), S((FFh, D), F32),
        ],
        in_specs=[hbm] * (8 + 2 * tiles + G),
        out_specs=[hbm] * 11,
        scratch_shapes=[
            V(got.out.shape, BF), V(got.ig.shape, BF), V((HW, D), BF),
            V((tiles, FFh // tiles, D), BF), V((tiles, D, FFh // tiles), BF),
            V((G, 3 * GW, D), BF), V(by_head, F32), V((HW, D), F32), V((D, FFh), F32),
            V((FFh, D), F32), V((4, 1, D // T), F32), V((1, FFh), F32),
            pltpu.SemaphoreType.DMA((18 + 4 * tiles + 2 * G,)),
        ],
        compiler_params=pltpu.CompilerParams(vmem_limit_bytes=60 * 2**20),
    )(
        got.out, got.ig, got.grad_ga, got.grad_sa, got.grad_gm, got.grad_sm, got.bias_out,
        got.out_sum, *[getattr(got, n + "_sum") for n in CHUNKS if n != "out"],
    )
    out, ig, ga, sa, qkv, wo, gm, sm, up, bias, down = results
    return (
        out.reshape(layout), ig.reshape(layout), ga[0], sa[0], qkv.transpose(2, 0, 1), wo, gm[0],
        sm[0], up, bias[0], down,
    )


def body(
    sizes,
    inputs,
    cotangent,
    live_frames,
    gain_attn,
    shift_attn,
    w_qkv,
    w_out,
    gain_mlp,
    shift_mlp,
    w_up,
    up_bias,
    w_down,
):
    N, T, DP = sizes["ctx"], sizes["tensor"], sizes["dp"]
    C, _, _, tok, D = inputs.shape
    heads, head_dim = w_qkv.shape[1], w_qkv.shape[2] // 3
    HW = heads * head_dim
    GW = min(128, HW)
    FFh = w_up.shape[1]
    L = 2 * N * tok
    by_chip = T == 2 and HW == 256 and head_dim == 64 and N == 8 and tok == PATCH and N % 2 == 0 and C == N and DP == 2 and FFh == 2 * D
    S_ = 2 if by_chip else T
    R = L // S_
    cfg = SimpleNamespace(
        N=N, T=T, DP=DP, L=L, R=R, FO=2 * N // S_, tok=tok, D=D, HW=HW, GW=GW, G=HW // GW,
        FFh=FFh, QB=256, head_dim=head_dim,
    )
    G = cfg.G
    core, rest = [("ctx", 1)], [("ctx", b) for b in bits_of(N)[1:]]
    over_dp = [("dp", b) for b in bits_of(DP)]
    over_t = [("tensor", b) for b in reversed(bits_of(T))]
    if by_chip:
        steps = {
            "x": over_dp, "y": over_t, "z": rest[:1], "Z": rest[1:-1] + [rest[-1] + ("f",)],
            "R": rest[1:], "X": [over_dp[-1] + ("f",)],
        }
        cfg.plans = plans = {}
        cfg.script, cfg.order = SCRIPT, ORDER
        leads, widths, tiles = {}, {}, len(ORDER) // 2
        for name, order in ORDERS.items():
            begin = [("ctx", 1, "p")] if name[0] == "q" else core
            if name[0] == "d":
                leads[name], widths[name] = (T, FFh // tiles), D
            elif name[0] == "u":
                leads[name], widths[name] = (T, D), FFh // tiles
            elif name[0] == "o":
                leads[name], widths[name] = (T, HW), D
            else:
                leads[name], widths[name] = (T, 3 * GW), D
            plans[name] = plan_levels(*leads[name], begin + sum((steps[c] for c in order), []))
    else:
        cfg.plans = plans = {
            "down": plan_levels(T, FFh, core + over_dp + over_t + rest),
            "up": plan_levels(T, D, core + over_t + over_dp + rest),
            "out": plan_levels(T, HW, core + over_t + over_dp + rest),
            "qkv": plan_levels(1, D, core + over_dp + rest),
        }
        leads = {"down": (T, FFh), "up": (T, D), "out": (T, HW), "qkv": (1, D)}
        widths = {"down": D, "up": FFh, "out": D, "qkv": 3 * HW}

    x = inputs.reshape(C, 2, tok, D)
    cot = cotangent.reshape(C, 2, tok, D)
    wq = w_qkv.transpose(1, 2, 0)
    if not by_chip:
        wq = w_qkv.reshape(D, heads, 3, head_dim).transpose(0, 2, 1, 3).reshape(D, 3 * HW)

    vm = pl.BlockSpec(memory_space=pltpu.VMEM)
    hbm = pl.BlockSpec(memory_space=pl.ANY)
    near = hbm if by_chip else vm
    ins = dict(
        x=(x, hbm),
        cot=(cot, hbm),
        live=(live_frames, pl.BlockSpec(memory_space=pltpu.SMEM)),
        gain_attn=(gain_attn.reshape(1, D), near),
        shift_attn=(shift_attn.reshape(1, D), near),
        gain_mlp=(gain_mlp.reshape(1, D), near),
        shift_mlp=(shift_mlp.reshape(1, D), near),
        w_qkv=(wq, hbm if by_chip else vm),
        w_out=(w_out, hbm),
        w_up=(w_up, hbm),
        w_down=(w_down, hbm),
        bias=(up_bias.reshape(1, FFh), near),
    )
    S = jax.ShapeDtypeStruct
    outs = dict(out=S((C, 2, tok, D), BF), ig=S((C, 2, tok, D), BF))
    if by_chip:
        for name in plans:
            outs[name + "_sum"] = S((leads[name][1], widths[name]), BF)
    else:
        outs.update(
            down_fin=S((FFh, D), BF), up_fin=S((D, FFh), BF), out_fin=S((HW, D), BF),
            qkv_fin=S((D, 3 * HW), BF),
        )
    vector = S((1, D // T), F32)
    outs.update(
        grad_ga=vector, grad_sa=vector, grad_gm=vector, grad_sm=vector, bias_out=S((1, FFh), F32)
    )
    W = max(D, FFh)
    SR = -(-(4 + T) // 8) * 8
    n_all = len(bits_of(N)) + len(bits_of(DP)) + len(bits_of(T))
    RC = min(256, R)
    piece = min(cfg.QB, R)
    FO = cfg.FO
    dma = pltpu.SemaphoreType.DMA
    V = pltpu.VMEM
    scratch = dict(
        xb=V((L, D), BF), rx=dma((2 * N,)),
        cb=V((R, D), BF), rc=dma((FO,)),
        w_out_full=V((T, HW, D), BF), w_up_full=V((T, D, FFh), BF),
        w_down_full=V((T, FFh, D), BF), bias_full=V((T, 1, FFh), F32), lw=dma((4,)),
        nb=V((L, D), BF),
        probs=V((heads, L, L), BF), mo=V((L, HW), BF), mr=V((S_, R, HW), BF),
        second=V((R, D), BF), act=V((T, R, FFh), BF), gpre=V((T, R, FFh), BF),
        mlow=V((R, D), BF), gmid=V((R, D), F32), gst=V((T, R, HW), BF), gx=V((L, HW), BF),
        ob=V((R, D), BF), so=dma((FO,)), ro=dma((N, 2)),
        igb=V((R, D), BF), si=dma((FO,)), ri=dma((N, 2)),
        sv=V((n_all + 1, SR, W), F32), rsv=V((n_all, SR, W), F32),
        sv_ss=dma((n_all,)), sv_rs=dma((n_all,)),
        gpb=V((L, 3 * HW), BF),
    )
    if by_chip:
        scratch.update(
            q=V((heads, L, GW), BF), k=V((heads, L, GW), BF), v=V((heads, L, GW), BF),
            inv=V((L, HW), F32), dk=V((2, L, GW), F32), dv=V((2, L, GW), F32),
            sx=dma((N // 2, 2)), fx=dma((N // 2, 2)), sc=dma((N // 2, 2)),
            wq=V((3 * HW, D), BF), rq=dma((3,)), bq=dma((3 * heads,)), sq=dma((2,)),
            rw=dma((4, 4)), sw=dma((4, 4)), rm=dma((R // 256, G)), sm=dma((L // 256, G)),
            mid=V((R, D), F32), bsum=V((T, 8, FFh), F32),
            mlp_sum=V((R, D), F32), sec_sum=V((R, D), F32),
            sg=dma((R // RC,)), rg=dma((R // RC,)),
            fo=dma((N // 2, 2)), fi=dma((N // 2, 2)),
            gns=V((R, D), BF), gnr=V((R, D), BF), sn=dma((1,)), rn=dma((1,)), end=dma((len(plans),)),
            vecs=V((4, 1, D), F32), vl=dma((4,)), gain_sums=V((4, 1, D // T), F32),
            bias_sums=V((1, FFh), F32), vo=dma((5,)),
        )
    else:
        scratch.update(
            q=V((G, L, GW), BF), k=V((G, L, GW), BF), v=V((G, L, GW), BF),
            dk=V((L, GW), F32), dv=V((L, GW), F32),
            sx=dma((N, 2)), fx=dma((T, FO)), sc=dma((N, 2)), rw=dma((4, 4, T)), sw=dma((4, 4, T)),
            rm=dma((T, R // piece, G)), sm=dma((L // piece, G)),
            sg=dma((T, R // RC)), rg=dma((T, R // RC)), fo=dma((T, N, 2)), fi=dma((T, N, 2)),
            mlp_sum=V((RC, D), F32), sec_sum=V((RC, D), F32),
            gns=V((max(T - 1, 1), R, D), BF), gnr=V((max(T - 1, 1), R, D), BF),
            sn=dma((T,)), rn=dma((T,)),
        )
    for name, levels in plans.items():
        scratch[name + "_acc"] = V(leads[name] + (widths[name],), BF)
        if by_chip:
            scratch[name + "_fin"] = V((leads[name][1], widths[name]), BF)
        scratch[name + "_ss"] = dma((2 * len(levels),))
        scratch[name + "_rs"] = dma((2 * len(levels),))
        for n, (_, _, kind, lead, rows) in enumerate(levels):
            if kind == "p":
                continue
            scratch[name + "_buf" + str(n)] = V((lead, rows, widths[name]), BF)
    names = list(ins) + list(outs) + list(scratch)
    results = pl.pallas_call(
        functools.partial(chip_kernel if by_chip else spread_kernel, cfg, names),
        out_shape=list(outs.values()),
        in_specs=[s for _, s in ins.values()],
        out_specs=[hbm if by_chip else vm] * len(outs),
        scratch_shapes=list(scratch.values()),
        compiler_params=pltpu.CompilerParams(
            collective_id=0, has_side_effects=True, vmem_limit_bytes=60 * 2**20
        ),
    )(*[a for a, _ in ins.values()])
    got = SimpleNamespace(**dict(zip(outs, results)))
    if by_chip:
        return finish(got, inputs.shape, w_qkv.shape, (D, HW, FFh, GW, G, head_dim, tiles), T)
    grad_qkv = got.qkv_fin.reshape(D, 3, heads, head_dim).transpose(0, 2, 1, 3)
    return (
        got.out.reshape(inputs.shape),
        got.ig.reshape(inputs.shape),
        got.grad_ga[0],
        got.grad_sa[0],
        grad_qkv.reshape(w_qkv.shape).astype(F32),
        got.out_fin.astype(F32),
        got.grad_gm[0],
        got.grad_sm[0],
        got.up_fin.astype(F32),
        got.bias_out[0],
        got.down_fin.astype(F32),
    )


def solution(mesh):
    return jax.shard_map(
        functools.partial(body, dict(mesh.shape)),
        mesh=mesh,
        in_specs=(
            P("dp", None, "ctx", None, None),
            P("dp", None, "ctx", None, None),
            P("dp"),
            P(),
            P(),
            P(None, "tensor", None),
            P("tensor", None),
            P(),
            P(),
            P(None, "tensor"),
            P("tensor"),
            P("tensor", None),
        ),
        out_specs=(
            P("dp", None, "ctx", None, None),
            P("dp", None, "ctx", None, None),
            P("tensor"),
            P("tensor"),
            P(None, "tensor", None),
            P("tensor", None),
            P("tensor"),
            P("tensor"),
            P(None, "tensor"),
            P("tensor"),
            P("tensor", None),
        ),
        check_vma=False,
    )
```

```python
import functools
from types import SimpleNamespace

import jax
import jax.numpy as jnp
from jax import lax
from jax.experimental import pallas as pl
from jax.experimental.pallas import tpu as pltpu
from jax.sharding import PartitionSpec as P

PATCH = 64
EPSILON = 1e-05
MESH = pl.DeviceIdType.MESH
BF = jnp.bfloat16
F32 = jnp.float32

NN = (((1,), (0,)), ((), ()))
NT = (((1,), (1,)), ((), ()))
TN = (((0,), (0,)), ((), ()))


def dot(a, b, dims=NN):
    return lax.dot_general(a, b, dims, preferred_element_type=F32)


def bits_of(size):
    found, bit = [], 1
    while bit < size:
        found.append(bit)
        bit *= 2
    return found


def flip(index, bit):
    return index + bit - 2 * bit * ((index // bit) % 2)


def bit_of(index, bit):
    return (index // bit) % 2


def row_ds(start, size, unit=16):
    return pl.ds(pl.multiple_of(start, unit), size)


def remote(src, dst, send_sem, recv_sem, where):
    return pltpu.make_async_remote_copy(
        src_ref=src,
        dst_ref=dst,
        send_sem=send_sem,
        recv_sem=recv_sem,
        device_id=where,
        device_id_type=MESH,
    )


def arrived(dst, sem):
    pltpu.make_async_copy(dst, dst, sem).wait()


def norm_parts(values):
    mean = jnp.mean(values, axis=-1, keepdims=True)
    centered = values - mean
    var = jnp.mean(centered * centered, axis=-1, keepdims=True)
    rstd = lax.rsqrt(var + EPSILON)
    return centered * rstd, rstd


def norm_back(grad, gain, xhat, rstd):
    scaled = grad * gain
    first = jnp.mean(scaled, axis=-1, keepdims=True)
    second = jnp.mean(scaled * xhat, axis=-1, keepdims=True)
    return rstd * (scaled - first - xhat * second)


def plan_levels(lead, rows, order):
    levels = []
    for axis, bit, *forced in order:
        if forced:
            kind = forced[0]
            rows = rows // 2 if kind == "p" else rows
        elif axis == "tensor":
            lead //= 2
            kind = "t"
        elif rows % 32 == 0:
            rows //= 2
            kind = "r"
        else:
            kind = "f"
        levels.append((axis, bit, kind, lead, rows))
    return levels


ORDERS = {
    "down0": "zxyZ",
    "down1": "yxzZ",
    "up0": "yzxZ",
    "up1": "xyzZ",
    "out": "yxzZ",
    "qkv0": "yxzZ",
    "qkv1": "yxzZ",
}
CHUNKS = tuple(ORDERS)
VECTORS, OUTPUT, INPUT_GRAD, MARK = range(7, 11)
ORDER = tuple(CHUNKS[n] for n in (0, 2, 1, 3))
SCRIPT = (
    10, 0, 10, 2, 3, 1, 10, 10, 10, 10, 10, 10, 10, 10, 10, 2, 5, 6, 10, 1, 3, 5, 4, 1, 2, 9, 6,
    5, 2, 0, 9, 3, 5, 7, 1, 4, 6, 3, 0, 4, 5, 0, 9, 9, 2, 1, 4, 6, 8, 5, 3, 8, 1, 7, 0, 4, 2, 8,
    5, 3, 6, 4, 1, 8, 7, 0, 6, 7, 5, 2, 4, 1, 3, 0, 6, 4, 3, 2, 0, 7, 6,
)


class Reduce:
    def __init__(self, levels, acc, fin, bufs, ss, rs, place):
        self.levels, self.acc, self.fin = levels, acc, fin
        self.bufs, self.ss, self.rs, self.place = bufs, ss, rs, place
        self.lead, self.rows = acc.shape[0], acc.shape[1]
        self.toff, self.roff = 0, 0
        self.marks = []
        self.copy = self.result = None
        self.steps = []
        count = len(levels)
        for n in range(count):
            self.steps.append(functools.partial(self.step, n))
        self.steps.append(self.turn)

    def send(self, n):
        axis, bit, kind, lead, rows = self.levels[n]
        mine = bit_of(self.place[axis], bit)
        self.marks.append((self.toff, self.roff, self.lead, self.rows))
        toff, roff = self.toff, self.roff
        dst = self.bufs[n]
        if kind == "p":
            toff = mine
            roff = self.roff + (1 - mine) * rows
            self.roff = self.roff + mine * rows
            dst = self.acc.at[pl.ds(toff, 1), row_ds(roff, rows)]
            self.copy = remote(
                dst, dst, self.ss.at[n], self.rs.at[n], {axis: flip(self.place[axis], bit)}
            )
            self.lead, self.rows = lead, rows
            self.copy.start()
            return
        if kind == "t":
            toff = self.toff + (1 - mine) * lead
            self.toff = self.toff + mine * lead
        elif kind == "r":
            roff = self.roff + (1 - mine) * rows
            self.roff = self.roff + mine * rows
        self.lead, self.rows = lead, rows
        self.copy = remote(
            self.acc.at[pl.ds(toff, lead), row_ds(roff, rows)],
            dst,
            self.ss.at[n],
            self.rs.at[n],
            {axis: flip(self.place[axis], bit)},
        )
        self.copy.start()

    def absorb(self, n):
        self.copy.wait()
        if self.levels[n][2] == "p":
            return
        buf = self.bufs[n]
        part = 32 if self.rows % 32 == 0 else 16
        for a in range(self.lead):

            def add(b, _):
                off = pl.multiple_of(b * part, 16)
                at = row_ds(self.roff + off, part)
                old = self.acc[self.toff + a, at, :].astype(F32)
                new = buf[a, pl.ds(off, part), :].astype(F32)
                self.acc[self.toff + a, at, :] = (old + new).astype(BF)
                return 0

            lax.fori_loop(0, self.rows // part, add, 0)

    def step(self, n):
        if n > 0:
            self.absorb(n - 1)
        self.send(n)

    def turn(self):
        count = len(self.levels)
        self.absorb(count - 1)
        at = row_ds(self.roff, self.rows)
        self.fin[at, :] = self.acc[self.toff, at, :]
        back = [n for n in reversed(range(count)) if self.levels[n][2] in "pr"]
        for k, n in enumerate(back):
            if k == 0:
                self.gather(n, True)
            else:
                self.steps.append(functools.partial(self.gather, n, False))
        self.steps.append(self.close)

    def gather(self, n, first):
        if not first:
            self.copy.wait()
        axis, bit, kind, lead, rows = self.levels[n]
        part = self.fin.at[row_ds(self.roff, rows)]
        count = len(self.levels)
        self.copy = remote(
            part,
            part,
            self.ss.at[count + n],
            self.rs.at[count + n],
            {axis: flip(self.place[axis], bit)},
        )
        self.copy.start()
        self.roff = self.marks[n][1]

    def close(self):
        self.copy.wait()
        if self.result is not None:
            self.result.start()

    def tick(self):
        if self.steps:
            self.steps.pop(0)()
            return True
        return False

    def drain(self):
        while self.tick():
            pass


def spread_kernel(cfg, names, *refs):
    ref = SimpleNamespace(**dict(zip(names, refs)))
    N, T, DP = cfg.N, cfg.T, cfg.DP
    L, R, FO, tok = cfg.L, cfg.R, cfg.FO, cfg.tok
    D, HW, GW, G, FFh, QB = cfg.D, cfg.HW, cfg.GW, cfg.G, cfg.FFh, cfg.QB
    head_dim = cfg.head_dim
    HG = GW // head_dim
    scale = head_dim ** (-0.5)
    d = lax.axis_index("dp")
    i = lax.axis_index("ctx")
    t = lax.axis_index("tensor")
    place = {"dp": d, "ctx": i, "tensor": t}
    x_in, cot_in = ref.x, ref.cot
    sends = []

    bar = pltpu.get_barrier_semaphore()
    peers = [{"ctx": lax.rem(i + p, N)} for p in range(1, N)]
    peers += [{"tensor": lax.rem(t + p, T)} for p in range(1, T)]
    peers += [{"dp": flip(d, b)} for b in bits_of(DP)]
    for peer in peers:
        pl.semaphore_signal(bar, inc=1, device_id=peer, device_id_type=MESH)
    pl.semaphore_wait(bar, len(peers))

    frames = (i, 2 * N - 1 - i)

    def owns(h):
        return frames[h] // FO == t

    xb, rx, sx, fx = ref.xb, ref.rx, ref.sx, ref.fx
    for p in range(N):
        c = lax.rem(i + p, N)
        for h in (0, 1):
            to = xb.at[row_ds(frames[h] * tok, tok)]

            @pl.when(owns(h))
            def _(p=p, c=c, h=h, to=to):
                if p == 0:
                    pltpu.make_async_copy(x_in.at[c, h], to, rx.at[frames[h]]).start()
                else:
                    remote(
                        x_in.at[c, h], to, sx.at[p, h], rx.at[frames[h]], {"ctx": c}
                    ).start()

            if p > 0:

                def done(p=p, c=c, h=h, to=to):
                    @pl.when(owns(h))
                    def _():
                        remote(
                            x_in.at[c, h], to, sx.at[p, h], rx.at[frames[h]], {"ctx": c}
                        ).wait_send()

                sends.append(done)

    def near(k):
        return t * FO + lax.rem(i + k, FO)

    for k in range(FO):
        f = near(k)
        part = xb.at[row_ds(f * tok, tok)]
        arrived(part, rx.at[f])
        for p in range(1, T):
            copy = remote(
                part, part, fx.at[p, k], rx.at[f], {"tensor": lax.rem(t + p, T)}
            )
            copy.start()
            sends.append(copy.wait_send)

    cb, rc, sc = ref.cb, ref.rc, ref.sc
    for p in range(N):
        c = lax.rem(i + p, N)
        for h in (0, 1):
            slot = lax.rem(frames[h], FO)
            to = cb.at[row_ds(slot * tok, tok)]

            @pl.when(owns(h))
            def _(p=p, c=c, h=h, to=to, slot=slot):
                if p == 0:
                    pltpu.make_async_copy(cot_in.at[c, h], to, rc.at[slot]).start()
                else:
                    remote(cot_in.at[c, h], to, sc.at[p, h], rc.at[slot], {"ctx": c}).start()

            if p > 0:

                def done(p=p, c=c, h=h, to=to, slot=slot):
                    @pl.when(owns(h))
                    def _():
                        remote(
                            cot_in.at[c, h], to, sc.at[p, h], rc.at[slot], {"ctx": c}
                        ).wait_send()

                sends.append(done)

    share = 2 * lax.rem(d, 2) + lax.rem(i, 2)
    wide = ("w_out", "w_up", "w_down")
    full = {n: getattr(ref, n + "_full") for n in wide + ("bias",)}
    rw, sw, lw = ref.rw, ref.sw, ref.lw
    own_copies = []
    for n, name in enumerate(wide + ("bias",)):
        copy = pltpu.make_async_copy(getattr(ref, name), full[name].at[t], lw.at[n])
        copy.start()
        own_copies.append(copy)
    for p in range(1, T):
        to = {"tensor": lax.rem(t + p, T)}
        copy = remote(ref.bias, full["bias"].at[t], sw.at[3, 0, p], rw.at[3, 0, t], to)
        copy.start()
        sends.append(copy.wait_send)
    for n, name in enumerate(wide):
        quarter = getattr(ref, name).shape[0] // 4
        at = row_ds(share * quarter, quarter)
        for p in range(1, T):
            to = {"tensor": lax.rem(t + p, T)}
            copy = remote(
                getattr(ref, name).at[at], full[name].at[t, at], sw.at[n, 0, p], rw.at[n, 0, t], to
            )
            copy.start()
            sends.append(copy.wait_send)

    other_dp = 2 * (1 - lax.rem(d, 2)) + lax.rem(i, 2)
    other_core = 2 * lax.rem(d, 2) + 1 - lax.rem(i, 2)
    other_both = 2 * (1 - lax.rem(d, 2)) + 1 - lax.rem(i, 2)

    def weight_part(name, s, which):
        quarter = getattr(ref, name).shape[0] // 4
        return full[name].at[s, row_ds(which * quarter, quarter)]

    def weights_second(n, name):
        for p in range(1, T):
            s = lax.rem(t + p, T)
            part = weight_part(name, s, share)
            arrived(part, rw.at[n, 0, s])
            for stage, to in ((1, {"dp": flip(d, 1)}), (2, {"ctx": flip(i, 1)})):
                copy = remote(part, part, sw.at[n, stage, p], rw.at[n, stage, s], to)
                copy.start()
                sends.append(copy.wait_send)

    def weights_third(n, name):
        for p in range(1, T):
            s = lax.rem(t + p, T)
            part = weight_part(name, s, other_dp)
            arrived(part, rw.at[n, 1, s])
            copy = remote(
                part, part, sw.at[n, 3, p], rw.at[n, 3, s], {"ctx": flip(i, 1)}
            )
            copy.start()
            sends.append(copy.wait_send)

    def weights_ready(n, name):
        own_copies[n].wait()
        for p in range(1, T):
            s = lax.rem(t + p, T)
            if name == "bias":
                arrived(full[name].at[s], rw.at[n, 0, s])
            else:
                arrived(weight_part(name, s, other_core), rw.at[n, 2, s])
                arrived(weight_part(name, s, other_both), rw.at[n, 3, s])

    RB = min(256, R)
    nb, qb_, kb_, vb_ = ref.nb, ref.q, ref.k, ref.v
    vec = (ref.gain_attn, ref.shift_attn, ref.gain_mlp, ref.shift_mlp)
    wqkv = ref.w_qkv

    def project(start):
        rows = row_ds(start, RB, 64)
        xhat, _ = norm_parts(xb[rows, :].astype(F32))
        normed = (xhat * vec[0][...] + vec[1][...]).astype(BF)
        nb[rows, :] = normed
        packed = dot(normed, wqkv[...])
        for g in range(G):
            lo = g * GW
            qb_[g, rows, :] = (packed[:, lo : lo + GW].astype(BF).astype(F32) * scale).astype(BF)
            kb_[g, rows, :] = packed[:, HW + lo : HW + lo + GW].astype(BF)
            vb_[g, rows, :] = packed[:, 2 * HW + lo : 2 * HW + lo + GW].astype(BF)

    for k in range(R // RB):
        project(t * R + k * RB)
    for p in range(1, T):
        s = lax.rem(t + p, T)
        for k in range(FO):
            f = s * FO + k
            arrived(xb.at[row_ds(f * tok, tok)], rx.at[f])
        for k in range(R // RB):
            project(s * R + k * RB)

    for n, name in enumerate(wide):
        weights_second(n, name)

    live = ref.live[i]
    probs, mo, mr = ref.probs, ref.mo, ref.mr
    rm, sm = ref.rm, ref.sm
    piece = min(QB, R)
    NQ = L // QB
    lane = lax.broadcasted_iota(jnp.int32, (QB, GW), 1) // head_dim

    def pick(parts):
        out = parts[0]
        for a in range(1, HG):
            out = jnp.where(lane == a, parts[a], out)
        return out

    def only(values, a):
        if HG == 1:
            return values
        return jnp.where(lane == a, values, jnp.zeros_like(values))

    def hand_over(qb, g):
        for b in range(QB // piece):
            row = qb * QB + b * piece
            s = row // R
            slot = (row - s * R) // piece
            src = mo.at[pl.ds(row, piece), pl.ds(g * GW, GW)]
            dst = mr.at[t, pl.ds(row - s * R, piece), pl.ds(g * GW, GW)]
            index = row // piece

            @pl.when(s == t)
            def _():
                mr[t, pl.ds(row - s * R, piece), pl.ds(g * GW, GW)] = mo[
                    pl.ds(row, piece), pl.ds(g * GW, GW)
                ]

            @pl.when(s != t)
            def _():
                remote(src, dst, sm.at[index, g], rm.at[t, slot, g], {"tensor": s}).start()

            def done(s=s, src=src, dst=dst, index=index, slot=slot):
                @pl.when(s != t)
                def _():
                    remote(
                        src, dst, sm.at[index, g], rm.at[t, slot, g], {"tensor": s}
                    ).wait_send()

            sends.append(done)

    pumps = [functools.partial(weights_third, n, name) for n, name in enumerate(wide)]
    def mask_shift(qb):
        K = (qb + 1) * QB
        row_frame = (qb * QB + lax.broadcasted_iota(jnp.int32, (QB, K), 0)) // PATCH
        col_frame = lax.broadcasted_iota(jnp.int32, (QB, K), 1) // PATCH
        allowed = (col_frame <= row_frame) & (col_frame < live)
        return jnp.where(allowed, 0.0, -1e30)

    def attend_block(qb, g, shift):
        K = (qb + 1) * QB
        rows = pl.ds(qb * QB, QB)
        qv = qb_[g, rows, :]
        kv = kb_[g, pl.ds(0, K), :]
        vv = vb_[g, pl.ds(0, K), :]
        outs = []
        for a in range(HG):
            scores = dot(only(qv, a), kv, NT) + shift
            top = jnp.max(scores, axis=-1, keepdims=True)
            weights = jnp.exp(scores - top)
            total = jnp.sum(weights, axis=-1, keepdims=True)
            prob = (weights * (1.0 / total)).astype(BF)
            probs[g * HG + a, rows, pl.ds(0, K)] = prob
            outs.append(dot(prob, vv))
        mo[rows, pl.ds(g * GW, GW)] = pick(outs).astype(BF)

    for qb in reversed(range(NQ)):
        shift = mask_shift(qb)
        for g in range(G):
            attend_block(qb, g, shift)
            hand_over(qb, g)
        if pumps:
            pumps.pop(0)()
    while pumps:
        pumps.pop(0)()

    for n, name in enumerate(wide + ("bias",)):
        weights_ready(n, name)
    for p in range(1, T):
        s = lax.rem(t + p, T)
        for slot in range(R // piece):
            for g in range(G):
                arrived(
                    mr.at[s, pl.ds(slot * piece, piece), pl.ds(g * GW, GW)], rm.at[s, slot, g]
                )
    for k in range(FO):
        arrived(cb.at[pl.ds(k * tok, tok)], rc.at[k])

    wof, wuf, wdf, bf_ = full["w_out"], full["w_up"], full["w_down"], full["bias"]
    second, act, gpre = ref.second, ref.act, ref.gpre
    mlow, gmid, gst, gx = ref.mlow, ref.gmid, ref.gst, ref.gx
    ob, out_ref, ig_ref = ref.ob, ref.out, ref.ig
    sv = ref.sv
    mlp_sum, sec_sum = ref.mlp_sum, ref.sec_sum
    RC = min(256, R)
    FT = min(512, FFh)
    c0 = 0.7978845608028654
    sv[0] = jnp.zeros_like(sv[0])

    def frame_home(k):
        f = t * FO + k
        high = f // N
        j = f * (1 - high) + (2 * N - 1 - f) * high
        return j, high

    def give_back(buf, dst_ref, ss, rs, k):
        j, h = frame_home(k)
        src = buf.at[pl.ds(k * tok, tok)]

        @pl.when(j == i)
        def _():
            pltpu.make_async_copy(src, dst_ref.at[i, h], rs.at[i, h]).start()

        @pl.when(j != i)
        def _():
            remote(src, dst_ref.at[i, h], ss.at[k], rs.at[i, h], {"ctx": j}).start()

        def done():
            @pl.when(j != i)
            def _():
                remote(src, dst_ref.at[i, h], ss.at[k], rs.at[i, h], {"ctx": j}).wait_send()

        sends.append(done)

    def pass_on(dst_ref, fs, rs):
        for p in range(N):
            c = lax.rem(i + p, N)
            for h in (0, 1):
                part = dst_ref.at[c, h]

                @pl.when(owns(h))
                def _(p=p, c=c, h=h, part=part):
                    arrived(part, rs.at[c, h])
                    for q in range(1, T):
                        remote(
                            part, part, fs.at[q, p, h], rs.at[c, h], {"tensor": lax.rem(t + q, T)}
                        ).start()

                def done(p=p, c=c, h=h, part=part):
                    @pl.when(owns(h))
                    def _():
                        for q in range(1, T):
                            remote(
                                part,
                                part,
                                fs.at[q, p, h],
                                rs.at[c, h],
                                {"tensor": lax.rem(t + q, T)},
                            ).wait_send()

                sends.append(done)

    def take_rest(dst_ref, rs):
        for c in range(N):
            for h in (0, 1):

                @pl.when(frames[h] // FO != t)
                def _(c=c, h=h):
                    arrived(dst_ref.at[c, h], rs.at[c, h])

    sg, rg = ref.sg, ref.rg
    def feed_forward(rc_index):
        rows = pl.ds(rc_index * RC, RC)
        attn = dot(mr[0, rows, :], wof[0])
        for s in range(1, T):
            attn = attn + dot(mr[s, rows, :], wof[s])
        middle = xb[row_ds(t * R + rc_index * RC, RC, 64), :].astype(F32) + attn
        xhat, rstd = norm_parts(middle)
        sec = (xhat * vec[2][...] + vec[3][...]).astype(BF)
        second[rows, :] = sec
        cot = cb[rows, :]
        for s in range(T):
            for j in range(FFh // FT):
                cols = pl.ds(j * FT, FT)
                pre = dot(sec, wuf[s, :, cols]) + bf_[s, 0:1, cols]
                gact = dot(cot, wdf[s, cols, :], NT)
                sq = pre * pre
                th = jnp.tanh(c0 * pre * (1.0 + 0.044715 * sq))
                half = 0.5 * (1.0 + th)
                a = (pre * half).astype(BF)
                slope = half + 0.5 * pre * (1.0 - th * th) * (c0 * (1.0 + 0.134145 * sq))
                gp = (gact * slope).astype(BF)
                act[s, rows, cols] = a
                gpre[s, rows, cols] = gp
                sv[0, 4 + s : 5 + s, cols] = sv[0, 4 + s : 5 + s, cols] + jnp.sum(
                    gp.astype(F32), axis=0, keepdims=True
                )
                up = dot(a, wdf[s, cols, :])
                back = dot(gp, wuf[s, :, cols], NT)
                if s == 0 and j == 0:
                    mlp_sum[...] = up
                    sec_sum[...] = back
                else:
                    mlp_sum[...] = mlp_sum[...] + up
                    sec_sum[...] = sec_sum[...] + back
        ob[rows, :] = (middle + mlp_sum[...]).astype(BF)
        gsec = sec_sum[...]
        sv[0, 2:3, 0:D] = sv[0, 2:3, 0:D] + jnp.sum(gsec * xhat, axis=0, keepdims=True)
        sv[0, 3:4, 0:D] = sv[0, 3:4, 0:D] + jnp.sum(gsec, axis=0, keepdims=True)
        gm = cot.astype(F32) + norm_back(gsec, vec[2][...], xhat, rstd)
        gmid[rows, :] = gm
        low = gm.astype(BF)
        mlow[rows, :] = low
        for s in range(T):
            gst[s, rows, :] = dot(low, wof[s], NT).astype(BF)

    for rc_index in range(R // RC):
        rows = pl.ds(rc_index * RC, RC)
        feed_forward(rc_index)
        for s in range(T):
            src = gst.at[s, rows]
            dst = gx.at[row_ds(t * R + rc_index * RC, RC, 64)]

            @pl.when(s == t)
            def _():
                gx[row_ds(t * R + rc_index * RC, RC, 64), :] = gst[s, rows, :]

            @pl.when(s != t)
            def _():
                remote(
                    src, dst, sg.at[s, rc_index], rg.at[t, rc_index], {"tensor": s}
                ).start()

            def done(s=s, src=src, dst=dst, rc_index=rc_index):
                @pl.when(s != t)
                def _():
                    remote(
                        src, dst, sg.at[s, rc_index], rg.at[t, rc_index], {"tensor": s}
                    ).wait_send()

            sends.append(done)
        for k in range(rc_index * RC // tok, (rc_index + 1) * RC // tok):
            give_back(ob, out_ref, ref.so, ref.ro, k)

    reduces = {}
    for name in cfg.plans:
        levels = cfg.plans[name]
        bufs = [getattr(ref, name + "_buf" + str(n)) for n in range(len(levels))]
        reduces[name] = Reduce(
            levels, getattr(ref, name + "_acc"), getattr(ref, name + "_fin"), bufs, getattr(ref, name + "_ss"),
            getattr(ref, name + "_rs"), place,
        )
    cot = cb[...]
    for s in range(T):
        ref.down_acc[s] = dot(act[s], cot, TN).astype(BF)
    reduces["down"].tick()
    for s in range(T):
        ref.up_acc[s] = dot(second[...], gpre[s], TN).astype(BF)
    reduces["up"].tick()
    for s in range(T):
        ref.out_acc[s] = dot(mr[s], mlow[...], TN).astype(BF)
    reduces["out"].tick()

    for p in range(1, T):
        s = lax.rem(t + p, T)
        for n in range(R // RC):
            arrived(gx.at[row_ds(s * R + n * RC, RC, 64)], rg.at[s, n])

    dk, dv, gpb = ref.dk, ref.dv, ref.gpb

    def attend_back_block(g, qb):
        K = (qb + 1) * QB
        rows = pl.ds(qb * QB, QB)
        keys = pl.ds(0, K)
        lanes = pl.ds(g * GW, GW)
        go = gx[rows, lanes]
        prod = go.astype(F32) * mo[rows, lanes].astype(F32)
        qv = qb_[g, rows, :]
        kv = kb_[g, keys, :]
        vv = vb_[g, keys, :]
        outs = []
        dk_sum = dv_sum = None
        for a in range(HG):
            delta = jnp.sum(only(prod, a), axis=-1, keepdims=True)
            goa = only(go, a)
            prob = probs[g * HG + a, rows, keys]
            gprob = dot(goa, vv, NT)
            gs = (prob.astype(F32) * (gprob - delta)).astype(BF)
            outs.append(dot(gs, kv))
            dk_part = dot(gs, only(qv, a), TN)
            dv_part = dot(prob, goa, TN)
            dk_sum = dk_part if dk_sum is None else dk_sum + dk_part
            dv_sum = dv_part if dv_sum is None else dv_sum + dv_part
        gpb[rows, lanes] = (pick(outs) * scale).astype(BF)
        if qb == NQ - 1:
            dk[keys, :] = dk_sum
            dv[keys, :] = dv_sum
        else:
            dk[keys, :] = dk[keys, :] + dk_sum
            dv[keys, :] = dv[keys, :] + dv_sum

    turns = 0
    for g in range(G):
        for qb in reversed(range(NQ)):
            attend_back_block(g, qb)
            if turns == 1:
                pass_on(out_ref, ref.fo, ref.ro)
            reduces["down"].tick()
            reduces["up"].tick()
            reduces["out"].tick()
            turns += 1
        gpb[:, pl.ds(HW + g * GW, GW)] = dk[...].astype(BF)
        gpb[:, pl.ds(2 * HW + g * GW, GW)] = dv[...].astype(BF)

    gns, gnr = ref.gns, ref.gnr
    for p in range(1, T):
        s = lax.rem(t + p, T)
        gns[p - 1] = dot(gpb[row_ds(s * R, R, 64), :], wqkv[...], NT).astype(BF)
        copy = remote(gns.at[p - 1], gnr.at[p - 1], ref.sn.at[p - 1], ref.rn.at[p - 1], {"tensor": s})
        copy.start()
        sends.append(copy.wait_send)
    ref.qkv_acc[0] = dot(nb[...], gpb[...], TN).astype(BF)
    reduces["qkv"].tick()
    own = dot(gpb[row_ds(t * R, R, 64), :], wqkv[...], NT)
    for p in range(1, T):
        arrived(gnr.at[p - 1], ref.rn.at[p - 1])
        own = own + gnr[p - 1].astype(F32)
    xhat, rstd = norm_parts(xb[row_ds(t * R, R, 64), :].astype(F32))
    sv[0, 0:1, 0:D] = jnp.sum(own * xhat, axis=0, keepdims=True)
    sv[0, 1:2, 0:D] = jnp.sum(own, axis=0, keepdims=True)
    igb = ref.igb
    igb[...] = (gmid[...] + norm_back(own, vec[0][...], xhat, rstd)).astype(BF)
    for k in range(FO):
        give_back(igb, ig_ref, ref.si, ref.ri, k)

    rsv = ref.rsv
    everyone = [(a, b) for a, n in (("ctx", N), ("dp", DP), ("tensor", T)) for b in bits_of(n)]
    for n, (axis, bit) in enumerate(everyone):
        copy = remote(
            sv.at[n], rsv.at[n], ref.sv_ss.at[n], ref.sv_rs.at[n],
            {axis: flip(place[axis], bit)},
        )
        copy.start()
        reduces["qkv"].tick()
        copy.wait()
        sv[n + 1] = sv[n] + rsv[n]
    pass_on(ig_ref, ref.fi, ref.ri)
    last = sv[len(everyone)]
    part = D // T
    gains = last[0:4, 0:part]
    bias = last[4:5, 0:FFh]
    for s in range(1, T):
        gains = jnp.where(t == s, last[0:4, s * part : (s + 1) * part], gains)
        bias = jnp.where(t == s, last[4 + s : 5 + s, 0:FFh], bias)
    for n, got in enumerate((ref.grad_ga, ref.grad_sa, ref.grad_gm, ref.grad_sm)):
        got[...] = gains[n : n + 1, :]
    ref.bias_out[...] = bias

    for name in ("down", "up", "out", "qkv"):
        reduces[name].drain()
    take_rest(out_ref, ref.ro)
    take_rest(ig_ref, ref.ri)
    for done in sends:
        done()


def chip_kernel(cfg, names, *refs):
    ref = SimpleNamespace(**dict(zip(names, refs)))
    N, T, DP = cfg.N, cfg.T, cfg.DP
    L, R, FO, tok = cfg.L, cfg.R, cfg.FO, cfg.tok
    D, HW, GW, G, FFh, QB = cfg.D, cfg.HW, cfg.GW, cfg.G, cfg.FFh, cfg.QB
    head_dim = cfg.head_dim
    Z = N // 2
    HG = GW // head_dim
    scale = head_dim ** (-0.5)
    d = lax.axis_index("dp")
    i = lax.axis_index("ctx")
    t = lax.axis_index("tensor")
    z, kap = i // 2, lax.rem(i, 2)
    clip = 2 * z + t
    mate, mirror, beside = {"ctx": flip(i, 1)}, {"tensor": 1 - t}, {"dp": flip(d, 1)}
    place = {"dp": d, "ctx": i, "tensor": t}
    x_in, cot_in = ref.x, ref.cot
    sends = []

    def go(src, dst, send_sem, recv_sem, where):
        copy = remote(src, dst, send_sem, recv_sem, where)
        copy.start()
        sends.append(copy.wait_send)

    def go_if(cond, *args):
        @pl.when(cond)
        def _():
            remote(*args).start()

        def done():
            @pl.when(cond)
            def _():
                remote(*args).wait_send()

        sends.append(done)

    vec = [ref.vecs.at[n] for n in range(4)]
    vec_loads = []
    for n, src in enumerate((ref.gain_attn, ref.shift_attn, ref.gain_mlp, ref.shift_mlp)):
        vec_loads.append(pltpu.make_async_copy(src, vec[n], ref.vl.at[n]))
        vec_loads[-1].start()

    bar = pltpu.get_barrier_semaphore()
    peers = [{"ctx": lax.rem(i + p, N)} for p in (4, 3, 5, 2, 6, 1, 7)]
    peers += [mirror] + [{"dp": flip(d, b)} for b in bits_of(DP)]
    for peer in peers:
        pl.semaphore_signal(bar, inc=1, device_id=peer, device_id_type=MESH)

    wqkv, rq = ref.wq, ref.rq
    blocks = []
    for n in range(HW // head_dim):
        for b in range(3):
            src = ref.w_qkv.at[n, pl.ds(b * head_dim, head_dim)]
            dst = wqkv.at[pl.ds(b * HW + n * head_dim, head_dim)]
            blocks.append((src, dst, ref.bq.at[3 * n + b]))

    @pl.when(kap == t)
    def _():
        for block in blocks:
            pltpu.make_async_copy(*block).start()
        for block in blocks:
            pltpu.make_async_copy(*block).wait()

    pl.semaphore_wait(bar, len(peers))

    frames = (i, 2 * N - 1 - i)
    hops = [0, Z // 2] + [p for p in range(1, Z) if p != Z // 2]

    def deal(src_ref, dst_ref, spot, ss, rs):
        for p in hops:
            zz = lax.rem(z + p, Z)
            for h in (0, 1):
                src = src_ref.at[2 * zz + t, h]
                dst = dst_ref.at[row_ds(spot(h) * tok, tok)]
                to = {"ctx": 2 * zz + h}
                sem = rs.at[spot(h)]
                if p == 0:

                    @pl.when(kap == h)
                    def _(src=src, dst=dst, sem=sem):
                        pltpu.make_async_copy(src, dst, sem).start()

                    go_if(kap != h, src, dst, ss.at[p, h], sem, to)
                else:
                    go(src, dst, ss.at[p, h], sem, to)

    xb, rx = ref.xb, ref.rx
    deal(x_in, xb, lambda h: frames[h], ref.sx, rx)
    cb, rc = ref.cb, ref.rc
    deal(cot_in, cb, lambda h: frames[h] - h * FO, ref.sc, rc)

    half = 3 * HW // 2
    first_half = row_ds(lax.rem(d, 2) * half, half)
    other_half = row_ds((1 - lax.rem(d, 2)) * half, half)
    go_if(
        kap == t, wqkv.at[first_half], wqkv.at[first_half], ref.sq.at[0], rq.at[1],
        mirror,
    )

    share = 2 * lax.rem(d, 2) + kap
    other_dp = 2 * (1 - lax.rem(d, 2)) + kap
    other_core = 2 * lax.rem(d, 2) + 1 - kap
    other_both = 2 * (1 - lax.rem(d, 2)) + 1 - kap
    wide = ("w_out", "w_up", "w_down")
    full = {n: getattr(ref, n + "_full") for n in wide + ("bias",)}
    rw, sw, lw = ref.rw, ref.sw, ref.lw
    own_copies = {}
    for n, name in enumerate(wide + ("bias",)):
        own_copies[name] = pltpu.make_async_copy(getattr(ref, name), full[name].at[t], lw.at[n])
        own_copies[name].start()

    def weight_part(name, s, which):
        quarter = getattr(ref, name).shape[0] // 4
        return full[name].at[s, row_ds(which * quarter, quarter)]

    for n, name in enumerate(wide):
        quarter = getattr(ref, name).shape[0] // 4
        src = getattr(ref, name).at[row_ds(share * quarter, quarter)]
        go(src, weight_part(name, t, share), sw.at[n, 0], rw.at[n, 0], mirror)
    go(ref.bias, full["bias"].at[t], sw.at[3, 0], rw.at[3, 0], mirror)

    def weights_second(name):
        n = wide.index(name)
        part = weight_part(name, 1 - t, share)
        arrived(part, rw.at[n, 0])
        go(part, part, sw.at[n, 1], rw.at[n, 1], beside)
        go(part, part, sw.at[n, 2], rw.at[n, 2], mate)

    def weights_third(name):
        n = wide.index(name)
        part = weight_part(name, 1 - t, other_dp)
        arrived(part, rw.at[n, 1])
        go(part, part, sw.at[n, 3], rw.at[n, 3], mate)

    def weights_ready(name):
        n = wide.index(name)
        arrived(weight_part(name, 1 - t, other_core), rw.at[n, 2])
        arrived(weight_part(name, 1 - t, other_both), rw.at[n, 3])

    RB = 2 * tok
    nb, qa, ka, va = ref.nb, ref.q, ref.k, ref.v
    live = ref.live[clip]
    for load in vec_loads:
        load.wait()

    def project(start):
        rows = row_ds(start, RB, 64)
        xhat, _ = norm_parts(xb[rows, :].astype(F32))
        normed = (xhat * vec[0][...] + vec[1][...]).astype(BF)
        nb[rows, :] = normed
        packed = dot(normed, wqkv[...], NT)
        side = lax.broadcasted_iota(jnp.int32, (RB, GW), 1)
        frame = (start + lax.broadcasted_iota(jnp.int32, (RB, GW), 0)) // PATCH
        for n in range(G * HG):
            g, h = n // HG, n % HG
            mine = side // head_dim == h
            other = side - (1 - h) * head_dim
            lo = g * GW
            query = packed[:, lo : lo + GW].astype(BF).astype(F32) * scale
            key = packed[:, HW + lo : HW + lo + GW]
            value = packed[:, 2 * HW + lo : 2 * HW + lo + GW]
            hidden = (other < L // PATCH) & ((frame > other) | (frame >= live))
            qa[n, rows, :] = jnp.where(mine, query, jnp.where(frame == other, 1.0, 0.0)).astype(BF)
            ka[n, rows, :] = jnp.where(mine, key, jnp.where(hidden, -1e30, 0.0)).astype(BF)
            va[n, rows, :] = jnp.where(mine, value, 1.0).astype(BF)

    @pl.when(kap != t)
    def _():
        arrived(wqkv.at[first_half], rq.at[1])

    go_if(
        kap != t, wqkv.at[first_half], wqkv.at[first_half], ref.sq.at[1], rq.at[2], beside
    )
    weights_second("w_out")
    def first_row(p, core):
        far = 2 * lax.rem(z + Z - p, Z)
        return (far * (1 - core) + (2 * N - 2 - far) * core) * tok

    for p in hops:
        for n in range(2):
            row = first_row(p, kap) + n * tok
            part = xb.at[row_ds(row, tok)]
            arrived(part, rx.at[row // tok])
            go(part, part, ref.fx.at[p, n], rx.at[row // tok], mate)
        if p == 0:

            @pl.when(kap != t)
            def _():
                arrived(wqkv.at[other_half], rq.at[2])

        if p != hops[-1]:
            project(first_row(p, kap))
    for p in hops:
        if p == hops[-1]:
            project(first_row(p, kap))
        for n in range(2):
            row = first_row(p, 1 - kap) + n * tok
            arrived(xb.at[row_ds(row, tok)], rx.at[row // tok])
        if p == hops[-1]:
            weights_second("w_up")
        project(first_row(p, 1 - kap))

    probs, mo, mr = ref.probs, ref.mo, ref.mr
    rm, sm = ref.rm, ref.sm
    NQ = L // QB
    lane = lax.broadcasted_iota(jnp.int32, (QB, GW), 1)

    def pick(first, second):
        return jnp.where(lane < head_dim, first, second)

    def hand_over(qb, g):
        row = qb * QB
        s = row // R
        off = row - s * R
        lanes = pl.ds(g * GW, GW)
        src = mo.at[pl.ds(row, QB), lanes]
        dst = mr.at[kap, pl.ds(off, QB), lanes]

        @pl.when(kap == s)
        def _():
            mr[kap, pl.ds(off, QB), lanes] = mo[pl.ds(row, QB), lanes]

        go_if(kap != s, src, dst, sm.at[qb, g], rm.at[off // QB, g], mate)

    def attend_block(qb, g):
        K = (qb + 1) * QB
        rows, keys = pl.ds(qb * QB, QB), pl.ds(0, K)
        outs, sums = [], []
        for n in range(g * HG, (g + 1) * HG):
            scores = dot(qa[n, rows, :], ka[n, keys, :], NT)
            top = jnp.max(scores, axis=-1, keepdims=True)
            weights = jnp.exp(scores - top).astype(BF)
            probs[n, rows, keys] = weights
            both = dot(weights, va[n, keys, :])
            outs.append(both)
            sums.append(pltpu.roll(both, head_dim, 1))
        inverse = 1.0 / pick(*sums)
        lanes = pl.ds(g * GW, GW)
        ref.inv[rows, lanes] = inverse
        mo[rows, lanes] = (pick(*outs) * inverse).astype(BF)

    pumps = {
        (1, 1): functools.partial(weights_second, "w_down"),
        (2, 1): functools.partial(weights_third, "w_out"),
    }
    for qb in range(NQ):
        for g in range(G):
            attend_block(qb, g)
            hand_over(qb, g)
            if (qb, g) in pumps:
                pumps[qb, g]()

    wof, wuf, wdf, bf_ = full["w_out"], full["w_up"], full["w_down"], full["bias"]
    second, act, gpre = ref.second, ref.act, ref.gpre
    mlow, gmid, gst, gx = ref.mlow, ref.gmid, ref.gst, ref.gx
    ob, out_ref, ig_ref = ref.ob, ref.out, ref.ig
    mid, bsum, sv = ref.mid, ref.bsum, ref.sv
    mlp_sum, sec_sum = ref.mlp_sum, ref.sec_sum
    RC = min(256, R)
    FT = 2 * FFh // len(cfg.order)
    c0 = 0.7978845608028654

    def middle_rows(c):
        rows = pl.ds(c * RC, RC)
        attn = dot(mr[0, rows, :], wof[0])
        for s in range(1, T):
            attn = attn + dot(mr[s, rows, :], wof[s])
        middle = xb[row_ds(kap * R + c * RC, RC, 64), :].astype(F32) + attn
        mid[rows, :] = middle
        xhat, _ = norm_parts(middle)
        second[rows, :] = (xhat * vec[2][...] + vec[3][...]).astype(BF)

    def feed_forward(s, c, tiles, first):
        rows = pl.ds(c * RC, RC)
        sec = second[rows, :]
        cot = cb[rows, :]
        for j in tiles:
            cols = pl.ds(j * FT, FT)
            pre = dot(sec, wuf[s, :, cols]) + bf_[s, 0:1, cols]
            gact = dot(cot, wdf[s, cols, :], NT)
            sq = pre * pre
            th = jnp.tanh(c0 * pre * (1.0 + 0.044715 * sq))
            half = 0.5 * (1.0 + th)
            a = (pre * half).astype(BF)
            slope = half + 0.5 * pre * (1.0 - th * th) * (c0 * (1.0 + 0.134145 * sq))
            gp = (gact * slope).astype(BF)
            act[s, rows, cols] = a
            gpre[s, rows, cols] = gp
            sums = jnp.sum(gp.astype(F32), axis=0, keepdims=True)
            bsum[s, 0:1, cols] = sums if c == 0 else bsum[s, 0:1, cols] + sums
            up = dot(a, wdf[s, cols, :])
            back = dot(gp, wuf[s, :, cols], NT)
            if first and j == 0:
                mlp_sum[rows, :] = up
                sec_sum[rows, :] = back
            else:
                mlp_sum[rows, :] = mlp_sum[rows, :] + up
                sec_sum[rows, :] = sec_sum[rows, :] + back

    def finish_rows(c):
        rows = pl.ds(c * RC, RC)
        middle = mid[rows, :]
        xhat, rstd = norm_parts(middle)
        ob[rows, :] = (middle + mlp_sum[rows, :]).astype(BF)
        gsec = sec_sum[rows, :]
        gain_sum = jnp.sum(gsec * xhat, axis=0, keepdims=True)
        shift_sum = jnp.sum(gsec, axis=0, keepdims=True)
        if c > 0:
            gain_sum = gain_sum + sv[0, 2:3, 0:D]
            shift_sum = shift_sum + sv[0, 3:4, 0:D]
        sv[0, 2:3, 0:D] = gain_sum
        sv[0, 3:4, 0:D] = shift_sum
        gm = cb[rows, :].astype(F32) + norm_back(gsec, vec[2][...], xhat, rstd)
        gmid[rows, :] = gm
        low = gm.astype(BF)
        mlow[rows, :] = low
        for s in range(T):
            gst[s, rows, :] = dot(low, wof[s], NT).astype(BF)

    def give_back(buf, dst_ref, ss, rs, k):
        j = 2 * lax.rem(z + hops[k // 2], Z) + k % 2
        f = j * (1 - kap) + (2 * N - 1 - j) * kap
        src = buf.at[row_ds((f - kap * FO) * tok, tok)]
        dst, sem = dst_ref.at[clip, kap], rs.at[clip, kap]

        @pl.when(j == i)
        def _():
            pltpu.make_async_copy(src, dst, sem).start()

        go_if(j != i, src, dst, ss.at[k], sem, {"ctx": j})

    def pass_on(dst_ref, fs, rs, p):
        for h in (0, 1):
            cc = 2 * lax.rem(z + Z - hops[p], Z) + t
            part = dst_ref.at[cc, h]
            arrived(part, rs.at[cc, h])
            go(part, part, fs.at[p, h], rs.at[cc, h], mirror)

    def take_rest(dst_ref, rs):
        for p in range(Z):
            for h in (0, 1):
                cc = 2 * p + 1 - t
                arrived(dst_ref.at[cc, h], rs.at[cc, h])

    reduces = {}
    for name, levels in cfg.plans.items():
        bufs = [getattr(ref, name + "_buf" + str(n), None) for n in range(len(levels))]
        reduces[name] = Reduce(
            levels, getattr(ref, name + "_acc"), getattr(ref, name + "_fin"), bufs,
            getattr(ref, name + "_ss"), getattr(ref, name + "_rs"), place,
        )
        to, sem = getattr(ref, name + "_sum"), ref.end.at[len(reduces) - 1]
        reduces[name].result = pltpu.make_async_copy(reduces[name].fin, to, sem)

    def grad_wide(name, s):
        cols = pl.ds(int(name[-1]) * FT, FT)
        if name[0] == "d":
            getattr(ref, name + "_acc")[s] = dot(act[s, :, cols], cb[...], TN).astype(BF)
        else:
            getattr(ref, name + "_acc")[s] = dot(second[...], gpre[s, :, cols], TN).astype(BF)

    rsv = ref.rsv
    everyone = [("ctx", b) for b in bits_of(N)] + [("dp", b) for b in bits_of(DP)]
    everyone += [("tensor", b) for b in bits_of(T)]
    vec_copy = []

    def vec_step():
        n = len(vec_copy)
        if n > 0:
            vec_copy[-1].wait()
            sv[n] = sv[n - 1] + rsv[n - 1]
        if n < len(everyone):
            axis, bit = everyone[n]
            copy = remote(
                sv.at[n], rsv.at[n], ref.sv_ss.at[n], ref.sv_rs.at[n],
                {axis: flip(place[axis], bit)},
            )
            copy.start()
            vec_copy.append(copy)
        else:
            small_results()

    vec_out = []

    def small_results():
        last = sv[len(everyone)]
        part = D // T
        gains = last[0:4, 0:part]
        bias = last[4:5, 0:FFh]
        for s in range(1, T):
            gains = jnp.where(t == s, last[0:4, s * part : (s + 1) * part], gains)
            bias = jnp.where(t == s, last[4 + s : 5 + s, 0:FFh], bias)
        for n, to in enumerate((ref.grad_ga, ref.grad_sa, ref.grad_gm, ref.grad_sm)):
            ref.gain_sums[n] = gains[n : n + 1, :]
            vec_out.append(pltpu.make_async_copy(ref.gain_sums.at[n], to, ref.vo.at[n]))
        ref.bias_sums[...] = bias
        vec_out.append(pltpu.make_async_copy(ref.bias_sums, ref.bias_out, ref.vo.at[4]))
        for copy in vec_out:
            copy.start()

    out_done, ig_done = [], []
    script = list(cfg.script)
    old_sends = []

    def run_script():
        while script:
            for _ in range(min(3, len(old_sends))):
                old_sends.pop(0)()
            item = script.pop(0)
            if item == MARK:
                return
            if item == VECTORS:
                vec_step()
            elif item == OUTPUT:
                pass_on(out_ref, ref.fo, ref.ro, len(out_done))
                out_done.append(item)
            elif item == INPUT_GRAD:
                pass_on(ig_ref, ref.fi, ref.ri, len(ig_done))
                ig_done.append(item)
            else:
                reduces[CHUNKS[item]].tick()

    for name in wide + ("bias",):
        own_copies[name].wait()
    arrived(full["bias"].at[1 - t], rw.at[3, 0])
    weights_ready("w_out")
    for k in range(FO):
        arrived(cb.at[pl.ds(k * tok, tok)], rc.at[k])
    for c in range(R // RC):
        for g in range(G):
            rows, lanes = pl.ds(c * RC, RC), pl.ds(g * GW, GW)
            arrived(mr.at[1 - kap, rows, lanes], rm.at[c, g])
        middle_rows(c)
        feed_forward(t, c, range(FFh // FT), True)
        weights_third("w_up" if c == 0 else "w_down")
    for name in cfg.order:
        if name[-1] == "0":
            grad_wide(name, t)
    weights_ready("w_up")
    weights_ready("w_down")
    for j in range(FFh // FT):
        for c in range(R // RC):
            feed_forward(1 - t, c, (j,), False)
        run_script()
        for name in cfg.order:
            if name[-1] == str(j):
                if j > 0:
                    grad_wide(name, t)
                grad_wide(name, 1 - t)
                reduces[name].tick()
    sv[0, 4:5, 0:FFh] = bsum[0, 0:1, :]
    sv[0, 5:6, 0:FFh] = bsum[1, 0:1, :]
    sg, rg = ref.sg, ref.rg
    for c in range(R // RC):
        finish_rows(c)
        rows = pl.ds(c * RC, RC)
        home = row_ds(kap * R + c * RC, RC, 64)
        gx[home, :] = gst[kap, rows, :]
        go(gst.at[1 - kap, rows], gx.at[home], sg.at[c], rg.at[c], mate)
    for k in range(FO):
        give_back(ob, out_ref, ref.so, ref.ro, k)

    for s in range(T):
        ref.out_acc[s] = dot(mr[s], mlow[...], TN).astype(BF)
    reduces["out"].tick()
    run_script()
    for c in range(R // RC):
        arrived(gx.at[row_ds((1 - kap) * R + c * RC, RC, 64)], rg.at[c])

    dk, dv, gpb = ref.dk, ref.dv, ref.gpb

    def attend_back_block(g, qb):
        K = (qb + 1) * QB
        rows = pl.ds(qb * QB, QB)
        keys = pl.ds(0, K)
        lanes = pl.ds(g * GW, GW)
        grad = gx[rows, lanes].astype(F32) * ref.inv[rows, lanes]
        prod = grad * mo[rows, lanes].astype(F32)
        outs = []
        for n in range(g * HG, (g + 1) * HG):
            h = n - g * HG
            mine = lane // head_dim == h
            other = lane - (1 - h) * head_dim
            delta = jnp.sum(jnp.where(mine, prod, 0.0), axis=-1, keepdims=True)
            high = delta.astype(BF).astype(F32)
            rest = jnp.where(other == 0, -high, jnp.where(other == 1, high - delta, 0.0))
            grads = jnp.where(mine, grad, rest).astype(BF)
            prob = probs[n, rows, keys]
            gs = (prob.astype(F32) * dot(grads, va[n, keys, :], NT)).astype(BF)
            outs.append(dot(gs, ka[n, keys, :]))
            dk_part = dot(gs, qa[n, rows, :], TN)
            dv_part = dot(prob, grads, TN)
            if qb == NQ - 1:
                dk[h, keys, :] = dk_part
                dv[h, keys, :] = dv_part
            else:
                dk[h, keys, :] = dk[h, keys, :] + dk_part
                dv[h, keys, :] = dv[h, keys, :] + dv_part
        gpb[rows, lanes] = (pick(*outs) * scale).astype(BF)

    def key_parts(g):
        first = lax.broadcasted_iota(jnp.int32, (L, GW), 1) < head_dim
        for b, acc in ((1, dk), (2, dv)):
            gpb[:, pl.ds(b * HW + g * GW, GW)] = jnp.where(first, acc[0], acc[1]).astype(BF)

    for g in range(G):
        for qb in reversed(range(NQ)):
            attend_back_block(g, qb)
            if qb == 0:
                key_parts(g)
                for b in range(3):
                    getattr(ref, "qkv" + str(g) + "_acc")[kap, pl.ds(b * GW, GW), :] = dot(
                        gpb[:, pl.ds(b * HW + g * GW, GW)], nb[...], TN
                    ).astype(BF)
                reduces["qkv" + str(g)].tick()
            run_script()

    gns, gnr = ref.gns, ref.gnr
    gns[...] = dot(gpb[row_ds((1 - kap) * R, R, 64), :], wqkv[...]).astype(BF)
    go(gns, gnr, ref.sn.at[0], ref.rn.at[0], mate)
    run_script()
    own = dot(gpb[row_ds(kap * R, R, 64), :], wqkv[...])
    arrived(gnr, ref.rn.at[0])
    own = own + gnr[...].astype(F32)
    xhat, rstd = norm_parts(xb[row_ds(kap * R, R, 64), :].astype(F32))
    sv[0, 0:1, 0:D] = jnp.sum(own * xhat, axis=0, keepdims=True)
    sv[0, 1:2, 0:D] = jnp.sum(own, axis=0, keepdims=True)
    igb = ref.igb
    igb[...] = (gmid[...] + norm_back(own, vec[0][...], xhat, rstd)).astype(BF)
    for k in range(FO):
        give_back(igb, ig_ref, ref.si, ref.ri, k)
    vec_step()
    old_sends += sends[: -FO]
    del sends[: -FO]
    run_script()
    take_rest(out_ref, ref.ro)
    take_rest(ig_ref, ref.ri)
    for chunk in reduces.values():
        chunk.result.wait()
    for copy in vec_out:
        copy.wait()
    for done in old_sends + sends:
        done()


def finish_kernel(sizes, *refs):
    D, HW, FFh, GW, G, head_dim, tiles = sizes
    count = 8 + 2 * tiles + G
    out, ig, ga, sa, gm, sm, bias, wo, *wide = refs[:count]
    outs = refs[count : count + 11]
    (
        b_out, b_ig, b_wo, b_down, b_up, b_qkv, f_qkv, f_wo, f_up, f_down, b_vec, b_bias, sem,
    ) = refs[count + 11 :]
    downs, ups, qkvs = wide[:tiles], wide[tiles : 2 * tiles], wide[2 * tiles :]
    moves = []

    def move(src, dst):
        copy = pltpu.make_async_copy(src, dst, sem.at[len(moves)])
        copy.start()
        moves.append(copy)
        return copy

    ends = [move(out, b_out), move(ig, b_ig)]
    reads = [move(src, b_down.at[n]) for n, src in enumerate(downs)]
    reads += [move(src, b_up.at[n]) for n, src in enumerate(ups)]
    reads += [move(wo, b_wo)] + [move(src, b_qkv.at[g]) for g, src in enumerate(qkvs)]
    vectors = ((ga, b_vec.at[0], 2), (sa, b_vec.at[1], 3), (gm, b_vec.at[2], 6))
    vectors += ((sm, b_vec.at[3], 7), (bias, b_bias, 9))
    small = len(reads)
    reads += [move(src, mid) for src, mid, _ in vectors]
    for copy, src, dst in zip(ends, (b_out, b_ig), outs):
        copy.wait()
        move(src, dst)
    part = FFh // tiles
    for n in range(tiles):
        reads[n].wait()
        at = pl.ds(n * part, part)
        f_down[at, :] = b_down[n].astype(F32)
        move(f_down.at[at], outs[10].at[at])
    for n in range(tiles):
        reads[tiles + n].wait()
        at = pl.ds(n * part, part)
        f_up[:, at] = b_up[n].astype(F32)
    move(f_up, outs[8])
    reads[2 * tiles].wait()
    f_wo[...] = b_wo[...].astype(F32)
    move(f_wo, outs[5])
    for n, (_, mid, dst) in enumerate(vectors):
        reads[small + n].wait()
        move(mid, outs[dst])
    pair = GW // head_dim
    for g in range(G):
        reads[2 * tiles + 1 + g].wait()
        for h in range(pair):
            for b in range(3):
                f_qkv[g * pair + h, pl.ds(b * head_dim, head_dim), :] = b_qkv[
                    g, pl.ds(b * GW + h * head_dim, head_dim), :
                ].astype(F32)
        at = pl.ds(g * pair, pair)
        move(f_qkv.at[at], outs[4].at[at])
    for copy in moves[len(reads) + 2 :]:
        copy.wait()


def finish(got, layout, qkv_shape, sizes, T):
    D, HW, FFh, GW, G, head_dim, tiles = sizes
    hbm = pl.BlockSpec(memory_space=pl.ANY)
    S, V = jax.ShapeDtypeStruct, pltpu.VMEM
    small = S((1, D // T), F32)
    by_head = (qkv_shape[1], qkv_shape[2], qkv_shape[0])
    results = pl.pallas_call(
        functools.partial(finish_kernel, sizes),
        out_shape=[
            S(got.out.shape, BF), S(got.ig.shape, BF), small, small, S(by_head, F32),
            S((HW, D), F32), small, small, S((D, FFh), F32), S((1, FFh), F32), S((FFh, D), F32),
        ],
        in_specs=[hbm] * (8 + 2 * tiles + G),
        out_specs=[hbm] * 11,
        scratch_shapes=[
            V(got.out.shape, BF), V(got.ig.shape, BF), V((HW, D), BF),
            V((tiles, FFh // tiles, D), BF), V((tiles, D, FFh // tiles), BF),
            V((G, 3 * GW, D), BF), V(by_head, F32), V((HW, D), F32), V((D, FFh), F32),
            V((FFh, D), F32), V((4, 1, D // T), F32), V((1, FFh), F32),
            pltpu.SemaphoreType.DMA((18 + 4 * tiles + 2 * G,)),
        ],
        compiler_params=pltpu.CompilerParams(vmem_limit_bytes=60 * 2**20),
    )(
        got.out, got.ig, got.grad_ga, got.grad_sa, got.grad_gm, got.grad_sm, got.bias_out,
        got.out_sum, *[getattr(got, n + "_sum") for n in CHUNKS if n != "out"],
    )
    out, ig, ga, sa, qkv, wo, gm, sm, up, bias, down = results
    return (
        out.reshape(layout), ig.reshape(layout), ga[0], sa[0], qkv.transpose(2, 0, 1), wo, gm[0],
        sm[0], up, bias[0], down,
    )


def body(
    sizes,
    inputs,
    cotangent,
    live_frames,
    gain_attn,
    shift_attn,
    w_qkv,
    w_out,
    gain_mlp,
    shift_mlp,
    w_up,
    up_bias,
    w_down,
):
    N, T, DP = sizes["ctx"], sizes["tensor"], sizes["dp"]
    C, _, _, tok, D = inputs.shape
    heads, head_dim = w_qkv.shape[1], w_qkv.shape[2] // 3
    HW = heads * head_dim
    GW = min(128, HW)
    FFh = w_up.shape[1]
    L = 2 * N * tok
    by_chip = T == 2 and HW == 256 and head_dim == 64 and N == 8 and tok == PATCH and N % 2 == 0 and C == N and DP == 2 and FFh == 2 * D
    S_ = 2 if by_chip else T
    R = L // S_
    cfg = SimpleNamespace(
        N=N, T=T, DP=DP, L=L, R=R, FO=2 * N // S_, tok=tok, D=D, HW=HW, GW=GW, G=HW // GW,
        FFh=FFh, QB=256, head_dim=head_dim,
    )
    G = cfg.G
    core, rest = [("ctx", 1)], [("ctx", b) for b in bits_of(N)[1:]]
    over_dp = [("dp", b) for b in bits_of(DP)]
    over_t = [("tensor", b) for b in reversed(bits_of(T))]
    if by_chip:
        steps = {
            "x": over_dp, "y": over_t, "z": rest[:1], "Z": rest[1:-1] + [rest[-1] + ("f",)],
            "R": rest[1:], "X": [over_dp[-1] + ("f",)],
        }
        cfg.plans = plans = {}
        cfg.script, cfg.order = SCRIPT, ORDER
        leads, widths, tiles = {}, {}, len(ORDER) // 2
        for name, order in ORDERS.items():
            begin = [("ctx", 1, "p")] if name[0] == "q" else core
            if name[0] == "d":
                leads[name], widths[name] = (T, FFh // tiles), D
            elif name[0] == "u":
                leads[name], widths[name] = (T, D), FFh // tiles
            elif name[0] == "o":
                leads[name], widths[name] = (T, HW), D
            else:
                leads[name], widths[name] = (T, 3 * GW), D
            plans[name] = plan_levels(*leads[name], begin + sum((steps[c] for c in order), []))
    else:
        cfg.plans = plans = {
            "down": plan_levels(T, FFh, core + over_dp + over_t + rest),
            "up": plan_levels(T, D, core + over_t + over_dp + rest),
            "out": plan_levels(T, HW, core + over_t + over_dp + rest),
            "qkv": plan_levels(1, D, core + over_dp + rest),
        }
        leads = {"down": (T, FFh), "up": (T, D), "out": (T, HW), "qkv": (1, D)}
        widths = {"down": D, "up": FFh, "out": D, "qkv": 3 * HW}

    x = inputs.reshape(C, 2, tok, D)
    cot = cotangent.reshape(C, 2, tok, D)
    wq = w_qkv.transpose(1, 2, 0)
    if not by_chip:
        wq = w_qkv.reshape(D, heads, 3, head_dim).transpose(0, 2, 1, 3).reshape(D, 3 * HW)

    vm = pl.BlockSpec(memory_space=pltpu.VMEM)
    hbm = pl.BlockSpec(memory_space=pl.ANY)
    near = hbm if by_chip else vm
    ins = dict(
        x=(x, hbm),
        cot=(cot, hbm),
        live=(live_frames, pl.BlockSpec(memory_space=pltpu.SMEM)),
        gain_attn=(gain_attn.reshape(1, D), near),
        shift_attn=(shift_attn.reshape(1, D), near),
        gain_mlp=(gain_mlp.reshape(1, D), near),
        shift_mlp=(shift_mlp.reshape(1, D), near),
        w_qkv=(wq, hbm if by_chip else vm),
        w_out=(w_out, hbm),
        w_up=(w_up, hbm),
        w_down=(w_down, hbm),
        bias=(up_bias.reshape(1, FFh), near),
    )
    S = jax.ShapeDtypeStruct
    outs = dict(out=S((C, 2, tok, D), BF), ig=S((C, 2, tok, D), BF))
    if by_chip:
        for name in plans:
            outs[name + "_sum"] = S((leads[name][1], widths[name]), BF)
    else:
        outs.update(
            down_fin=S((FFh, D), BF), up_fin=S((D, FFh), BF), out_fin=S((HW, D), BF),
            qkv_fin=S((D, 3 * HW), BF),
        )
    vector = S((1, D // T), F32)
    outs.update(
        grad_ga=vector, grad_sa=vector, grad_gm=vector, grad_sm=vector, bias_out=S((1, FFh), F32)
    )
    W = max(D, FFh)
    SR = -(-(4 + T) // 8) * 8
    n_all = len(bits_of(N)) + len(bits_of(DP)) + len(bits_of(T))
    RC = min(256, R)
    piece = min(cfg.QB, R)
    FO = cfg.FO
    dma = pltpu.SemaphoreType.DMA
    V = pltpu.VMEM
    scratch = dict(
        xb=V((L, D), BF), rx=dma((2 * N,)),
        cb=V((R, D), BF), rc=dma((FO,)),
        w_out_full=V((T, HW, D), BF), w_up_full=V((T, D, FFh), BF),
        w_down_full=V((T, FFh, D), BF), bias_full=V((T, 1, FFh), F32), lw=dma((4,)),
        nb=V((L, D), BF),
        probs=V((heads, L, L), BF), mo=V((L, HW), BF), mr=V((S_, R, HW), BF),
        second=V((R, D), BF), act=V((T, R, FFh), BF), gpre=V((T, R, FFh), BF),
        mlow=V((R, D), BF), gmid=V((R, D), F32), gst=V((T, R, HW), BF), gx=V((L, HW), BF),
        ob=V((R, D), BF), so=dma((FO,)), ro=dma((N, 2)),
        igb=V((R, D), BF), si=dma((FO,)), ri=dma((N, 2)),
        sv=V((n_all + 1, SR, W), F32), rsv=V((n_all, SR, W), F32),
        sv_ss=dma((n_all,)), sv_rs=dma((n_all,)),
        gpb=V((L, 3 * HW), BF),
    )
    if by_chip:
        scratch.update(
            q=V((heads, L, GW), BF), k=V((heads, L, GW), BF), v=V((heads, L, GW), BF),
            inv=V((L, HW), F32), dk=V((2, L, GW), F32), dv=V((2, L, GW), F32),
            sx=dma((N // 2, 2)), fx=dma((N // 2, 2)), sc=dma((N // 2, 2)),
            wq=V((3 * HW, D), BF), rq=dma((3,)), bq=dma((3 * heads,)), sq=dma((2,)),
            rw=dma((4, 4)), sw=dma((4, 4)), rm=dma((R // 256, G)), sm=dma((L // 256, G)),
            mid=V((R, D), F32), bsum=V((T, 8, FFh), F32),
            mlp_sum=V((R, D), F32), sec_sum=V((R, D), F32),
            sg=dma((R // RC,)), rg=dma((R // RC,)),
            fo=dma((N // 2, 2)), fi=dma((N // 2, 2)),
            gns=V((R, D), BF), gnr=V((R, D), BF), sn=dma((1,)), rn=dma((1,)), end=dma((len(plans),)),
            vecs=V((4, 1, D), F32), vl=dma((4,)), gain_sums=V((4, 1, D // T), F32),
            bias_sums=V((1, FFh), F32), vo=dma((5,)),
        )
    else:
        scratch.update(
            q=V((G, L, GW), BF), k=V((G, L, GW), BF), v=V((G, L, GW), BF),
            dk=V((L, GW), F32), dv=V((L, GW), F32),
            sx=dma((N, 2)), fx=dma((T, FO)), sc=dma((N, 2)), rw=dma((4, 4, T)), sw=dma((4, 4, T)),
            rm=dma((T, R // piece, G)), sm=dma((L // piece, G)),
            sg=dma((T, R // RC)), rg=dma((T, R // RC)), fo=dma((T, N, 2)), fi=dma((T, N, 2)),
            mlp_sum=V((RC, D), F32), sec_sum=V((RC, D), F32),
            gns=V((max(T - 1, 1), R, D), BF), gnr=V((max(T - 1, 1), R, D), BF),
            sn=dma((T,)), rn=dma((T,)),
        )
    for name, levels in plans.items():
        scratch[name + "_acc"] = V(leads[name] + (widths[name],), BF)
        if by_chip:
            scratch[name + "_fin"] = V((leads[name][1], widths[name]), BF)
        scratch[name + "_ss"] = dma((2 * len(levels),))
        scratch[name + "_rs"] = dma((2 * len(levels),))
        for n, (_, _, kind, lead, rows) in enumerate(levels):
            if kind == "p":
                continue
            scratch[name + "_buf" + str(n)] = V((lead, rows, widths[name]), BF)
    names = list(ins) + list(outs) + list(scratch)
    results = pl.pallas_call(
        functools.partial(chip_kernel if by_chip else spread_kernel, cfg, names),
        out_shape=list(outs.values()),
        in_specs=[s for _, s in ins.values()],
        out_specs=[hbm if by_chip else vm] * len(outs),
        scratch_shapes=list(scratch.values()),
        compiler_params=pltpu.CompilerParams(
            collective_id=0, has_side_effects=True, vmem_limit_bytes=60 * 2**20
        ),
    )(*[a for a, _ in ins.values()])
    got = SimpleNamespace(**dict(zip(outs, results)))
    if by_chip:
        return finish(got, inputs.shape, w_qkv.shape, (D, HW, FFh, GW, G, head_dim, tiles), T)
    grad_qkv = got.qkv_fin.reshape(D, 3, heads, head_dim).transpose(0, 2, 1, 3)
    return (
        got.out.reshape(inputs.shape),
        got.ig.reshape(inputs.shape),
        got.grad_ga[0],
        got.grad_sa[0],
        grad_qkv.reshape(w_qkv.shape).astype(F32),
        got.out_fin.astype(F32),
        got.grad_gm[0],
        got.grad_sm[0],
        got.up_fin.astype(F32),
        got.bias_out[0],
        got.down_fin.astype(F32),
    )


def solution(mesh):
    return jax.shard_map(
        functools.partial(body, dict(mesh.shape)),
        mesh=mesh,
        in_specs=(
            P("dp", None, "ctx", None, None),
            P("dp", None, "ctx", None, None),
            P("dp"),
            P(),
            P(),
            P(None, "tensor", None),
            P("tensor", None),
            P(),
            P(),
            P(None, "tensor"),
            P("tensor"),
            P("tensor", None),
        ),
        out_specs=(
            P("dp", None, "ctx", None, None),
            P("dp", None, "ctx", None, None),
            P("tensor"),
            P("tensor"),
            P(None, "tensor", None),
            P("tensor", None),
            P("tensor"),
            P("tensor"),
            P(None, "tensor"),
            P("tensor"),
            P("tensor", None),
        ),
        check_vma=False,
    )
```

```python
import functools
from types import SimpleNamespace

import jax
import jax.numpy as jnp
from jax import lax
from jax.experimental import pallas as pl
from jax.experimental.pallas import tpu as pltpu
from jax.sharding import PartitionSpec as P

PATCH = 64
EPSILON = 1e-05
MESH = pl.DeviceIdType.MESH
BF = jnp.bfloat16
F32 = jnp.float32

NN = (((1,), (0,)), ((), ()))
NT = (((1,), (1,)), ((), ()))
TN = (((0,), (0,)), ((), ()))


def dot(a, b, dims=NN):
    return lax.dot_general(a, b, dims, preferred_element_type=F32)


def bits_of(size):
    found, bit = [], 1
    while bit < size:
        found.append(bit)
        bit *= 2
    return found


def flip(index, bit):
    return index + bit - 2 * bit * ((index // bit) % 2)


def bit_of(index, bit):
    return (index // bit) % 2


def row_ds(start, size, unit=16):
    return pl.ds(pl.multiple_of(start, unit), size)


def remote(src, dst, send_sem, recv_sem, where):
    return pltpu.make_async_remote_copy(
        src_ref=src,
        dst_ref=dst,
        send_sem=send_sem,
        recv_sem=recv_sem,
        device_id=where,
        device_id_type=MESH,
    )


def arrived(dst, sem):
    pltpu.make_async_copy(dst, dst, sem).wait()


def norm_parts(values):
    mean = jnp.mean(values, axis=-1, keepdims=True)
    centered = values - mean
    var = jnp.mean(centered * centered, axis=-1, keepdims=True)
    rstd = lax.rsqrt(var + EPSILON)
    return centered * rstd, rstd


def norm_back(grad, gain, xhat, rstd):
    scaled = grad * gain
    first = jnp.mean(scaled, axis=-1, keepdims=True)
    second = jnp.mean(scaled * xhat, axis=-1, keepdims=True)
    return rstd * (scaled - first - xhat * second)


def plan_levels(lead, rows, order):
    levels = []
    for axis, bit, *forced in order:
        if forced:
            kind = forced[0]
            rows = rows // 2 if kind == "p" else rows
        elif axis == "tensor":
            lead //= 2
            kind = "t"
        elif rows % 32 == 0:
            rows //= 2
            kind = "r"
        else:
            kind = "f"
        levels.append((axis, bit, kind, lead, rows))
    return levels


ORDERS = {
    "down0": "zxyZ",
    "down1": "yxzZ",
    "up0": "yzxZ",
    "up1": "xyzZ",
    "out": "yxzZ",
    "qkv0": "yxzZ",
    "qkv1": "yxzZ",
}
CHUNKS = tuple(ORDERS)
VECTORS, OUTPUT, INPUT_GRAD, MARK = range(7, 11)
ORDER = tuple(CHUNKS[n] for n in (0, 2, 1, 3))
SCRIPT = (
    10, 0, 10, 2, 3, 1, 10, 10, 10, 10, 10, 10, 10, 10, 10, 2, 5, 6, 10, 1, 3, 5, 4, 1, 2, 9, 6,
    5, 2, 0, 9, 3, 5, 7, 1, 4, 6, 3, 0, 4, 5, 0, 9, 9, 2, 1, 4, 6, 8, 5, 3, 8, 1, 7, 0, 4, 2, 8,
    5, 3, 6, 4, 1, 8, 7, 0, 6, 7, 5, 2, 4, 1, 3, 0, 6, 4, 3, 2, 0, 7, 6,
)


class Reduce:
    def __init__(self, levels, acc, fin, bufs, ss, rs, place):
        self.levels, self.acc, self.fin = levels, acc, fin
        self.bufs, self.ss, self.rs, self.place = bufs, ss, rs, place
        self.lead, self.rows = acc.shape[0], acc.shape[1]
        self.toff, self.roff = 0, 0
        self.marks = []
        self.copy = self.result = None
        self.steps = []
        count = len(levels)
        for n in range(count):
            self.steps.append(functools.partial(self.step, n))
        self.steps.append(self.turn)

    def send(self, n):
        axis, bit, kind, lead, rows = self.levels[n]
        mine = bit_of(self.place[axis], bit)
        self.marks.append((self.toff, self.roff, self.lead, self.rows))
        toff, roff = self.toff, self.roff
        dst = self.bufs[n]
        if kind == "p":
            toff = mine
            roff = self.roff + (1 - mine) * rows
            self.roff = self.roff + mine * rows
            dst = self.acc.at[pl.ds(toff, 1), row_ds(roff, rows)]
            self.copy = remote(
                dst, dst, self.ss.at[n], self.rs.at[n], {axis: flip(self.place[axis], bit)}
            )
            self.lead, self.rows = lead, rows
            self.copy.start()
            return
        if kind == "t":
            toff = self.toff + (1 - mine) * lead
            self.toff = self.toff + mine * lead
        elif kind == "r":
            roff = self.roff + (1 - mine) * rows
            self.roff = self.roff + mine * rows
        self.lead, self.rows = lead, rows
        self.copy = remote(
            self.acc.at[pl.ds(toff, lead), row_ds(roff, rows)],
            dst,
            self.ss.at[n],
            self.rs.at[n],
            {axis: flip(self.place[axis], bit)},
        )
        self.copy.start()

    def absorb(self, n):
        self.copy.wait()
        if self.levels[n][2] == "p":
            return
        buf = self.bufs[n]
        part = 32 if self.rows % 32 == 0 else 16
        for a in range(self.lead):

            def add(b, _):
                off = pl.multiple_of(b * part, 16)
                at = row_ds(self.roff + off, part)
                old = self.acc[self.toff + a, at, :].astype(F32)
                new = buf[a, pl.ds(off, part), :].astype(F32)
                self.acc[self.toff + a, at, :] = (old + new).astype(BF)
                return 0

            lax.fori_loop(0, self.rows // part, add, 0)

    def step(self, n):
        if n > 0:
            self.absorb(n - 1)
        self.send(n)

    def turn(self):
        count = len(self.levels)
        self.absorb(count - 1)
        at = row_ds(self.roff, self.rows)
        self.fin[at, :] = self.acc[self.toff, at, :]
        back = [n for n in reversed(range(count)) if self.levels[n][2] in "pr"]
        for k, n in enumerate(back):
            if k == 0:
                self.gather(n, True)
            else:
                self.steps.append(functools.partial(self.gather, n, False))
        self.steps.append(self.close)

    def gather(self, n, first):
        if not first:
            self.copy.wait()
        axis, bit, kind, lead, rows = self.levels[n]
        part = self.fin.at[row_ds(self.roff, rows)]
        count = len(self.levels)
        self.copy = remote(
            part,
            part,
            self.ss.at[count + n],
            self.rs.at[count + n],
            {axis: flip(self.place[axis], bit)},
        )
        self.copy.start()
        self.roff = self.marks[n][1]

    def close(self):
        self.copy.wait()
        if self.result is not None:
            self.result.start()

    def tick(self):
        if self.steps:
            self.steps.pop(0)()
            return True
        return False

    def drain(self):
        while self.tick():
            pass


def spread_kernel(cfg, names, *refs):
    ref = SimpleNamespace(**dict(zip(names, refs)))
    N, T, DP = cfg.N, cfg.T, cfg.DP
    L, R, FO, tok = cfg.L, cfg.R, cfg.FO, cfg.tok
    D, HW, GW, G, FFh, QB = cfg.D, cfg.HW, cfg.GW, cfg.G, cfg.FFh, cfg.QB
    head_dim = cfg.head_dim
    HG = GW // head_dim
    scale = head_dim ** (-0.5)
    d = lax.axis_index("dp")
    i = lax.axis_index("ctx")
    t = lax.axis_index("tensor")
    place = {"dp": d, "ctx": i, "tensor": t}
    x_in, cot_in = ref.x, ref.cot
    sends = []

    bar = pltpu.get_barrier_semaphore()
    peers = [{"ctx": lax.rem(i + p, N)} for p in range(1, N)]
    peers += [{"tensor": lax.rem(t + p, T)} for p in range(1, T)]
    peers += [{"dp": flip(d, b)} for b in bits_of(DP)]
    for peer in peers:
        pl.semaphore_signal(bar, inc=1, device_id=peer, device_id_type=MESH)
    pl.semaphore_wait(bar, len(peers))

    frames = (i, 2 * N - 1 - i)

    def owns(h):
        return frames[h] // FO == t

    xb, rx, sx, fx = ref.xb, ref.rx, ref.sx, ref.fx
    for p in range(N):
        c = lax.rem(i + p, N)
        for h in (0, 1):
            to = xb.at[row_ds(frames[h] * tok, tok)]

            @pl.when(owns(h))
            def _(p=p, c=c, h=h, to=to):
                if p == 0:
                    pltpu.make_async_copy(x_in.at[c, h], to, rx.at[frames[h]]).start()
                else:
                    remote(
                        x_in.at[c, h], to, sx.at[p, h], rx.at[frames[h]], {"ctx": c}
                    ).start()

            if p > 0:

                def done(p=p, c=c, h=h, to=to):
                    @pl.when(owns(h))
                    def _():
                        remote(
                            x_in.at[c, h], to, sx.at[p, h], rx.at[frames[h]], {"ctx": c}
                        ).wait_send()

                sends.append(done)

    def near(k):
        return t * FO + lax.rem(i + k, FO)

    for k in range(FO):
        f = near(k)
        part = xb.at[row_ds(f * tok, tok)]
        arrived(part, rx.at[f])
        for p in range(1, T):
            copy = remote(
                part, part, fx.at[p, k], rx.at[f], {"tensor": lax.rem(t + p, T)}
            )
            copy.start()
            sends.append(copy.wait_send)

    cb, rc, sc = ref.cb, ref.rc, ref.sc
    for p in range(N):
        c = lax.rem(i + p, N)
        for h in (0, 1):
            slot = lax.rem(frames[h], FO)
            to = cb.at[row_ds(slot * tok, tok)]

            @pl.when(owns(h))
            def _(p=p, c=c, h=h, to=to, slot=slot):
                if p == 0:
                    pltpu.make_async_copy(cot_in.at[c, h], to, rc.at[slot]).start()
                else:
                    remote(cot_in.at[c, h], to, sc.at[p, h], rc.at[slot], {"ctx": c}).start()

            if p > 0:

                def done(p=p, c=c, h=h, to=to, slot=slot):
                    @pl.when(owns(h))
                    def _():
                        remote(
                            cot_in.at[c, h], to, sc.at[p, h], rc.at[slot], {"ctx": c}
                        ).wait_send()

                sends.append(done)

    share = 2 * lax.rem(d, 2) + lax.rem(i, 2)
    wide = ("w_out", "w_up", "w_down")
    full = {n: getattr(ref, n + "_full") for n in wide + ("bias",)}
    rw, sw, lw = ref.rw, ref.sw, ref.lw
    own_copies = []
    for n, name in enumerate(wide + ("bias",)):
        copy = pltpu.make_async_copy(getattr(ref, name), full[name].at[t], lw.at[n])
        copy.start()
        own_copies.append(copy)
    for p in range(1, T):
        to = {"tensor": lax.rem(t + p, T)}
        copy = remote(ref.bias, full["bias"].at[t], sw.at[3, 0, p], rw.at[3, 0, t], to)
        copy.start()
        sends.append(copy.wait_send)
    for n, name in enumerate(wide):
        quarter = getattr(ref, name).shape[0] // 4
        at = row_ds(share * quarter, quarter)
        for p in range(1, T):
            to = {"tensor": lax.rem(t + p, T)}
            copy = remote(
                getattr(ref, name).at[at], full[name].at[t, at], sw.at[n, 0, p], rw.at[n, 0, t], to
            )
            copy.start()
            sends.append(copy.wait_send)

    other_dp = 2 * (1 - lax.rem(d, 2)) + lax.rem(i, 2)
    other_core = 2 * lax.rem(d, 2) + 1 - lax.rem(i, 2)
    other_both = 2 * (1 - lax.rem(d, 2)) + 1 - lax.rem(i, 2)

    def weight_part(name, s, which):
        quarter = getattr(ref, name).shape[0] // 4
        return full[name].at[s, row_ds(which * quarter, quarter)]

    def weights_second(n, name):
        for p in range(1, T):
            s = lax.rem(t + p, T)
            part = weight_part(name, s, share)
            arrived(part, rw.at[n, 0, s])
            for stage, to in ((1, {"dp": flip(d, 1)}), (2, {"ctx": flip(i, 1)})):
                copy = remote(part, part, sw.at[n, stage, p], rw.at[n, stage, s], to)
                copy.start()
                sends.append(copy.wait_send)

    def weights_third(n, name):
        for p in range(1, T):
            s = lax.rem(t + p, T)
            part = weight_part(name, s, other_dp)
            arrived(part, rw.at[n, 1, s])
            copy = remote(
                part, part, sw.at[n, 3, p], rw.at[n, 3, s], {"ctx": flip(i, 1)}
            )
            copy.start()
            sends.append(copy.wait_send)

    def weights_ready(n, name):
        own_copies[n].wait()
        for p in range(1, T):
            s = lax.rem(t + p, T)
            if name == "bias":
                arrived(full[name].at[s], rw.at[n, 0, s])
            else:
                arrived(weight_part(name, s, other_core), rw.at[n, 2, s])
                arrived(weight_part(name, s, other_both), rw.at[n, 3, s])

    RB = min(256, R)
    nb, qb_, kb_, vb_ = ref.nb, ref.q, ref.k, ref.v
    vec = (ref.gain_attn, ref.shift_attn, ref.gain_mlp, ref.shift_mlp)
    wqkv = ref.w_qkv

    def project(start):
        rows = row_ds(start, RB, 64)
        xhat, _ = norm_parts(xb[rows, :].astype(F32))
        normed = (xhat * vec[0][...] + vec[1][...]).astype(BF)
        nb[rows, :] = normed
        packed = dot(normed, wqkv[...])
        for g in range(G):
            lo = g * GW
            qb_[g, rows, :] = (packed[:, lo : lo + GW].astype(BF).astype(F32) * scale).astype(BF)
            kb_[g, rows, :] = packed[:, HW + lo : HW + lo + GW].astype(BF)
            vb_[g, rows, :] = packed[:, 2 * HW + lo : 2 * HW + lo + GW].astype(BF)

    for k in range(R // RB):
        project(t * R + k * RB)
    for p in range(1, T):
        s = lax.rem(t + p, T)
        for k in range(FO):
            f = s * FO + k
            arrived(xb.at[row_ds(f * tok, tok)], rx.at[f])
        for k in range(R // RB):
            project(s * R + k * RB)

    for n, name in enumerate(wide):
        weights_second(n, name)

    live = ref.live[i]
    probs, mo, mr = ref.probs, ref.mo, ref.mr
    rm, sm = ref.rm, ref.sm
    piece = min(QB, R)
    NQ = L // QB
    lane = lax.broadcasted_iota(jnp.int32, (QB, GW), 1) // head_dim

    def pick(parts):
        out = parts[0]
        for a in range(1, HG):
            out = jnp.where(lane == a, parts[a], out)
        return out

    def only(values, a):
        if HG == 1:
            return values
        return jnp.where(lane == a, values, jnp.zeros_like(values))

    def hand_over(qb, g):
        for b in range(QB // piece):
            row = qb * QB + b * piece
            s = row // R
            slot = (row - s * R) // piece
            src = mo.at[pl.ds(row, piece), pl.ds(g * GW, GW)]
            dst = mr.at[t, pl.ds(row - s * R, piece), pl.ds(g * GW, GW)]
            index = row // piece

            @pl.when(s == t)
            def _():
                mr[t, pl.ds(row - s * R, piece), pl.ds(g * GW, GW)] = mo[
                    pl.ds(row, piece), pl.ds(g * GW, GW)
                ]

            @pl.when(s != t)
            def _():
                remote(src, dst, sm.at[index, g], rm.at[t, slot, g], {"tensor": s}).start()

            def done(s=s, src=src, dst=dst, index=index, slot=slot):
                @pl.when(s != t)
                def _():
                    remote(
                        src, dst, sm.at[index, g], rm.at[t, slot, g], {"tensor": s}
                    ).wait_send()

            sends.append(done)

    pumps = [functools.partial(weights_third, n, name) for n, name in enumerate(wide)]
    def mask_shift(qb):
        K = (qb + 1) * QB
        row_frame = (qb * QB + lax.broadcasted_iota(jnp.int32, (QB, K), 0)) // PATCH
        col_frame = lax.broadcasted_iota(jnp.int32, (QB, K), 1) // PATCH
        allowed = (col_frame <= row_frame) & (col_frame < live)
        return jnp.where(allowed, 0.0, -1e30)

    def attend_block(qb, g, shift):
        K = (qb + 1) * QB
        rows = pl.ds(qb * QB, QB)
        qv = qb_[g, rows, :]
        kv = kb_[g, pl.ds(0, K), :]
        vv = vb_[g, pl.ds(0, K), :]
        outs = []
        for a in range(HG):
            scores = dot(only(qv, a), kv, NT) + shift
            top = jnp.max(scores, axis=-1, keepdims=True)
            weights = jnp.exp(scores - top)
            total = jnp.sum(weights, axis=-1, keepdims=True)
            prob = (weights * (1.0 / total)).astype(BF)
            probs[g * HG + a, rows, pl.ds(0, K)] = prob
            outs.append(dot(prob, vv))
        mo[rows, pl.ds(g * GW, GW)] = pick(outs).astype(BF)

    for qb in reversed(range(NQ)):
        shift = mask_shift(qb)
        for g in range(G):
            attend_block(qb, g, shift)
            hand_over(qb, g)
        if pumps:
            pumps.pop(0)()
    while pumps:
        pumps.pop(0)()

    for n, name in enumerate(wide + ("bias",)):
        weights_ready(n, name)
    for p in range(1, T):
        s = lax.rem(t + p, T)
        for slot in range(R // piece):
            for g in range(G):
                arrived(
                    mr.at[s, pl.ds(slot * piece, piece), pl.ds(g * GW, GW)], rm.at[s, slot, g]
                )
    for k in range(FO):
        arrived(cb.at[pl.ds(k * tok, tok)], rc.at[k])

    wof, wuf, wdf, bf_ = full["w_out"], full["w_up"], full["w_down"], full["bias"]
    second, act, gpre = ref.second, ref.act, ref.gpre
    mlow, gmid, gst, gx = ref.mlow, ref.gmid, ref.gst, ref.gx
    ob, out_ref, ig_ref = ref.ob, ref.out, ref.ig
    sv = ref.sv
    mlp_sum, sec_sum = ref.mlp_sum, ref.sec_sum
    RC = min(256, R)
    FT = min(512, FFh)
    c0 = 0.7978845608028654
    sv[0] = jnp.zeros_like(sv[0])

    def frame_home(k):
        f = t * FO + k
        high = f // N
        j = f * (1 - high) + (2 * N - 1 - f) * high
        return j, high

    def give_back(buf, dst_ref, ss, rs, k):
        j, h = frame_home(k)
        src = buf.at[pl.ds(k * tok, tok)]

        @pl.when(j == i)
        def _():
            pltpu.make_async_copy(src, dst_ref.at[i, h], rs.at[i, h]).start()

        @pl.when(j != i)
        def _():
            remote(src, dst_ref.at[i, h], ss.at[k], rs.at[i, h], {"ctx": j}).start()

        def done():
            @pl.when(j != i)
            def _():
                remote(src, dst_ref.at[i, h], ss.at[k], rs.at[i, h], {"ctx": j}).wait_send()

        sends.append(done)

    def pass_on(dst_ref, fs, rs):
        for p in range(N):
            c = lax.rem(i + p, N)
            for h in (0, 1):
                part = dst_ref.at[c, h]

                @pl.when(owns(h))
                def _(p=p, c=c, h=h, part=part):
                    arrived(part, rs.at[c, h])
                    for q in range(1, T):
                        remote(
                            part, part, fs.at[q, p, h], rs.at[c, h], {"tensor": lax.rem(t + q, T)}
                        ).start()

                def done(p=p, c=c, h=h, part=part):
                    @pl.when(owns(h))
                    def _():
                        for q in range(1, T):
                            remote(
                                part,
                                part,
                                fs.at[q, p, h],
                                rs.at[c, h],
                                {"tensor": lax.rem(t + q, T)},
                            ).wait_send()

                sends.append(done)

    def take_rest(dst_ref, rs):
        for c in range(N):
            for h in (0, 1):

                @pl.when(frames[h] // FO != t)
                def _(c=c, h=h):
                    arrived(dst_ref.at[c, h], rs.at[c, h])

    sg, rg = ref.sg, ref.rg
    def feed_forward(rc_index):
        rows = pl.ds(rc_index * RC, RC)
        attn = dot(mr[0, rows, :], wof[0])
        for s in range(1, T):
            attn = attn + dot(mr[s, rows, :], wof[s])
        middle = xb[row_ds(t * R + rc_index * RC, RC, 64), :].astype(F32) + attn
        xhat, rstd = norm_parts(middle)
        sec = (xhat * vec[2][...] + vec[3][...]).astype(BF)
        second[rows, :] = sec
        cot = cb[rows, :]
        for s in range(T):
            for j in range(FFh // FT):
                cols = pl.ds(j * FT, FT)
                pre = dot(sec, wuf[s, :, cols]) + bf_[s, 0:1, cols]
                gact = dot(cot, wdf[s, cols, :], NT)
                sq = pre * pre
                th = jnp.tanh(c0 * pre * (1.0 + 0.044715 * sq))
                half = 0.5 * (1.0 + th)
                a = (pre * half).astype(BF)
                slope = half + 0.5 * pre * (1.0 - th * th) * (c0 * (1.0 + 0.134145 * sq))
                gp = (gact * slope).astype(BF)
                act[s, rows, cols] = a
                gpre[s, rows, cols] = gp
                sv[0, 4 + s : 5 + s, cols] = sv[0, 4 + s : 5 + s, cols] + jnp.sum(
                    gp.astype(F32), axis=0, keepdims=True
                )
                up = dot(a, wdf[s, cols, :])
                back = dot(gp, wuf[s, :, cols], NT)
                if s == 0 and j == 0:
                    mlp_sum[...] = up
                    sec_sum[...] = back
                else:
                    mlp_sum[...] = mlp_sum[...] + up
                    sec_sum[...] = sec_sum[...] + back
        ob[rows, :] = (middle + mlp_sum[...]).astype(BF)
        gsec = sec_sum[...]
        sv[0, 2:3, 0:D] = sv[0, 2:3, 0:D] + jnp.sum(gsec * xhat, axis=0, keepdims=True)
        sv[0, 3:4, 0:D] = sv[0, 3:4, 0:D] + jnp.sum(gsec, axis=0, keepdims=True)
        gm = cot.astype(F32) + norm_back(gsec, vec[2][...], xhat, rstd)
        gmid[rows, :] = gm
        low = gm.astype(BF)
        mlow[rows, :] = low
        for s in range(T):
            gst[s, rows, :] = dot(low, wof[s], NT).astype(BF)

    for rc_index in range(R // RC):
        rows = pl.ds(rc_index * RC, RC)
        feed_forward(rc_index)
        for s in range(T):
            src = gst.at[s, rows]
            dst = gx.at[row_ds(t * R + rc_index * RC, RC, 64)]

            @pl.when(s == t)
            def _():
                gx[row_ds(t * R + rc_index * RC, RC, 64), :] = gst[s, rows, :]

            @pl.when(s != t)
            def _():
                remote(
                    src, dst, sg.at[s, rc_index], rg.at[t, rc_index], {"tensor": s}
                ).start()

            def done(s=s, src=src, dst=dst, rc_index=rc_index):
                @pl.when(s != t)
                def _():
                    remote(
                        src, dst, sg.at[s, rc_index], rg.at[t, rc_index], {"tensor": s}
                    ).wait_send()

            sends.append(done)
        for k in range(rc_index * RC // tok, (rc_index + 1) * RC // tok):
            give_back(ob, out_ref, ref.so, ref.ro, k)

    reduces = {}
    for name in cfg.plans:
        levels = cfg.plans[name]
        bufs = [getattr(ref, name + "_buf" + str(n)) for n in range(len(levels))]
        reduces[name] = Reduce(
            levels, getattr(ref, name + "_acc"), getattr(ref, name + "_fin"), bufs, getattr(ref, name + "_ss"),
            getattr(ref, name + "_rs"), place,
        )
    cot = cb[...]
    for s in range(T):
        ref.down_acc[s] = dot(act[s], cot, TN).astype(BF)
    reduces["down"].tick()
    for s in range(T):
        ref.up_acc[s] = dot(second[...], gpre[s], TN).astype(BF)
    reduces["up"].tick()
    for s in range(T):
        ref.out_acc[s] = dot(mr[s], mlow[...], TN).astype(BF)
    reduces["out"].tick()

    for p in range(1, T):
        s = lax.rem(t + p, T)
        for n in range(R // RC):
            arrived(gx.at[row_ds(s * R + n * RC, RC, 64)], rg.at[s, n])

    dk, dv, gpb = ref.dk, ref.dv, ref.gpb

    def attend_back_block(g, qb):
        K = (qb + 1) * QB
        rows = pl.ds(qb * QB, QB)
        keys = pl.ds(0, K)
        lanes = pl.ds(g * GW, GW)
        go = gx[rows, lanes]
        prod = go.astype(F32) * mo[rows, lanes].astype(F32)
        qv = qb_[g, rows, :]
        kv = kb_[g, keys, :]
        vv = vb_[g, keys, :]
        outs = []
        dk_sum = dv_sum = None
        for a in range(HG):
            delta = jnp.sum(only(prod, a), axis=-1, keepdims=True)
            goa = only(go, a)
            prob = probs[g * HG + a, rows, keys]
            gprob = dot(goa, vv, NT)
            gs = (prob.astype(F32) * (gprob - delta)).astype(BF)
            outs.append(dot(gs, kv))
            dk_part = dot(gs, only(qv, a), TN)
            dv_part = dot(prob, goa, TN)
            dk_sum = dk_part if dk_sum is None else dk_sum + dk_part
            dv_sum = dv_part if dv_sum is None else dv_sum + dv_part
        gpb[rows, lanes] = (pick(outs) * scale).astype(BF)
        if qb == NQ - 1:
            dk[keys, :] = dk_sum
            dv[keys, :] = dv_sum
        else:
            dk[keys, :] = dk[keys, :] + dk_sum
            dv[keys, :] = dv[keys, :] + dv_sum

    turns = 0
    for g in range(G):
        for qb in reversed(range(NQ)):
            attend_back_block(g, qb)
            if turns == 1:
                pass_on(out_ref, ref.fo, ref.ro)
            reduces["down"].tick()
            reduces["up"].tick()
            reduces["out"].tick()
            turns += 1
        gpb[:, pl.ds(HW + g * GW, GW)] = dk[...].astype(BF)
        gpb[:, pl.ds(2 * HW + g * GW, GW)] = dv[...].astype(BF)

    gns, gnr = ref.gns, ref.gnr
    for p in range(1, T):
        s = lax.rem(t + p, T)
        gns[p - 1] = dot(gpb[row_ds(s * R, R, 64), :], wqkv[...], NT).astype(BF)
        copy = remote(gns.at[p - 1], gnr.at[p - 1], ref.sn.at[p - 1], ref.rn.at[p - 1], {"tensor": s})
        copy.start()
        sends.append(copy.wait_send)
    ref.qkv_acc[0] = dot(nb[...], gpb[...], TN).astype(BF)
    reduces["qkv"].tick()
    own = dot(gpb[row_ds(t * R, R, 64), :], wqkv[...], NT)
    for p in range(1, T):
        arrived(gnr.at[p - 1], ref.rn.at[p - 1])
        own = own + gnr[p - 1].astype(F32)
    xhat, rstd = norm_parts(xb[row_ds(t * R, R, 64), :].astype(F32))
    sv[0, 0:1, 0:D] = jnp.sum(own * xhat, axis=0, keepdims=True)
    sv[0, 1:2, 0:D] = jnp.sum(own, axis=0, keepdims=True)
    igb = ref.igb
    igb[...] = (gmid[...] + norm_back(own, vec[0][...], xhat, rstd)).astype(BF)
    for k in range(FO):
        give_back(igb, ig_ref, ref.si, ref.ri, k)

    rsv = ref.rsv
    everyone = [(a, b) for a, n in (("ctx", N), ("dp", DP), ("tensor", T)) for b in bits_of(n)]
    for n, (axis, bit) in enumerate(everyone):
        copy = remote(
            sv.at[n], rsv.at[n], ref.sv_ss.at[n], ref.sv_rs.at[n],
            {axis: flip(place[axis], bit)},
        )
        copy.start()
        reduces["qkv"].tick()
        copy.wait()
        sv[n + 1] = sv[n] + rsv[n]
    pass_on(ig_ref, ref.fi, ref.ri)
    last = sv[len(everyone)]
    part = D // T
    gains = last[0:4, 0:part]
    bias = last[4:5, 0:FFh]
    for s in range(1, T):
        gains = jnp.where(t == s, last[0:4, s * part : (s + 1) * part], gains)
        bias = jnp.where(t == s, last[4 + s : 5 + s, 0:FFh], bias)
    for n, got in enumerate((ref.grad_ga, ref.grad_sa, ref.grad_gm, ref.grad_sm)):
        got[...] = gains[n : n + 1, :]
    ref.bias_out[...] = bias

    for name in ("down", "up", "out", "qkv"):
        reduces[name].drain()
    take_rest(out_ref, ref.ro)
    take_rest(ig_ref, ref.ri)
    for done in sends:
        done()


def chip_kernel(cfg, names, *refs):
    ref = SimpleNamespace(**dict(zip(names, refs)))
    N, T, DP = cfg.N, cfg.T, cfg.DP
    L, R, FO, tok = cfg.L, cfg.R, cfg.FO, cfg.tok
    D, HW, GW, G, FFh, QB = cfg.D, cfg.HW, cfg.GW, cfg.G, cfg.FFh, cfg.QB
    head_dim = cfg.head_dim
    Z = N // 2
    HG = GW // head_dim
    scale = head_dim ** (-0.5)
    d = lax.axis_index("dp")
    i = lax.axis_index("ctx")
    t = lax.axis_index("tensor")
    z, kap = i // 2, lax.rem(i, 2)
    clip = 2 * z + t
    mate, mirror, beside = {"ctx": flip(i, 1)}, {"tensor": 1 - t}, {"dp": flip(d, 1)}
    place = {"dp": d, "ctx": i, "tensor": t}
    x_in, cot_in = ref.x, ref.cot
    sends = []

    def go(src, dst, send_sem, recv_sem, where):
        copy = remote(src, dst, send_sem, recv_sem, where)
        copy.start()
        sends.append(copy.wait_send)

    def go_if(cond, *args):
        @pl.when(cond)
        def _():
            remote(*args).start()

        def done():
            @pl.when(cond)
            def _():
                remote(*args).wait_send()

        sends.append(done)

    vec = [ref.vecs.at[n] for n in range(4)]
    vec_loads = []
    for n, src in enumerate((ref.gain_attn, ref.shift_attn, ref.gain_mlp, ref.shift_mlp)):
        vec_loads.append(pltpu.make_async_copy(src, vec[n], ref.vl.at[n]))
        vec_loads[-1].start()

    bar = pltpu.get_barrier_semaphore()
    peers = [{"ctx": lax.rem(i + p, N)} for p in (4, 3, 5, 2, 6, 1, 7)]
    peers += [mirror] + [{"dp": flip(d, b)} for b in bits_of(DP)]
    for peer in peers:
        pl.semaphore_signal(bar, inc=1, device_id=peer, device_id_type=MESH)

    wqkv, rq = ref.wq, ref.rq
    blocks = []
    for n in range(HW // head_dim):
        for b in range(3):
            src = ref.w_qkv.at[n, pl.ds(b * head_dim, head_dim)]
            dst = wqkv.at[pl.ds(b * HW + n * head_dim, head_dim)]
            blocks.append((src, dst, ref.bq.at[3 * n + b]))

    @pl.when(kap == t)
    def _():
        for block in blocks:
            pltpu.make_async_copy(*block).start()
        for block in blocks:
            pltpu.make_async_copy(*block).wait()

    pl.semaphore_wait(bar, len(peers))

    frames = (i, 2 * N - 1 - i)
    hops = [0, Z // 2] + [p for p in range(1, Z) if p != Z // 2]

    def deal(src_ref, dst_ref, spot, ss, rs):
        for p in hops:
            zz = lax.rem(z + p, Z)
            for h in (0, 1):
                src = src_ref.at[2 * zz + t, h]
                dst = dst_ref.at[row_ds(spot(h) * tok, tok)]
                to = {"ctx": 2 * zz + h}
                sem = rs.at[spot(h)]
                if p == 0:

                    @pl.when(kap == h)
                    def _(src=src, dst=dst, sem=sem):
                        pltpu.make_async_copy(src, dst, sem).start()

                    go_if(kap != h, src, dst, ss.at[p, h], sem, to)
                else:
                    go(src, dst, ss.at[p, h], sem, to)

    xb, rx = ref.xb, ref.rx
    deal(x_in, xb, lambda h: frames[h], ref.sx, rx)
    cb, rc = ref.cb, ref.rc
    deal(cot_in, cb, lambda h: frames[h] - h * FO, ref.sc, rc)

    half = 3 * HW // 2
    first_half = row_ds(lax.rem(d, 2) * half, half)
    other_half = row_ds((1 - lax.rem(d, 2)) * half, half)
    go_if(
        kap == t, wqkv.at[first_half], wqkv.at[first_half], ref.sq.at[0], rq.at[1],
        mirror,
    )

    share = 2 * lax.rem(d, 2) + kap
    other_dp = 2 * (1 - lax.rem(d, 2)) + kap
    other_core = 2 * lax.rem(d, 2) + 1 - kap
    other_both = 2 * (1 - lax.rem(d, 2)) + 1 - kap
    wide = ("w_out", "w_up", "w_down")
    full = {n: getattr(ref, n + "_full") for n in wide + ("bias",)}
    rw, sw, lw = ref.rw, ref.sw, ref.lw
    own_copies = {}
    for n, name in enumerate(wide + ("bias",)):
        own_copies[name] = pltpu.make_async_copy(getattr(ref, name), full[name].at[t], lw.at[n])
        own_copies[name].start()

    def weight_part(name, s, which):
        quarter = getattr(ref, name).shape[0] // 4
        return full[name].at[s, row_ds(which * quarter, quarter)]

    for n, name in enumerate(wide):
        quarter = getattr(ref, name).shape[0] // 4
        src = getattr(ref, name).at[row_ds(share * quarter, quarter)]
        go(src, weight_part(name, t, share), sw.at[n, 0], rw.at[n, 0], mirror)
    go(ref.bias, full["bias"].at[t], sw.at[3, 0], rw.at[3, 0], mirror)

    def weights_second(name):
        n = wide.index(name)
        part = weight_part(name, 1 - t, share)
        arrived(part, rw.at[n, 0])
        go(part, part, sw.at[n, 1], rw.at[n, 1], beside)
        go(part, part, sw.at[n, 2], rw.at[n, 2], mate)

    def weights_third(name):
        n = wide.index(name)
        part = weight_part(name, 1 - t, other_dp)
        arrived(part, rw.at[n, 1])
        go(part, part, sw.at[n, 3], rw.at[n, 3], mate)

    def weights_ready(name):
        n = wide.index(name)
        arrived(weight_part(name, 1 - t, other_core), rw.at[n, 2])
        arrived(weight_part(name, 1 - t, other_both), rw.at[n, 3])

    RB = 2 * tok
    nb, qa, ka, va = ref.nb, ref.q, ref.k, ref.v
    live = ref.live[clip]
    for load in vec_loads:
        load.wait()

    def project(start):
        rows = row_ds(start, RB, 64)
        xhat, _ = norm_parts(xb[rows, :].astype(F32))
        normed = (xhat * vec[0][...] + vec[1][...]).astype(BF)
        nb[rows, :] = normed
        packed = dot(normed, wqkv[...], NT)
        side = lax.broadcasted_iota(jnp.int32, (RB, GW), 1)
        frame = (start + lax.broadcasted_iota(jnp.int32, (RB, GW), 0)) // PATCH
        for n in range(G * HG):
            g, h = n // HG, n % HG
            mine = side // head_dim == h
            other = side - (1 - h) * head_dim
            lo = g * GW
            query = packed[:, lo : lo + GW].astype(BF).astype(F32) * scale
            key = packed[:, HW + lo : HW + lo + GW]
            value = packed[:, 2 * HW + lo : 2 * HW + lo + GW]
            hidden = (other < L // PATCH) & ((frame > other) | (frame >= live))
            qa[n, rows, :] = jnp.where(mine, query, jnp.where(frame == other, 1.0, 0.0)).astype(BF)
            ka[n, rows, :] = jnp.where(mine, key, jnp.where(hidden, -1e30, 0.0)).astype(BF)
            va[n, rows, :] = jnp.where(mine, value, 1.0).astype(BF)

    @pl.when(kap != t)
    def _():
        arrived(wqkv.at[first_half], rq.at[1])

    go_if(
        kap != t, wqkv.at[first_half], wqkv.at[first_half], ref.sq.at[1], rq.at[2], beside
    )
    weights_second("w_out")
    def first_row(p, core):
        far = 2 * lax.rem(z + Z - p, Z)
        return (far * (1 - core) + (2 * N - 2 - far) * core) * tok

    for p in hops:
        for n in range(2):
            row = first_row(p, kap) + n * tok
            part = xb.at[row_ds(row, tok)]
            arrived(part, rx.at[row // tok])
            go(part, part, ref.fx.at[p, n], rx.at[row // tok], mate)
        if p == 0:

            @pl.when(kap != t)
            def _():
                arrived(wqkv.at[other_half], rq.at[2])

        if p != hops[-1]:
            project(first_row(p, kap))
    for p in hops:
        if p == hops[-1]:
            project(first_row(p, kap))
        for n in range(2):
            row = first_row(p, 1 - kap) + n * tok
            arrived(xb.at[row_ds(row, tok)], rx.at[row // tok])
        if p == hops[-1]:
            weights_second("w_up")
        project(first_row(p, 1 - kap))

    probs, mo, mr = ref.probs, ref.mo, ref.mr
    rm, sm = ref.rm, ref.sm
    NQ = L // QB
    lane = lax.broadcasted_iota(jnp.int32, (QB, GW), 1)

    def pick(first, second):
        return jnp.where(lane < head_dim, first, second)

    def hand_over(qb, g):
        row = qb * QB
        s = row // R
        off = row - s * R
        lanes = pl.ds(g * GW, GW)
        src = mo.at[pl.ds(row, QB), lanes]
        dst = mr.at[kap, pl.ds(off, QB), lanes]

        @pl.when(kap == s)
        def _():
            mr[kap, pl.ds(off, QB), lanes] = mo[pl.ds(row, QB), lanes]

        go_if(kap != s, src, dst, sm.at[qb, g], rm.at[off // QB, g], mate)

    def attend_block(qb, g):
        K = (qb + 1) * QB
        rows, keys = pl.ds(qb * QB, QB), pl.ds(0, K)
        outs, sums = [], []
        for n in range(g * HG, (g + 1) * HG):
            scores = dot(qa[n, rows, :], ka[n, keys, :], NT)
            top = jnp.max(scores, axis=-1, keepdims=True)
            weights = jnp.exp(scores - top).astype(BF)
            probs[n, rows, keys] = weights
            both = dot(weights, va[n, keys, :])
            outs.append(both)
            sums.append(pltpu.roll(both, head_dim, 1))
        inverse = 1.0 / pick(*sums)
        lanes = pl.ds(g * GW, GW)
        ref.inv[rows, lanes] = inverse
        mo[rows, lanes] = (pick(*outs) * inverse).astype(BF)

    pumps = {
        (1, 1): functools.partial(weights_second, "w_down"),
        (2, 1): functools.partial(weights_third, "w_out"),
    }
    for qb in range(NQ):
        for g in range(G):
            attend_block(qb, g)
            hand_over(qb, g)
            if (qb, g) in pumps:
                pumps[qb, g]()

    wof, wuf, wdf, bf_ = full["w_out"], full["w_up"], full["w_down"], full["bias"]
    second, act, gpre = ref.second, ref.act, ref.gpre
    mlow, gmid, gst, gx = ref.mlow, ref.gmid, ref.gst, ref.gx
    ob, out_ref, ig_ref = ref.ob, ref.out, ref.ig
    mid, bsum, sv = ref.mid, ref.bsum, ref.sv
    mlp_sum, sec_sum = ref.mlp_sum, ref.sec_sum
    RC = min(256, R)
    FT = 2 * FFh // len(cfg.order)
    c0 = 0.7978845608028654

    def middle_rows(c):
        rows = pl.ds(c * RC, RC)
        attn = dot(mr[0, rows, :], wof[0])
        for s in range(1, T):
            attn = attn + dot(mr[s, rows, :], wof[s])
        middle = xb[row_ds(kap * R + c * RC, RC, 64), :].astype(F32) + attn
        mid[rows, :] = middle
        xhat, _ = norm_parts(middle)
        second[rows, :] = (xhat * vec[2][...] + vec[3][...]).astype(BF)

    def feed_forward(s, c, tiles, first):
        rows = pl.ds(c * RC, RC)
        sec = second[rows, :]
        cot = cb[rows, :]
        for j in tiles:
            cols = pl.ds(j * FT, FT)
            pre = dot(sec, wuf[s, :, cols]) + bf_[s, 0:1, cols]
            gact = dot(cot, wdf[s, cols, :], NT)
            sq = pre * pre
            th = jnp.tanh(c0 * pre * (1.0 + 0.044715 * sq))
            half = 0.5 * (1.0 + th)
            a = (pre * half).astype(BF)
            slope = half + 0.5 * pre * (1.0 - th * th) * (c0 * (1.0 + 0.134145 * sq))
            gp = (gact * slope).astype(BF)
            act[s, rows, cols] = a
            gpre[s, rows, cols] = gp
            sums = jnp.sum(gp.astype(F32), axis=0, keepdims=True)
            bsum[s, 0:1, cols] = sums if c == 0 else bsum[s, 0:1, cols] + sums
            up = dot(a, wdf[s, cols, :])
            back = dot(gp, wuf[s, :, cols], NT)
            if first and j == 0:
                mlp_sum[rows, :] = up
                sec_sum[rows, :] = back
            else:
                mlp_sum[rows, :] = mlp_sum[rows, :] + up
                sec_sum[rows, :] = sec_sum[rows, :] + back

    def finish_rows(c):
        rows = pl.ds(c * RC, RC)
        middle = mid[rows, :]
        xhat, rstd = norm_parts(middle)
        ob[rows, :] = (middle + mlp_sum[rows, :]).astype(BF)
        gsec = sec_sum[rows, :]
        gain_sum = jnp.sum(gsec * xhat, axis=0, keepdims=True)
        shift_sum = jnp.sum(gsec, axis=0, keepdims=True)
        if c > 0:
            gain_sum = gain_sum + sv[0, 2:3, 0:D]
            shift_sum = shift_sum + sv[0, 3:4, 0:D]
        sv[0, 2:3, 0:D] = gain_sum
        sv[0, 3:4, 0:D] = shift_sum
        gm = cb[rows, :].astype(F32) + norm_back(gsec, vec[2][...], xhat, rstd)
        gmid[rows, :] = gm
        low = gm.astype(BF)
        mlow[rows, :] = low
        for s in range(T):
            gst[s, rows, :] = dot(low, wof[s], NT).astype(BF)

    def give_back(buf, dst_ref, ss, rs, k):
        j = 2 * lax.rem(z + hops[k // 2], Z) + k % 2
        f = j * (1 - kap) + (2 * N - 1 - j) * kap
        src = buf.at[row_ds((f - kap * FO) * tok, tok)]
        dst, sem = dst_ref.at[clip, kap], rs.at[clip, kap]

        @pl.when(j == i)
        def _():
            pltpu.make_async_copy(src, dst, sem).start()

        go_if(j != i, src, dst, ss.at[k], sem, {"ctx": j})

    def pass_on(dst_ref, fs, rs, p):
        for h in (0, 1):
            cc = 2 * lax.rem(z + Z - hops[p], Z) + t
            part = dst_ref.at[cc, h]
            arrived(part, rs.at[cc, h])
            go(part, part, fs.at[p, h], rs.at[cc, h], mirror)

    def take_rest(dst_ref, rs):
        for p in range(Z):
            for h in (0, 1):
                cc = 2 * p + 1 - t
                arrived(dst_ref.at[cc, h], rs.at[cc, h])

    reduces = {}
    for name, levels in cfg.plans.items():
        bufs = [getattr(ref, name + "_buf" + str(n), None) for n in range(len(levels))]
        reduces[name] = Reduce(
            levels, getattr(ref, name + "_acc"), getattr(ref, name + "_fin"), bufs,
            getattr(ref, name + "_ss"), getattr(ref, name + "_rs"), place,
        )
        to, sem = getattr(ref, name + "_sum"), ref.end.at[len(reduces) - 1]
        reduces[name].result = pltpu.make_async_copy(reduces[name].fin, to, sem)

    def grad_wide(name, s):
        cols = pl.ds(int(name[-1]) * FT, FT)
        if name[0] == "d":
            getattr(ref, name + "_acc")[s] = dot(act[s, :, cols], cb[...], TN).astype(BF)
        else:
            getattr(ref, name + "_acc")[s] = dot(second[...], gpre[s, :, cols], TN).astype(BF)

    rsv = ref.rsv
    everyone = [("ctx", b) for b in bits_of(N)] + [("dp", b) for b in bits_of(DP)]
    everyone += [("tensor", b) for b in bits_of(T)]
    vec_copy = []

    def vec_step():
        n = len(vec_copy)
        if n > 0:
            vec_copy[-1].wait()
            sv[n] = sv[n - 1] + rsv[n - 1]
        if n < len(everyone):
            axis, bit = everyone[n]
            copy = remote(
                sv.at[n], rsv.at[n], ref.sv_ss.at[n], ref.sv_rs.at[n],
                {axis: flip(place[axis], bit)},
            )
            copy.start()
            vec_copy.append(copy)
        else:
            small_results()

    vec_out = []

    def small_results():
        last = sv[len(everyone)]
        part = D // T
        gains = last[0:4, 0:part]
        bias = last[4:5, 0:FFh]
        for s in range(1, T):
            gains = jnp.where(t == s, last[0:4, s * part : (s + 1) * part], gains)
            bias = jnp.where(t == s, last[4 + s : 5 + s, 0:FFh], bias)
        for n, to in enumerate((ref.grad_ga, ref.grad_sa, ref.grad_gm, ref.grad_sm)):
            ref.gain_sums[n] = gains[n : n + 1, :]
            vec_out.append(pltpu.make_async_copy(ref.gain_sums.at[n], to, ref.vo.at[n]))
        ref.bias_sums[...] = bias
        vec_out.append(pltpu.make_async_copy(ref.bias_sums, ref.bias_out, ref.vo.at[4]))
        for copy in vec_out:
            copy.start()

    out_done, ig_done = [], []
    script = list(cfg.script)
    old_sends = []

    def run_script():
        while script:
            for _ in range(min(3, len(old_sends))):
                old_sends.pop(0)()
            item = script.pop(0)
            if item == MARK:
                return
            if item == VECTORS:
                vec_step()
            elif item == OUTPUT:
                pass_on(out_ref, ref.fo, ref.ro, len(out_done))
                out_done.append(item)
            elif item == INPUT_GRAD:
                pass_on(ig_ref, ref.fi, ref.ri, len(ig_done))
                ig_done.append(item)
            else:
                reduces[CHUNKS[item]].tick()

    for name in wide + ("bias",):
        own_copies[name].wait()
    arrived(full["bias"].at[1 - t], rw.at[3, 0])
    weights_ready("w_out")
    for k in range(FO):
        arrived(cb.at[pl.ds(k * tok, tok)], rc.at[k])
    for c in range(R // RC):
        for g in range(G):
            rows, lanes = pl.ds(c * RC, RC), pl.ds(g * GW, GW)
            arrived(mr.at[1 - kap, rows, lanes], rm.at[c, g])
        middle_rows(c)
        feed_forward(t, c, (0,), True)
        weights_third("w_up" if c == 0 else "w_down")
        feed_forward(t, c, range(1, FFh // FT), True)
    for name in cfg.order:
        if name[-1] == "0":
            grad_wide(name, t)
    weights_ready("w_up")
    weights_ready("w_down")
    for j in range(FFh // FT):
        for c in range(R // RC):
            feed_forward(1 - t, c, (j,), False)
        run_script()
        for name in cfg.order:
            if name[-1] == str(j):
                if j > 0:
                    grad_wide(name, t)
                grad_wide(name, 1 - t)
                reduces[name].tick()
    sv[0, 4:5, 0:FFh] = bsum[0, 0:1, :]
    sv[0, 5:6, 0:FFh] = bsum[1, 0:1, :]
    sg, rg = ref.sg, ref.rg
    for c in range(R // RC):
        finish_rows(c)
        rows = pl.ds(c * RC, RC)
        home = row_ds(kap * R + c * RC, RC, 64)
        gx[home, :] = gst[kap, rows, :]
        go(gst.at[1 - kap, rows], gx.at[home], sg.at[c], rg.at[c], mate)
    for k in range(FO):
        give_back(ob, out_ref, ref.so, ref.ro, k)

    for s in range(T):
        ref.out_acc[s] = dot(mr[s], mlow[...], TN).astype(BF)
    reduces["out"].tick()
    run_script()
    for c in range(R // RC):
        arrived(gx.at[row_ds((1 - kap) * R + c * RC, RC, 64)], rg.at[c])

    dk, dv, gpb = ref.dk, ref.dv, ref.gpb

    def attend_back_block(g, qb):
        K = (qb + 1) * QB
        rows = pl.ds(qb * QB, QB)
        keys = pl.ds(0, K)
        lanes = pl.ds(g * GW, GW)
        grad = gx[rows, lanes].astype(F32) * ref.inv[rows, lanes]
        prod = grad * mo[rows, lanes].astype(F32)
        outs = []
        for n in range(g * HG, (g + 1) * HG):
            h = n - g * HG
            mine = lane // head_dim == h
            other = lane - (1 - h) * head_dim
            delta = jnp.sum(jnp.where(mine, prod, 0.0), axis=-1, keepdims=True)
            high = delta.astype(BF).astype(F32)
            rest = jnp.where(other == 0, -high, jnp.where(other == 1, high - delta, 0.0))
            grads = jnp.where(mine, grad, rest).astype(BF)
            prob = probs[n, rows, keys]
            gs = (prob.astype(F32) * dot(grads, va[n, keys, :], NT)).astype(BF)
            outs.append(dot(gs, ka[n, keys, :]))
            dk_part = dot(gs, qa[n, rows, :], TN)
            dv_part = dot(prob, grads, TN)
            if qb == NQ - 1:
                dk[h, keys, :] = dk_part
                dv[h, keys, :] = dv_part
            else:
                dk[h, keys, :] = dk[h, keys, :] + dk_part
                dv[h, keys, :] = dv[h, keys, :] + dv_part
        gpb[rows, lanes] = (pick(*outs) * scale).astype(BF)

    def key_parts(g):
        first = lax.broadcasted_iota(jnp.int32, (L, GW), 1) < head_dim
        for b, acc in ((1, dk), (2, dv)):
            gpb[:, pl.ds(b * HW + g * GW, GW)] = jnp.where(first, acc[0], acc[1]).astype(BF)

    for g in range(G):
        for qb in reversed(range(NQ)):
            attend_back_block(g, qb)
            if qb == 0:
                key_parts(g)
                for b in range(3):
                    getattr(ref, "qkv" + str(g) + "_acc")[kap, pl.ds(b * GW, GW), :] = dot(
                        gpb[:, pl.ds(b * HW + g * GW, GW)], nb[...], TN
                    ).astype(BF)
                reduces["qkv" + str(g)].tick()
            run_script()

    gns, gnr = ref.gns, ref.gnr
    gns[...] = dot(gpb[row_ds((1 - kap) * R, R, 64), :], wqkv[...]).astype(BF)
    go(gns, gnr, ref.sn.at[0], ref.rn.at[0], mate)
    run_script()
    own = dot(gpb[row_ds(kap * R, R, 64), :], wqkv[...])
    arrived(gnr, ref.rn.at[0])
    own = own + gnr[...].astype(F32)
    xhat, rstd = norm_parts(xb[row_ds(kap * R, R, 64), :].astype(F32))
    sv[0, 0:1, 0:D] = jnp.sum(own * xhat, axis=0, keepdims=True)
    sv[0, 1:2, 0:D] = jnp.sum(own, axis=0, keepdims=True)
    igb = ref.igb
    igb[...] = (gmid[...] + norm_back(own, vec[0][...], xhat, rstd)).astype(BF)
    for k in range(FO):
        give_back(igb, ig_ref, ref.si, ref.ri, k)
    vec_step()
    old_sends += sends[: -FO]
    del sends[: -FO]
    run_script()
    take_rest(out_ref, ref.ro)
    take_rest(ig_ref, ref.ri)
    for chunk in reduces.values():
        chunk.result.wait()
    for copy in vec_out:
        copy.wait()
    for done in old_sends + sends:
        done()


def finish_kernel(sizes, *refs):
    D, HW, FFh, GW, G, head_dim, tiles = sizes
    count = 8 + 2 * tiles + G
    out, ig, ga, sa, gm, sm, bias, wo, *wide = refs[:count]
    outs = refs[count : count + 11]
    (
        b_out, b_ig, b_wo, b_down, b_up, b_qkv, f_qkv, f_wo, f_up, f_down, b_vec, b_bias, sem,
    ) = refs[count + 11 :]
    downs, ups, qkvs = wide[:tiles], wide[tiles : 2 * tiles], wide[2 * tiles :]
    moves = []

    def move(src, dst):
        copy = pltpu.make_async_copy(src, dst, sem.at[len(moves)])
        copy.start()
        moves.append(copy)
        return copy

    ends = [move(out, b_out), move(ig, b_ig)]
    reads = [move(src, b_down.at[n]) for n, src in enumerate(downs)]
    reads += [move(src, b_up.at[n]) for n, src in enumerate(ups)]
    reads += [move(wo, b_wo)] + [move(src, b_qkv.at[g]) for g, src in enumerate(qkvs)]
    vectors = ((ga, b_vec.at[0], 2), (sa, b_vec.at[1], 3), (gm, b_vec.at[2], 6))
    vectors += ((sm, b_vec.at[3], 7), (bias, b_bias, 9))
    small = len(reads)
    reads += [move(src, mid) for src, mid, _ in vectors]
    for copy, src, dst in zip(ends, (b_out, b_ig), outs):
        copy.wait()
        move(src, dst)
    part = FFh // tiles
    for n in range(tiles):
        reads[n].wait()
        at = pl.ds(n * part, part)
        f_down[at, :] = b_down[n].astype(F32)
        move(f_down.at[at], outs[10].at[at])
    for n in range(tiles):
        reads[tiles + n].wait()
        at = pl.ds(n * part, part)
        f_up[:, at] = b_up[n].astype(F32)
    move(f_up, outs[8])
    reads[2 * tiles].wait()
    f_wo[...] = b_wo[...].astype(F32)
    move(f_wo, outs[5])
    for n, (_, mid, dst) in enumerate(vectors):
        reads[small + n].wait()
        move(mid, outs[dst])
    pair = GW // head_dim
    for g in range(G):
        reads[2 * tiles + 1 + g].wait()
        for h in range(pair):
            for b in range(3):
                f_qkv[g * pair + h, pl.ds(b * head_dim, head_dim), :] = b_qkv[
                    g, pl.ds(b * GW + h * head_dim, head_dim), :
                ].astype(F32)
        at = pl.ds(g * pair, pair)
        move(f_qkv.at[at], outs[4].at[at])
    for copy in moves[len(reads) + 2 :]:
        copy.wait()


def finish(got, layout, qkv_shape, sizes, T):
    D, HW, FFh, GW, G, head_dim, tiles = sizes
    hbm = pl.BlockSpec(memory_space=pl.ANY)
    S, V = jax.ShapeDtypeStruct, pltpu.VMEM
    small = S((1, D // T), F32)
    by_head = (qkv_shape[1], qkv_shape[2], qkv_shape[0])
    results = pl.pallas_call(
        functools.partial(finish_kernel, sizes),
        out_shape=[
            S(got.out.shape, BF), S(got.ig.shape, BF), small, small, S(by_head, F32),
            S((HW, D), F32), small, small, S((D, FFh), F32), S((1, FFh), F32), S((FFh, D), F32),
        ],
        in_specs=[hbm] * (8 + 2 * tiles + G),
        out_specs=[hbm] * 11,
        scratch_shapes=[
            V(got.out.shape, BF), V(got.ig.shape, BF), V((HW, D), BF),
            V((tiles, FFh // tiles, D), BF), V((tiles, D, FFh // tiles), BF),
            V((G, 3 * GW, D), BF), V(by_head, F32), V((HW, D), F32), V((D, FFh), F32),
            V((FFh, D), F32), V((4, 1, D // T), F32), V((1, FFh), F32),
            pltpu.SemaphoreType.DMA((18 + 4 * tiles + 2 * G,)),
        ],
        compiler_params=pltpu.CompilerParams(vmem_limit_bytes=60 * 2**20),
    )(
        got.out, got.ig, got.grad_ga, got.grad_sa, got.grad_gm, got.grad_sm, got.bias_out,
        got.out_sum, *[getattr(got, n + "_sum") for n in CHUNKS if n != "out"],
    )
    out, ig, ga, sa, qkv, wo, gm, sm, up, bias, down = results
    return (
        out.reshape(layout), ig.reshape(layout), ga[0], sa[0], qkv.transpose(2, 0, 1), wo, gm[0],
        sm[0], up, bias[0], down,
    )


def body(
    sizes,
    inputs,
    cotangent,
    live_frames,
    gain_attn,
    shift_attn,
    w_qkv,
    w_out,
    gain_mlp,
    shift_mlp,
    w_up,
    up_bias,
    w_down,
):
    N, T, DP = sizes["ctx"], sizes["tensor"], sizes["dp"]
    C, _, _, tok, D = inputs.shape
    heads, head_dim = w_qkv.shape[1], w_qkv.shape[2] // 3
    HW = heads * head_dim
    GW = min(128, HW)
    FFh = w_up.shape[1]
    L = 2 * N * tok
    by_chip = T == 2 and HW == 256 and head_dim == 64 and N == 8 and tok == PATCH and N % 2 == 0 and C == N and DP == 2 and FFh == 2 * D
    S_ = 2 if by_chip else T
    R = L // S_
    cfg = SimpleNamespace(
        N=N, T=T, DP=DP, L=L, R=R, FO=2 * N // S_, tok=tok, D=D, HW=HW, GW=GW, G=HW // GW,
        FFh=FFh, QB=256, head_dim=head_dim,
    )
    G = cfg.G
    core, rest = [("ctx", 1)], [("ctx", b) for b in bits_of(N)[1:]]
    over_dp = [("dp", b) for b in bits_of(DP)]
    over_t = [("tensor", b) for b in reversed(bits_of(T))]
    if by_chip:
        steps = {
            "x": over_dp, "y": over_t, "z": rest[:1], "Z": rest[1:-1] + [rest[-1] + ("f",)],
            "R": rest[1:], "X": [over_dp[-1] + ("f",)],
        }
        cfg.plans = plans = {}
        cfg.script, cfg.order = SCRIPT, ORDER
        leads, widths, tiles = {}, {}, len(ORDER) // 2
        for name, order in ORDERS.items():
            begin = [("ctx", 1, "p")] if name[0] == "q" else core
            if name[0] == "d":
                leads[name], widths[name] = (T, FFh // tiles), D
            elif name[0] == "u":
                leads[name], widths[name] = (T, D), FFh // tiles
            elif name[0] == "o":
                leads[name], widths[name] = (T, HW), D
            else:
                leads[name], widths[name] = (T, 3 * GW), D
            plans[name] = plan_levels(*leads[name], begin + sum((steps[c] for c in order), []))
    else:
        cfg.plans = plans = {
            "down": plan_levels(T, FFh, core + over_dp + over_t + rest),
            "up": plan_levels(T, D, core + over_t + over_dp + rest),
            "out": plan_levels(T, HW, core + over_t + over_dp + rest),
            "qkv": plan_levels(1, D, core + over_dp + rest),
        }
        leads = {"down": (T, FFh), "up": (T, D), "out": (T, HW), "qkv": (1, D)}
        widths = {"down": D, "up": FFh, "out": D, "qkv": 3 * HW}

    x = inputs.reshape(C, 2, tok, D)
    cot = cotangent.reshape(C, 2, tok, D)
    wq = w_qkv.transpose(1, 2, 0)
    if not by_chip:
        wq = w_qkv.reshape(D, heads, 3, head_dim).transpose(0, 2, 1, 3).reshape(D, 3 * HW)

    vm = pl.BlockSpec(memory_space=pltpu.VMEM)
    hbm = pl.BlockSpec(memory_space=pl.ANY)
    near = hbm if by_chip else vm
    ins = dict(
        x=(x, hbm),
        cot=(cot, hbm),
        live=(live_frames, pl.BlockSpec(memory_space=pltpu.SMEM)),
        gain_attn=(gain_attn.reshape(1, D), near),
        shift_attn=(shift_attn.reshape(1, D), near),
        gain_mlp=(gain_mlp.reshape(1, D), near),
        shift_mlp=(shift_mlp.reshape(1, D), near),
        w_qkv=(wq, hbm if by_chip else vm),
        w_out=(w_out, hbm),
        w_up=(w_up, hbm),
        w_down=(w_down, hbm),
        bias=(up_bias.reshape(1, FFh), near),
    )
    S = jax.ShapeDtypeStruct
    outs = dict(out=S((C, 2, tok, D), BF), ig=S((C, 2, tok, D), BF))
    if by_chip:
        for name in plans:
            outs[name + "_sum"] = S((leads[name][1], widths[name]), BF)
    else:
        outs.update(
            down_fin=S((FFh, D), BF), up_fin=S((D, FFh), BF), out_fin=S((HW, D), BF),
            qkv_fin=S((D, 3 * HW), BF),
        )
    vector = S((1, D // T), F32)
    outs.update(
        grad_ga=vector, grad_sa=vector, grad_gm=vector, grad_sm=vector, bias_out=S((1, FFh), F32)
    )
    W = max(D, FFh)
    SR = -(-(4 + T) // 8) * 8
    n_all = len(bits_of(N)) + len(bits_of(DP)) + len(bits_of(T))
    RC = min(256, R)
    piece = min(cfg.QB, R)
    FO = cfg.FO
    dma = pltpu.SemaphoreType.DMA
    V = pltpu.VMEM
    scratch = dict(
        xb=V((L, D), BF), rx=dma((2 * N,)),
        cb=V((R, D), BF), rc=dma((FO,)),
        w_out_full=V((T, HW, D), BF), w_up_full=V((T, D, FFh), BF),
        w_down_full=V((T, FFh, D), BF), bias_full=V((T, 1, FFh), F32), lw=dma((4,)),
        nb=V((L, D), BF),
        probs=V((heads, L, L), BF), mo=V((L, HW), BF), mr=V((S_, R, HW), BF),
        second=V((R, D), BF), act=V((T, R, FFh), BF), gpre=V((T, R, FFh), BF),
        mlow=V((R, D), BF), gmid=V((R, D), F32), gst=V((T, R, HW), BF), gx=V((L, HW), BF),
        ob=V((R, D), BF), so=dma((FO,)), ro=dma((N, 2)),
        igb=V((R, D), BF), si=dma((FO,)), ri=dma((N, 2)),
        sv=V((n_all + 1, SR, W), F32), rsv=V((n_all, SR, W), F32),
        sv_ss=dma((n_all,)), sv_rs=dma((n_all,)),
        gpb=V((L, 3 * HW), BF),
    )
    if by_chip:
        scratch.update(
            q=V((heads, L, GW), BF), k=V((heads, L, GW), BF), v=V((heads, L, GW), BF),
            inv=V((L, HW), F32), dk=V((2, L, GW), F32), dv=V((2, L, GW), F32),
            sx=dma((N // 2, 2)), fx=dma((N // 2, 2)), sc=dma((N // 2, 2)),
            wq=V((3 * HW, D), BF), rq=dma((3,)), bq=dma((3 * heads,)), sq=dma((2,)),
            rw=dma((4, 4)), sw=dma((4, 4)), rm=dma((R // 256, G)), sm=dma((L // 256, G)),
            mid=V((R, D), F32), bsum=V((T, 8, FFh), F32),
            mlp_sum=V((R, D), F32), sec_sum=V((R, D), F32),
            sg=dma((R // RC,)), rg=dma((R // RC,)),
            fo=dma((N // 2, 2)), fi=dma((N // 2, 2)),
            gns=V((R, D), BF), gnr=V((R, D), BF), sn=dma((1,)), rn=dma((1,)), end=dma((len(plans),)),
            vecs=V((4, 1, D), F32), vl=dma((4,)), gain_sums=V((4, 1, D // T), F32),
            bias_sums=V((1, FFh), F32), vo=dma((5,)),
        )
    else:
        scratch.update(
            q=V((G, L, GW), BF), k=V((G, L, GW), BF), v=V((G, L, GW), BF),
            dk=V((L, GW), F32), dv=V((L, GW), F32),
            sx=dma((N, 2)), fx=dma((T, FO)), sc=dma((N, 2)), rw=dma((4, 4, T)), sw=dma((4, 4, T)),
            rm=dma((T, R // piece, G)), sm=dma((L // piece, G)),
            sg=dma((T, R // RC)), rg=dma((T, R // RC)), fo=dma((T, N, 2)), fi=dma((T, N, 2)),
            mlp_sum=V((RC, D), F32), sec_sum=V((RC, D), F32),
            gns=V((max(T - 1, 1), R, D), BF), gnr=V((max(T - 1, 1), R, D), BF),
            sn=dma((T,)), rn=dma((T,)),
        )
    for name, levels in plans.items():
        scratch[name + "_acc"] = V(leads[name] + (widths[name],), BF)
        if by_chip:
            scratch[name + "_fin"] = V((leads[name][1], widths[name]), BF)
        scratch[name + "_ss"] = dma((2 * len(levels),))
        scratch[name + "_rs"] = dma((2 * len(levels),))
        for n, (_, _, kind, lead, rows) in enumerate(levels):
            if kind == "p":
                continue
            scratch[name + "_buf" + str(n)] = V((lead, rows, widths[name]), BF)
    names = list(ins) + list(outs) + list(scratch)
    results = pl.pallas_call(
        functools.partial(chip_kernel if by_chip else spread_kernel, cfg, names),
        out_shape=list(outs.values()),
        in_specs=[s for _, s in ins.values()],
        out_specs=[hbm if by_chip else vm] * len(outs),
        scratch_shapes=list(scratch.values()),
        compiler_params=pltpu.CompilerParams(
            collective_id=0, has_side_effects=True, vmem_limit_bytes=60 * 2**20
        ),
    )(*[a for a, _ in ins.values()])
    got = SimpleNamespace(**dict(zip(outs, results)))
    if by_chip:
        return finish(got, inputs.shape, w_qkv.shape, (D, HW, FFh, GW, G, head_dim, tiles), T)
    grad_qkv = got.qkv_fin.reshape(D, 3, heads, head_dim).transpose(0, 2, 1, 3)
    return (
        got.out.reshape(inputs.shape),
        got.ig.reshape(inputs.shape),
        got.grad_ga[0],
        got.grad_sa[0],
        grad_qkv.reshape(w_qkv.shape).astype(F32),
        got.out_fin.astype(F32),
        got.grad_gm[0],
        got.grad_sm[0],
        got.up_fin.astype(F32),
        got.bias_out[0],
        got.down_fin.astype(F32),
    )


def solution(mesh):
    return jax.shard_map(
        functools.partial(body, dict(mesh.shape)),
        mesh=mesh,
        in_specs=(
            P("dp", None, "ctx", None, None),
            P("dp", None, "ctx", None, None),
            P("dp"),
            P(),
            P(),
            P(None, "tensor", None),
            P("tensor", None),
            P(),
            P(),
            P(None, "tensor"),
            P("tensor"),
            P("tensor", None),
        ),
        out_specs=(
            P("dp", None, "ctx", None, None),
            P("dp", None, "ctx", None, None),
            P("tensor"),
            P("tensor"),
            P(None, "tensor", None),
            P("tensor", None),
            P("tensor"),
            P("tensor"),
            P(None, "tensor"),
            P("tensor"),
            P("tensor", None),
        ),
        check_vma=False,
    )
```
